256 devices in a mesh: slab: 64 (over x, y, z_lo), rep: 4 (over z_hi, core).
Axes of the slice: x: 4, y: 4, z: 8 (z_hi: 2, z_lo: 4; z = z_hi * 4 + z_lo), core: 2. Of those that a mesh axis runs over, the one named last changes fastest.
Arguments:
- cubes: bfloat16 [4, 256, 32, 32, 64], P('rep', 'slab'), may hold values from -6 to 6
- weight_a: bfloat16 [3, 3, 3, 64, 128], replicated, may hold values from -0.15625 to 0.15625
- weight_b: bfloat16 [3, 3, 3, 128, 256], replicated, may hold values from -0.109375 to 0.109375
- cotangent: bfloat16 [4, 64, 8, 8, 256], P('rep', 'slab'), may hold values from -6 to 6
Outputs:
- features: bfloat16 [4, 64, 8, 8, 256], P('rep', 'slab')
- grad_cubes: bfloat16 [4, 256, 32, 32, 64], P('rep', 'slab')
- grad_weight_a: float32 [3, 3, 3, 64, 128], replicated
- grad_weight_b: float32 [3, 3, 3, 128, 256], replicated
The draws below stay inside these ranges and needn't reach their ends.
All inputs are finite; a program needn't handle non-finite values.
Results may differ from the reference program's by a relative error of at most 0.015.
Values may be sent and summed in bfloat16 or wider, within the bound.
No kernel may reach another device: no remote copies, remote signals or barrier semaphores. Data moves between devices by JAX's collectives and lax.ppermute only.
A program may use at most 128 MiB of HBM per device.

```python
import jax
import jax.numpy as jnp
from jax import lax

CIN = 64
MID = 128
COUT = 256
GY = 32
GZ = 32
GX = 256
SAMPLES = 4


def block_scale(rng, dims, cuts, smallest, largest):
    factor_of = 1.0
    for dim, shards_of in cuts:
        steps = jax.random.uniform(jax.random.fold_in(jax.random.fold_in(rng, 6), dim), (shards_of,), jnp.float32, smallest / len(cuts), largest / len(cuts))
        factor_of = factor_of * jnp.repeat(jnp.exp(steps), dims[dim] // shards_of).reshape((-1,) + (1,) * (len(dims) - 1 - dim))
    return factor_of


def scatter_about(rng, dims, deviation, bound, shards=(), dtype=jnp.bfloat16):
    drawn = jax.random.normal(rng, dims, jnp.float32) * deviation
    if len(shards) > 0:
        drawn = block_scale(rng, dims, shards, -0.22, 0.18) * drawn
    return jnp.clip(drawn, min=-bound, max=bound).astype(dtype)


def setup_inputs(seed: int = 0) -> dict:
    arg_keys = jax.random.split(jax.random.key(seed), 5)
    cubes = scatter_about(arg_keys[0], (SAMPLES, GX, GY, GZ, CIN), 1.0, 6.0, ((0, 4), (1, 64)))
    weight_a = scatter_about(arg_keys[1], (3, 3, 3, CIN, MID), (27 * CIN) ** -0.5, 0.15625)
    weight_b = scatter_about(arg_keys[2], (3, 3, 3, MID, COUT), (27 * MID) ** -0.5, 0.109375)
    cotangent = scatter_about(arg_keys[3], (SAMPLES, GX // 4, GY // 4, GZ // 4, COUT), 1.0, 6.0, ((0, 4), (1, 64)))
    return dict(cubes=cubes, weight_a=weight_a, weight_b=weight_b, cotangent=cotangent)


def conv_same(field, weight):
    padded = jnp.pad(field.astype(jnp.float32), ((0, 0), (1, 1), (1, 1), (1, 1), (0, 0)))
    return lax.conv_general_dilated(padded, weight.astype(jnp.float32), (1, 1, 1), 'VALID', dimension_numbers=('NDHWC', 'DHWIO', 'NDHWC'), precision=lax.Precision.HIGHEST)

def flipped(weight):
    return jnp.swapaxes(weight[::-1, ::-1, ::-1], 3, 4)

def weight_grad(field, grad):
    padded = jnp.pad(field.astype(jnp.float32), ((0, 0), (1, 1), (1, 1), (1, 1), (0, 0)))
    samples, extent_x, extent_y, extent_z, channels = field.shape
    grad_rows = grad.astype(jnp.float32).reshape(-1, grad.shape[-1])
    blocks = []
    for offset in range(27):
        shift_x, shift_y, shift_z = (offset // 9, offset // 3 % 3, offset % 3)
        window = padded[:, shift_x:shift_x + extent_x, shift_y:shift_y + extent_y, shift_z:shift_z + extent_z, :]
        blocks.append(lax.dot_general(window.reshape(-1, channels), grad_rows, (((0,), (0,)), ((), ())), precision=lax.Precision.HIGHEST))
    return jnp.stack(blocks).reshape(3, 3, 3, channels, grad.shape[-1])

def pool_cells(field):
    samples, extent_x, extent_y, extent_z, channels = field.shape
    blocks = field.reshape(samples, extent_x // 2, 2, extent_y // 2, 2, extent_z // 2, 2, channels)
    return lax.optimization_barrier(jnp.mean(blocks, axis=(2, 4, 6)))

def spread_cells(field):
    samples, extent_x, extent_y, extent_z, channels = field.shape
    wide = jnp.broadcast_to(field.astype(jnp.float32)[:, :, None, :, None, :, None, :], (samples, extent_x, 2, extent_y, 2, extent_z, 2, channels))
    return wide.reshape(samples, 2 * extent_x, 2 * extent_y, 2 * extent_z, channels) / 8.0

def silu_slope(value):
    sigma = jax.nn.sigmoid(value)
    return sigma * (1.0 + value * (1.0 - sigma))

def reference(cubes, weight_a, weight_b, cotangent):
    pre_a = conv_same(cubes, weight_a)
    pooled_a = pool_cells(jax.nn.silu(pre_a)).astype(jnp.bfloat16)
    pre_b = conv_same(pooled_a, weight_b)
    features = pool_cells(jax.nn.silu(pre_b)).astype(jnp.bfloat16)
    grad_pre_b = (spread_cells(cotangent) * silu_slope(pre_b)).astype(jnp.bfloat16)
    grad_weight_b = weight_grad(pooled_a, grad_pre_b) / SAMPLES
    grad_pooled = conv_same(grad_pre_b, flipped(weight_b)).astype(jnp.bfloat16)
    grad_pre_a = (spread_cells(grad_pooled) * silu_slope(pre_a)).astype(jnp.bfloat16)
    grad_weight_a = weight_grad(cubes, grad_pre_a) / SAMPLES
    grad_cubes = conv_same(grad_pre_a, flipped(weight_a)).astype(jnp.bfloat16)
    return (features, grad_cubes, grad_weight_a, grad_weight_b)
```

```python
import jax
import jax.numpy as jnp
from jax import lax
from jax.sharding import PartitionSpec as P


def extended(cells, sides, width):
    for axis, dim in sides:
        count = lax.axis_size(axis)
        ends = count - 1
        head = lax.slice_in_dim(cells, 0, width, axis=dim)
        tail = lax.slice_in_dim(cells, cells.shape[dim] - width, cells.shape[dim], axis=dim)
        cells = jnp.concatenate(
            [
                lax.ppermute(tail, axis, [(i, (i + 1) % count) for i in range(ends)]),
                cells,
                lax.ppermute(head, axis, [((i + 1) % count, i) for i in range(ends)]),
            ],
            axis=dim,
        )
    return cells


def pad_sides(field):
    return jnp.pad(field, ((0, 0), (0, 0), (1, 1), (1, 1), (0, 0)))


def conv_valid(padded, weight):
    return lax.conv_general_dilated(
        padded,
        weight,
        (1, 1, 1),
        "VALID",
        dimension_numbers=("NDHWC", "DHWIO", "NDHWC"),
        preferred_element_type=jnp.float32,
    )


def flipped(weight):
    return jnp.swapaxes(weight[::-1, ::-1, ::-1], 3, 4)


def weight_grad(padded, grad):
    samples, extent_x, extent_y, extent_z, outputs = grad.shape
    channels = padded.shape[-1]
    grad_rows = grad.reshape(-1, outputs)
    blocks = []
    for offset in range(27):
        shift_x, shift_y, shift_z = (offset // 9, offset // 3 % 3, offset % 3)
        window = padded[
            :,
            shift_x : shift_x + extent_x,
            shift_y : shift_y + extent_y,
            shift_z : shift_z + extent_z,
            :,
        ]
        blocks.append(
            lax.dot_general(
                window.reshape(-1, channels),
                grad_rows,
                (((0,), (0,)), ((), ())),
                preferred_element_type=jnp.float32,
            )
        )
    return jnp.stack(blocks).reshape(3, 3, 3, channels, outputs)


def pool_cells(field):
    samples, extent_x, extent_y, extent_z, channels = field.shape
    blocks = field.reshape(samples, extent_x // 2, 2, extent_y // 2, 2, extent_z // 2, 2, channels)
    return jnp.mean(blocks, axis=(2, 4, 6))


def spread_cells(field):
    samples, extent_x, extent_y, extent_z, channels = field.shape
    wide = jnp.broadcast_to(
        field.astype(jnp.float32)[:, :, None, :, None, :, None, :],
        (samples, extent_x, 2, extent_y, 2, extent_z, 2, channels),
    )
    return wide.reshape(samples, 2 * extent_x, 2 * extent_y, 2 * extent_z, channels) / 8.0


def silu_slope(value):
    sigma = jax.nn.sigmoid(value)
    return sigma * (1.0 + value * (1.0 - sigma))


AXES = ("slab", "rep")
SIZES = {"x": 4, "y": 4, "zl": 4, "zh": 2, "core": 2}


def coordinates(index):
    slab, rep = divmod(index, 4)
    return {"x": slab // 16, "y": slab // 4 % 4, "zl": slab % 4, "zh": rep // 2, "core": rep % 2}


def index_of(place):
    return ((place["x"] * 4 + place["y"]) * 4 + place["zl"]) * 4 + place["zh"] * 2 + place["core"]


def move(value, dim, step):
    pairs = []
    for source in range(256):
        place = coordinates(source)
        place[dim] = (place[dim] + step) % SIZES[dim]
        pairs.append((source, index_of(place)))
    return lax.ppermute(value, AXES, pairs)


def own_coordinate(dim):
    slab, rep = lax.axis_index("slab"), lax.axis_index("rep")
    return {"x": slab // 16, "y": slab // 4 % 4, "zl": slab % 4, "zh": rep // 2, "core": rep % 2}[dim]


def chunk(value, index, count):
    rows = value.shape[0] // count
    return lax.dynamic_slice_in_dim(value, index * rows, rows, axis=0)


def send_shares(value, dim):
    here, count = own_coordinate(dim), SIZES[dim]
    return [
        move(chunk(value, (here + step) % count, count).astype(jnp.bfloat16), dim, step)
        for step in range(1, count)
    ]


def add_shares(value, shares, dim):
    total = chunk(value, own_coordinate(dim), SIZES[dim]).astype(jnp.float32)
    for share in shares:
        total = total + share.astype(jnp.float32)
    return total


def send_block(block, dim):
    return [move(block, dim, step) for step in range(1, SIZES[dim])]


def join_blocks(block, others, dim):
    here, count = own_coordinate(dim), SIZES[dim]
    rows = block.shape[0]
    whole = jnp.zeros((rows * count, block.shape[1]), block.dtype)
    for step, piece in enumerate([block] + others):
        whole = lax.dynamic_update_slice_in_dim(whole, piece, (here - step) % count * rows, axis=0)
    return whole


def reduce_everywhere(rows):
    mine = add_shares(rows, send_shares(rows, "core"), "core")
    half = mine.shape[0] // 2
    first, second = mine[:half], mine[half:]
    shares_first, shares_second = send_shares(first, "x"), send_shares(second, "y")
    first, second = add_shares(first, shares_first, "x"), add_shares(second, shares_second, "y")
    shares_first, shares_second = send_shares(first, "y"), send_shares(second, "x")
    first, second = add_shares(first, shares_first, "y"), add_shares(second, shares_second, "x")
    both = jnp.concatenate([first, second]).astype(jnp.bfloat16)
    (other,) = send_block(both, "zh")
    both = (both.astype(jnp.float32) + other.astype(jnp.float32)).astype(jnp.bfloat16)
    one, two, three = (piece.astype(jnp.float32) for piece in send_block(both, "zl"))
    both = ((both.astype(jnp.float32) + two) + (one + three)).astype(jnp.bfloat16)
    half = both.shape[0] // 2
    first, second = both[:half], both[half:]
    got_first, got_second = send_block(first, "y"), send_block(second, "x")
    first, second = join_blocks(first, got_first, "y"), join_blocks(second, got_second, "x")
    got_first, got_second = send_block(first, "x"), send_block(second, "y")
    first, second = join_blocks(first, got_first, "x"), join_blocks(second, got_second, "y")
    both = jnp.concatenate([first, second])
    return join_blocks(both, send_block(both, "core"), "core")


def sum_kernels(local_a, local_b):
    part_a = local_a.reshape(1728, 128)
    part_b = local_b.reshape(3456, 256)
    rows = jnp.concatenate([part_a, part_b[:, :128], part_b[:, 128:], jnp.zeros((64, 128), jnp.float32)])
    total = reduce_everywhere(rows * 0.25).astype(jnp.float32)
    sum_a = total[:1728].reshape(3, 3, 3, 64, 128)
    sum_b = jnp.concatenate([total[1728:5184], total[5184:8640]], axis=1).reshape(3, 3, 3, 128, 256)
    return sum_a, sum_b


def shards(cubes, weight_a, weight_b, cotangent):
    rimmed = extended(cubes, (("slab", 1),), 1)
    padded = pad_sides(rimmed)
    pre_a = conv_valid(padded, weight_a)
    pooled_a = pool_cells(jax.nn.silu(pre_a)).astype(jnp.bfloat16)
    pooled_pad = pad_sides(extended(pooled_a, (("slab", 1),), 1))
    pre_b = conv_valid(pooled_pad, weight_b)
    features = pool_cells(jax.nn.silu(pre_b)).astype(jnp.bfloat16)
    grad_pre_b = (spread_cells(cotangent) * silu_slope(pre_b)).astype(jnp.bfloat16)
    local_b = weight_grad(pooled_pad, grad_pre_b)
    grad_b_rimmed = extended(grad_pre_b, (("slab", 1),), 1)
    grad_pooled = conv_valid(pad_sides(grad_b_rimmed), flipped(weight_b)).astype(jnp.bfloat16)
    grad_pre_a = (spread_cells(grad_pooled) * silu_slope(pre_a)).astype(jnp.bfloat16)
    local_a = weight_grad(padded, grad_pre_a)
    grad_rimmed = extended(grad_pre_a, (("slab", 1),), 1)
    grad_cubes = conv_valid(pad_sides(grad_rimmed), flipped(weight_a)).astype(jnp.bfloat16)
    summed_a, summed_b = sum_kernels(local_a, local_b)
    return (features, grad_cubes, summed_a, summed_b)


def solution(mesh):
    return jax.shard_map(
        shards,
        mesh=mesh,
        in_specs=(P("rep", "slab", None, None, None), P(), P(), P("rep", "slab", None, None, None)),
        out_specs=(
            P("rep", "slab", None, None, None),
            P("rep", "slab", None, None, None),
            P(),
            P(),
        ),
        check_vma=False,
    )
```

```python
import jax
import jax.numpy as jnp
from jax import lax
from jax.experimental import pallas as pl
from jax.experimental.pallas import tpu as pltpu
from jax.sharding import PartitionSpec as P

BF16 = jnp.bfloat16
F32 = jnp.float32
ROOM = 50 * 1024 * 1024


def nt_dot(lhs, rhs):
    return lax.dot_general(lhs, rhs, (((1,), (1,)), ((), ())), preferred_element_type=F32)


def nn_dot(lhs, rhs):
    return jnp.dot(lhs, rhs, preferred_element_type=F32)


def next_rows(value, period):
    rows = value.shape[0]
    row = lax.broadcasted_iota(jnp.int32, value.shape, 0) % period
    return jnp.where(row == period - 1, 0.0, pltpu.roll(value, rows - 1, 0))


def previous_rows(value, period):
    row = lax.broadcasted_iota(jnp.int32, value.shape, 0) % period
    return jnp.where(row == 0, 0.0, pltpu.roll(value, 1, 0))


def low_lanes(shape):
    return lax.broadcasted_iota(jnp.int32, shape, 1) < 64


def forward_a_kernel(left_ref, cells_ref, right_ref, weight_ref, window_ref, slope_ref, pooled_ref):
    edge = jnp.zeros((16, 256), BF16)
    for layer in range(6):
        if layer == 0:
            pairs = left_ref[...]
        elif layer == 5:
            pairs = right_ref[...]
        else:
            pairs = cells_ref[layer - 1]
        wide = pairs.astype(F32)
        outer = jnp.where(low_lanes(wide.shape), next_rows(wide, 16), previous_rows(wide, 16))
        window_ref[layer, 0:16, :] = edge
        window_ref[layer, 528:544, :] = edge
        window_ref[layer, 16:528, 0:128] = pairs
        window_ref[layer, 16:528, 128:256] = outer.astype(BF16)
    for half in range(2):
        total = None
        for tap in range(9):
            shift_x, shift_y = tap // 3, tap % 3
            first = 2 * half + shift_x
            window = window_ref[first : first + 2, 16 * shift_y : 16 * shift_y + 512, :]
            term = nn_dot(window.reshape(1024, 256), weight_ref[tap])
            total = term if total is None else total + term
        sigma = 1.0 / (1.0 + jnp.exp(-total))
        active = total * sigma
        slope = sigma * (1.0 + total * (1.0 - sigma))
        slope_ref[2 * half : 2 * half + 2] = slope.astype(BF16).reshape(2, 512, 256)
        blocks = active.reshape(2, 16, 2, 16, 256)
        blocks = (blocks[0] + blocks[1])
        blocks = blocks[:, 0] + blocks[:, 1]
        pooled = (blocks[:, :, :128] + blocks[:, :, 128:]) * 0.125
        pooled_ref[half] = pooled.astype(BF16).reshape(256, 128)


def forward_a(left, cells, right, weight):
    return pl.pallas_call(
        forward_a_kernel,
        out_shape=(
            jax.ShapeDtypeStruct((6, 544, 256), BF16),
            jax.ShapeDtypeStruct((4, 512, 256), BF16),
            jax.ShapeDtypeStruct((2, 256, 128), BF16),
        ),
        compiler_params=pltpu.CompilerParams(vmem_limit_bytes=ROOM),
        cost_estimate=pl.CostEstimate(flops=2 * 2048 * 2304 * 256, bytes_accessed=6 * 10**6, transcendentals=10**6),
    )(left, cells, right, weight)


def block_b_kernel(left_ref, cells_ref, right_ref, weight_ref, cot_ref, features_ref, low_ref, high_ref, grad_ref, window, grads, column):
    edge = jnp.zeros((16, 384), BF16)
    for layer in range(6):
        if layer < 2:
            cells = left_ref[layer]
        elif layer < 4:
            cells = cells_ref[layer - 2]
        else:
            cells = right_ref[layer - 4]
        wide = cells.astype(F32)
        window[layer, 0:16, :] = edge
        window[layer, 272:288, :] = edge
        window[layer, 16:272, 0:128] = previous_rows(wide, 16).astype(BF16)
        window[layer, 16:272, 128:256] = cells
        window[layer, 16:272, 256:384] = next_rows(wide, 16).astype(BF16)
    total = None
    for tap in range(9):
        shift_x, shift_y = tap // 3, tap % 3
        view = window[shift_x : shift_x + 4, 16 * shift_y : 16 * shift_y + 256, :]
        term = nn_dot(view.reshape(1024, 384), weight_ref[tap])
        total = term if total is None else total + term
    sigma = 1.0 / (1.0 + jnp.exp(-total))
    active = (total * sigma)[256:768].reshape(2, 8, 2, 16, 256)
    active = active[0] + active[1]
    active = (active[:, 0] + active[:, 1]).reshape(128, 256)
    for part in range(2):
        lanes = slice(128 * part, 128 * part + 128)
        column[part] = active[:, lanes]
        pooled = column[part, pl.ds(0, 64, stride=2), :] + column[part, pl.ds(1, 64, stride=2), :]
        features_ref[:, lanes] = (pooled * 0.125).astype(BF16)
    slope = sigma * (1.0 + total * (1.0 - sigma))
    for layer in range(4):
        spread = cot_ref[(layer + 1) // 2].astype(F32).reshape(8, 1, 16, 256) * 0.125
        spread = jnp.broadcast_to(spread, (8, 2, 16, 256)).reshape(256, 256)
        grads[layer, 0:16, :] = edge[:, :256]
        grads[layer, 272:288, :] = edge[:, :256]
        grads[layer, 16:272, :] = (spread * slope[256 * layer : 256 * layer + 256]).astype(BF16)
    own = grads[1:3, 16:272, :].reshape(512, 256)
    turned = own.T
    for tap in range(9):
        shift_x, shift_y = tap // 3, tap % 3
        view = window[1 + shift_x : 3 + shift_x, 16 * shift_y : 16 * shift_y + 256, :].reshape(512, 384)
        terms = (nn_dot(turned, view) * 0.25).T.astype(BF16)
        low_ref[tap] = terms[:, :128]
        high_ref[tap] = terms[:, 128:]
    total = None
    for tap in range(9):
        shift_x, shift_y = tap // 3, tap % 3
        view = grads[2 - shift_x : 4 - shift_x, 32 - 16 * shift_y : 288 - 16 * shift_y, :].reshape(512, 256)
        term = nt_dot(view, weight_ref[tap])
        total = term if total is None else total + term
    result = next_rows(total[:, 0:128], 16) + total[:, 128:256] + previous_rows(total[:, 256:384], 16)
    grad_ref[...] = result.astype(BF16).reshape(2, 256, 128)


def block_b(left, cells, right, weight, cot):
    return pl.pallas_call(
        block_b_kernel,
        out_shape=(
            jax.ShapeDtypeStruct((64, 256), BF16),
            jax.ShapeDtypeStruct((9, 384, 128), BF16),
            jax.ShapeDtypeStruct((9, 384, 128), BF16),
            jax.ShapeDtypeStruct((2, 256, 128), BF16),
        ),
        scratch_shapes=[
            pltpu.VMEM((6, 288, 384), BF16),
            pltpu.VMEM((4, 288, 256), BF16),
            pltpu.VMEM((2, 128, 128), F32),
        ],
        compiler_params=pltpu.CompilerParams(vmem_limit_bytes=ROOM),
        cost_estimate=pl.CostEstimate(flops=4 * 2 * 512 * 3456 * 256, bytes_accessed=5 * 10**6, transcendentals=5 * 10**5),
    )(left, cells, right, weight, cot)


def kernel_a_kernel(grad_ref, slope_ref, window_ref, pre_ref, kernel_ref):
    for layer in range(4):
        spread = grad_ref[layer // 2].astype(F32).reshape(16, 1, 16, 128) * 0.125
        spread = jnp.broadcast_to(spread, (16, 2, 16, 128)).reshape(512, 128)
        slope = slope_ref[layer].astype(F32)
        pre_ref[layer, :, 0:128] = (spread * slope[:, 0:128]).astype(BF16)
        pre_ref[layer, :, 128:256] = (spread * slope[:, 128:256]).astype(BF16)
    turned = pre_ref[...].reshape(2048, 256).T
    for tap in range(9):
        shift_x, shift_y = tap // 3, tap % 3
        view = window_ref[shift_x : shift_x + 4, 16 * shift_y : 16 * shift_y + 512, :].reshape(2048, 256)
        terms = nn_dot(turned, view)
        terms = (terms[:128] + pltpu.roll(terms[128:], 192, 1)) * 0.25
        terms = terms.T.astype(BF16)
        kernel_ref[tap, 0:64] = terms[192:256]
        kernel_ref[tap, 64:192] = terms[0:128]


def kernel_a(grad, slope, window):
    return pl.pallas_call(
        kernel_a_kernel,
        out_shape=(
            jax.ShapeDtypeStruct((4, 512, 256), BF16),
            jax.ShapeDtypeStruct((9, 192, 128), BF16),
        ),
        compiler_params=pltpu.CompilerParams(vmem_limit_bytes=ROOM),
        cost_estimate=pl.CostEstimate(flops=2 * 2048 * 2304 * 256, bytes_accessed=6 * 10**6, transcendentals=0),
    )(grad, slope, window)


def back_a_kernel(left_ref, cells_ref, right_ref, weight_ref, out_ref, grads):
    edge = jnp.zeros((16, 256), BF16)
    for layer in range(6):
        grads[layer, 0:16, :] = edge
        grads[layer, 528:544, :] = edge
        if layer == 0:
            grads[layer, 16:528, :] = left_ref[...]
        elif layer == 5:
            grads[layer, 16:528, :] = right_ref[...]
        else:
            grads[layer, 16:528, :] = cells_ref[layer - 1]
    for half in range(2):
        total = None
        for tap in range(9):
            shift_x, shift_y = tap // 3, tap % 3
            first = 2 * half + 2 - shift_x
            view = grads[first : first + 2, 32 - 16 * shift_y : 544 - 16 * shift_y, :].reshape(1024, 256)
            term = nt_dot(view, weight_ref[tap])
            total = term if total is None else total + term
        outer = total[:, 128:256]
        outer = jnp.where(low_lanes(outer.shape), previous_rows(outer, 16), next_rows(outer, 16))
        out_ref[2 * half : 2 * half + 2] = (total[:, 0:128] + outer).astype(BF16).reshape(2, 512, 128)


def back_a(left, cells, right, weight):
    return pl.pallas_call(
        back_a_kernel,
        out_shape=jax.ShapeDtypeStruct((4, 512, 128), BF16),
        scratch_shapes=[pltpu.VMEM((6, 544, 256), BF16)],
        compiler_params=pltpu.CompilerParams(vmem_limit_bytes=ROOM),
        cost_estimate=pl.CostEstimate(flops=2 * 2048 * 2304 * 256, bytes_accessed=5 * 10**6, transcendentals=0),
    )(left, cells, right, weight)


def paired_weight(weight):
    taps = weight.reshape(9, 3, 64, 128)
    none = jnp.zeros((9, 64, 128), weight.dtype)
    even = jnp.concatenate([taps[:, 1], taps[:, 2], none, taps[:, 0]], axis=1)
    odd = jnp.concatenate([taps[:, 0], taps[:, 1], taps[:, 2], none], axis=1)
    return jnp.concatenate([even, odd], axis=2)


AXES = ("slab", "rep")
SIZES = {"x": 4, "y": 4, "zl": 4, "zh": 2, "core": 2}


def coordinates(index):
    slab, rep = divmod(index, 4)
    return {"x": slab // 16, "y": slab // 4 % 4, "zl": slab % 4, "zh": rep // 2, "core": rep % 2}


def index_of(place):
    return ((place["x"] * 4 + place["y"]) * 4 + place["zl"]) * 4 + place["zh"] * 2 + place["core"]


def move(value, dim, step):
    pairs = []
    for source in range(256):
        place = coordinates(source)
        place[dim] = (place[dim] + step) % SIZES[dim]
        pairs.append((source, index_of(place)))
    return lax.ppermute(value, AXES, pairs)


def own_coordinate(dim):
    slab, rep = lax.axis_index("slab"), lax.axis_index("rep")
    return {"x": slab // 16, "y": slab // 4 % 4, "zl": slab % 4, "zh": rep // 2, "core": rep % 2}[dim]


def chunk(value, index, count):
    rows = value.shape[0] // count
    return lax.dynamic_slice_in_dim(value, index * rows, rows, axis=0)


def send_shares(value, dim):
    here, count = own_coordinate(dim), SIZES[dim]
    return [move(chunk(value, (here + step) % count, count), dim, step) for step in range(1, count)]


def add_shares(value, shares, dim):
    total = chunk(value, own_coordinate(dim), SIZES[dim]).astype(F32)
    for share in shares:
        total = total + share.astype(F32)
    return total.astype(BF16)


def send_block(block, dim):
    return [move(block, dim, step) for step in range(1, SIZES[dim])]


def join_blocks(block, others, dim):
    here, count = own_coordinate(dim), SIZES[dim]
    rows = block.shape[0]
    whole = jnp.zeros((rows * count, block.shape[1]), block.dtype)
    for step, piece in enumerate([block] + others):
        whole = lax.dynamic_update_slice_in_dim(whole, piece, (here - step) % count * rows, axis=0)
    return whole


def reduce_over_chips(rows):
    half = rows.shape[0] // 2
    first, second = rows[:half], rows[half:]
    shares_first, shares_second = send_shares(first, "x"), send_shares(second, "y")
    first, second = add_shares(first, shares_first, "x"), add_shares(second, shares_second, "y")
    shares_first, shares_second = send_shares(first, "y"), send_shares(second, "x")
    first, second = add_shares(first, shares_first, "y"), add_shares(second, shares_second, "x")
    both = jnp.concatenate([first, second])
    (other,) = send_block(both, "zh")
    both = (both.astype(F32) + other.astype(F32)).astype(BF16)
    one, two, three = (piece.astype(F32) for piece in send_block(both, "zl"))
    both = ((both.astype(F32) + two) + (one + three)).astype(BF16)
    half = both.shape[0] // 2
    first, second = both[:half], both[half:]
    got_first, got_second = send_block(first, "y"), send_block(second, "x")
    first, second = join_blocks(first, got_first, "y"), join_blocks(second, got_second, "x")
    got_first, got_second = send_block(first, "x"), send_block(second, "y")
    return join_blocks(first, got_first, "x"), join_blocks(second, got_second, "y")


def neighbours(to_left, to_right):
    count = lax.axis_size("slab")
    up = [(i, i + 1) for i in range(count - 1)]
    down = [(i + 1, i) for i in range(count - 1)]
    return lax.ppermute(to_right, "slab", up), lax.ppermute(to_left, "slab", down)


def shards(cubes, weight_a, weight_b, cotangent):
    core = own_coordinate("core")
    pair_weight = paired_weight(weight_a)
    taps_b = weight_b.reshape(9, 384, 256)
    cells = cubes.reshape(4, 512, 128)
    cot = cotangent.reshape(64, 256)
    cot_rows = [cot[:, :128], cot[:, 128:]]
    left, right = neighbours(jnp.concatenate([cells[0]] + cot_rows), jnp.concatenate([cells[3]] + cot_rows))
    window, slope_a, pooled = forward_a(left[:512], cells, right[:512], pair_weight)
    pooled_left, pooled_right = neighbours(pooled, pooled)
    cots = [jnp.concatenate([side[512:576], side[576:640]], axis=1) for side in (left, right)]
    cots = jnp.stack([cots[0], cot, cots[1]])
    cots = jnp.broadcast_to(cots[:, :, None, :], (3, 64, 2, 256)).reshape(3, 128, 256)
    features, low, high, grad_pooled = block_b(pooled_left, pooled, pooled_right, taps_b, cots)
    low, high = low.reshape(3456, 128), high.reshape(3456, 128)
    other_b = move(jnp.where(core == 0, high, low), "core", 1)
    grad_pre, local_a = kernel_a(grad_pooled, slope_a, window)
    local_a = local_a.reshape(1728, 128)
    other_a = move(chunk(local_a, 1 - core, 2), "core", 1)
    grad_left, grad_right = neighbours(grad_pre[0], grad_pre[3])
    grad_cubes = back_a(grad_left, grad_pre, grad_right, pair_weight)
    rows_b = jnp.where(core == 0, low, high).astype(F32) + other_b.astype(F32)
    rows_a = chunk(local_a, core, 2).astype(F32) + other_a.astype(F32)
    rows = jnp.concatenate([rows_a.astype(BF16), rows_b.astype(BF16), jnp.zeros((32, 128), BF16)])
    first, second = reduce_over_chips(rows)
    first_away, second_away = move(first, "core", 1), move(second, "core", 1)
    mine, away = jnp.concatenate([first, second]), jnp.concatenate([first_away, second_away])
    zero, one = jnp.where(core == 0, mine, away), jnp.where(core == 0, away, mine)
    sum_a = jnp.concatenate([zero[:864], one[:864]]).astype(F32)
    sum_b = jnp.concatenate([zero[864:4320], one[864:4320]], axis=1).astype(F32)
    return (
        features.reshape(1, 1, 8, 8, 256),
        grad_cubes.reshape(1, 4, 32, 32, 64),
        sum_a.reshape(3, 3, 3, 64, 128),
        sum_b.reshape(3, 3, 3, 128, 256),
    )


def solution(mesh):
    return jax.shard_map(
        shards,
        mesh=mesh,
        in_specs=(P("rep", "slab", None, None, None), P(), P(), P("rep", "slab", None, None, None)),
        out_specs=(
            P("rep", "slab", None, None, None),
            P("rep", "slab", None, None, None),
            P(),
            P(),
        ),
        check_vma=False,
    )
```

```python
import jax
import jax.numpy as jnp
from jax import lax
from jax.experimental import pallas as pl
from jax.experimental.pallas import tpu as pltpu
from jax.sharding import PartitionSpec as P

BF16 = jnp.bfloat16
F32 = jnp.float32
ROOM = 50 * 1024 * 1024
SCALAR = pl.BlockSpec(memory_space=pltpu.SMEM)
WHOLE = pl.BlockSpec(memory_space=pltpu.VMEM)


def nt_dot(lhs, rhs):
    return lax.dot_general(lhs, rhs, (((1,), (1,)), ((), ())), preferred_element_type=F32)


def nn_dot(lhs, rhs):
    return jnp.dot(lhs, rhs, preferred_element_type=F32)


def next_rows(value, period):
    rows = value.shape[0]
    row = lax.broadcasted_iota(jnp.int32, value.shape, 0) % period
    return jnp.where(row == period - 1, 0.0, pltpu.roll(value, rows - 1, 0))


def previous_rows(value, period):
    row = lax.broadcasted_iota(jnp.int32, value.shape, 0) % period
    return jnp.where(row == 0, 0.0, pltpu.roll(value, 1, 0))


def low_lanes(shape):
    return lax.broadcasted_iota(jnp.int32, shape, 1) < 64


def forward_a_kernel(left_ref, cells_ref, right_ref, weight_ref, window_ref, slope_ref, pooled_ref):
    edge = jnp.zeros((16, 256), BF16)
    for layer in range(6):
        if layer == 0:
            pairs = left_ref[...]
        elif layer == 5:
            pairs = right_ref[...]
        else:
            pairs = cells_ref[layer - 1]
        wide = pairs.astype(F32)
        outer = jnp.where(low_lanes(wide.shape), next_rows(wide, 16), previous_rows(wide, 16))
        window_ref[layer, 0:16, :] = edge
        window_ref[layer, 528:544, :] = edge
        window_ref[layer, 16:528, 0:128] = pairs
        window_ref[layer, 16:528, 128:256] = outer.astype(BF16)
    for half in range(2):
        total = None
        for tap in range(9):
            shift_x, shift_y = tap // 3, tap % 3
            first = 2 * half + shift_x
            window = window_ref[first : first + 2, 16 * shift_y : 16 * shift_y + 512, :]
            term = nn_dot(window.reshape(1024, 256), weight_ref[tap])
            total = term if total is None else total + term
        sigma = 1.0 / (1.0 + jnp.exp(-total))
        active = total * sigma
        slope = sigma * (1.0 + total * (1.0 - sigma))
        slope_ref[2 * half : 2 * half + 2] = slope.astype(BF16).reshape(2, 512, 256)
        blocks = active.reshape(2, 16, 2, 16, 256)
        blocks = (blocks[0] + blocks[1])
        blocks = blocks[:, 0] + blocks[:, 1]
        pooled = (blocks[:, :, :128] + blocks[:, :, 128:]) * 0.125
        pooled_ref[half] = pooled.astype(BF16).reshape(256, 128)


def forward_a(left, cells, right, weight):
    return pl.pallas_call(
        forward_a_kernel,
        out_shape=(
            jax.ShapeDtypeStruct((6, 544, 256), BF16),
            jax.ShapeDtypeStruct((4, 512, 256), BF16),
            jax.ShapeDtypeStruct((2, 256, 128), BF16),
        ),
        compiler_params=pltpu.CompilerParams(vmem_limit_bytes=ROOM),
        cost_estimate=pl.CostEstimate(flops=2 * 2048 * 2304 * 256, bytes_accessed=6 * 10**6, transcendentals=10**6),
    )(left, cells, right, weight)


def block_b_kernel(core_ref, left_ref, cells_ref, right_ref, weight_ref, cot_ref, features_ref, keep_ref, send_ref, grad_ref, window, grads, column):
    edge = jnp.zeros((16, 384), BF16)
    for layer in range(6):
        if layer < 2:
            cells = left_ref[layer]
        elif layer < 4:
            cells = cells_ref[layer - 2]
        else:
            cells = right_ref[layer - 4]
        wide = cells.astype(F32)
        window[layer, 0:16, :] = edge
        window[layer, 272:288, :] = edge
        window[layer, 16:272, 0:128] = previous_rows(wide, 16).astype(BF16)
        window[layer, 16:272, 128:256] = cells
        window[layer, 16:272, 256:384] = next_rows(wide, 16).astype(BF16)
    total = None
    for tap in range(9):
        shift_x, shift_y = tap // 3, tap % 3
        view = window[shift_x : shift_x + 4, 16 * shift_y : 16 * shift_y + 256, :]
        term = nn_dot(view.reshape(1024, 384), weight_ref[tap])
        total = term if total is None else total + term
    sigma = 1.0 / (1.0 + jnp.exp(-total))
    active = (total * sigma)[256:768].reshape(2, 8, 2, 16, 256)
    active = active[0] + active[1]
    active = (active[:, 0] + active[:, 1]).reshape(128, 256)
    for part in range(2):
        lanes = slice(128 * part, 128 * part + 128)
        column[part] = active[:, lanes]
        pooled = column[part, pl.ds(0, 64, stride=2), :] + column[part, pl.ds(1, 64, stride=2), :]
        features_ref[:, lanes] = (pooled * 0.125).astype(BF16)
    slope = sigma * (1.0 + total * (1.0 - sigma))
    for layer in range(4):
        spread = cot_ref[(layer + 1) // 2].astype(F32).reshape(8, 1, 16, 256) * 0.125
        spread = jnp.broadcast_to(spread, (8, 2, 16, 256)).reshape(256, 256)
        grads[layer, 0:16, :] = edge[:, :256]
        grads[layer, 272:288, :] = edge[:, :256]
        grads[layer, 16:272, :] = (spread * slope[256 * layer : 256 * layer + 256]).astype(BF16)
    core = core_ref[0]
    own = grads[1:3, 16:272, :].reshape(512, 256)
    turned = own.T
    for tap in range(9):
        shift_x, shift_y = tap // 3, tap % 3
        view = window[1 + shift_x : 3 + shift_x, 16 * shift_y : 16 * shift_y + 256, :].reshape(512, 384)
        terms = (nn_dot(turned, view) * 0.25).T.astype(BF16)
        keep_ref[tap] = jnp.where(core == 0, terms[:, :128], terms[:, 128:])
        send_ref[tap] = jnp.where(core == 0, terms[:, 128:], terms[:, :128])
    total = None
    for tap in range(9):
        shift_x, shift_y = tap // 3, tap % 3
        view = grads[2 - shift_x : 4 - shift_x, 32 - 16 * shift_y : 288 - 16 * shift_y, :].reshape(512, 256)
        term = nt_dot(view, weight_ref[tap])
        total = term if total is None else total + term
    result = next_rows(total[:, 0:128], 16) + total[:, 128:256] + previous_rows(total[:, 256:384], 16)
    grad_ref[...] = result.astype(BF16).reshape(2, 256, 128)


def block_b(core, left, cells, right, weight, cot):
    return pl.pallas_call(
        block_b_kernel,
        in_specs=[SCALAR] + [WHOLE] * 5,
        out_shape=(
            jax.ShapeDtypeStruct((64, 256), BF16),
            jax.ShapeDtypeStruct((9, 384, 128), BF16),
            jax.ShapeDtypeStruct((9, 384, 128), BF16),
            jax.ShapeDtypeStruct((2, 256, 128), BF16),
        ),
        scratch_shapes=[
            pltpu.VMEM((6, 288, 384), BF16),
            pltpu.VMEM((4, 288, 256), BF16),
            pltpu.VMEM((2, 128, 128), F32),
        ],
        compiler_params=pltpu.CompilerParams(vmem_limit_bytes=ROOM),
        cost_estimate=pl.CostEstimate(flops=4 * 2 * 512 * 3456 * 256, bytes_accessed=5 * 10**6, transcendentals=5 * 10**5),
    )(core, left, cells, right, weight, cot)


def kernel_a_kernel(core_ref, grad_ref, slope_ref, window_ref, pre_ref, keep_ref, send_ref):
    core = core_ref[0]
    for layer in range(4):
        spread = grad_ref[layer // 2].astype(F32).reshape(16, 1, 16, 128) * 0.125
        spread = jnp.broadcast_to(spread, (16, 2, 16, 128)).reshape(512, 128)
        slope = slope_ref[layer].astype(F32)
        pre_ref[layer, :, 0:128] = (spread * slope[:, 0:128]).astype(BF16)
        pre_ref[layer, :, 128:256] = (spread * slope[:, 128:256]).astype(BF16)
    turned = pre_ref[...].reshape(2048, 256).T
    for tap in range(9):
        shift_x, shift_y = tap // 3, tap % 3
        view = window_ref[shift_x : shift_x + 4, 16 * shift_y : 16 * shift_y + 512, :].reshape(2048, 256)
        terms = nn_dot(turned, view)
        terms = (terms[:128] + pltpu.roll(terms[128:], 192, 1)) * 0.25
        terms = terms.T.astype(BF16)
        first = jnp.concatenate([terms[192:256], terms[0:32]])
        second = terms[32:128]
        keep_ref[tap] = jnp.where(core == 0, first, second)
        send_ref[tap] = jnp.where(core == 0, second, first)


def kernel_a(core, grad, slope, window):
    return pl.pallas_call(
        kernel_a_kernel,
        in_specs=[SCALAR] + [WHOLE] * 3,
        out_shape=(
            jax.ShapeDtypeStruct((4, 512, 256), BF16),
            jax.ShapeDtypeStruct((9, 96, 128), BF16),
            jax.ShapeDtypeStruct((9, 96, 128), BF16),
        ),
        compiler_params=pltpu.CompilerParams(vmem_limit_bytes=ROOM),
        cost_estimate=pl.CostEstimate(flops=2 * 2048 * 2304 * 256, bytes_accessed=6 * 10**6, transcendentals=0),
    )(core, grad, slope, window)


def back_a_kernel(left_ref, cells_ref, right_ref, weight_ref, out_ref, grads):
    edge = jnp.zeros((16, 256), BF16)
    for layer in range(6):
        grads[layer, 0:16, :] = edge
        grads[layer, 528:544, :] = edge
        if layer == 0:
            grads[layer, 16:528, :] = left_ref[...]
        elif layer == 5:
            grads[layer, 16:528, :] = right_ref[...]
        else:
            grads[layer, 16:528, :] = cells_ref[layer - 1]
    for half in range(2):
        total = None
        for tap in range(9):
            shift_x, shift_y = tap // 3, tap % 3
            first = 2 * half + 2 - shift_x
            view = grads[first : first + 2, 32 - 16 * shift_y : 544 - 16 * shift_y, :].reshape(1024, 256)
            term = nt_dot(view, weight_ref[tap])
            total = term if total is None else total + term
        outer = total[:, 128:256]
        outer = jnp.where(low_lanes(outer.shape), previous_rows(outer, 16), next_rows(outer, 16))
        out_ref[2 * half : 2 * half + 2] = (total[:, 0:128] + outer).astype(BF16).reshape(2, 512, 128)


def back_a(left, cells, right, weight):
    return pl.pallas_call(
        back_a_kernel,
        out_shape=jax.ShapeDtypeStruct((4, 512, 128), BF16),
        scratch_shapes=[pltpu.VMEM((6, 544, 256), BF16)],
        compiler_params=pltpu.CompilerParams(vmem_limit_bytes=ROOM),
        cost_estimate=pl.CostEstimate(flops=2 * 2048 * 2304 * 256, bytes_accessed=5 * 10**6, transcendentals=0),
    )(left, cells, right, weight)


def paired_weight(weight):
    taps = weight.reshape(9, 3, 64, 128)
    none = jnp.zeros((9, 64, 128), weight.dtype)
    even = jnp.concatenate([taps[:, 1], taps[:, 2], none, taps[:, 0]], axis=1)
    odd = jnp.concatenate([taps[:, 0], taps[:, 1], taps[:, 2], none], axis=1)
    return jnp.concatenate([even, odd], axis=2)


def unpack_kernel(core_ref, mine_ref, away_ref, sum_a_ref, sum_b_ref):
    core = core_ref[0]
    for tap in range(9):
        rows = slice(96 * tap, 96 * tap + 96)
        mine, away = mine_ref[rows].astype(F32), away_ref[rows].astype(F32)
        sum_a_ref[tap, 0] = jnp.where(core == 0, mine, away)
        sum_a_ref[tap, 1] = jnp.where(core == 0, away, mine)
        rows = slice(864 + 384 * tap, 1248 + 384 * tap)
        mine, away = mine_ref[rows].astype(F32), away_ref[rows].astype(F32)
        sum_b_ref[tap, :, 0:128] = jnp.where(core == 0, mine, away)
        sum_b_ref[tap, :, 128:256] = jnp.where(core == 0, away, mine)


def unpack(core, mine, away):
    return pl.pallas_call(
        unpack_kernel,
        in_specs=[SCALAR] + [WHOLE] * 2,
        out_shape=(
            jax.ShapeDtypeStruct((9, 2, 96, 128), F32),
            jax.ShapeDtypeStruct((9, 384, 256), F32),
        ),
        compiler_params=pltpu.CompilerParams(vmem_limit_bytes=ROOM),
        cost_estimate=pl.CostEstimate(flops=0, bytes_accessed=7 * 10**6, transcendentals=0),
    )(core, mine, away)


AXES = ("slab", "rep")
ACROSS = [[((16 * x + 4 * y + z) * 4 + rep) for x in range(4) for y in range(4)] for z in range(4) for rep in range(4)]
ALONG = [[((4 * plane + z) * 4 + 2 * far + core) for far in range(2) for z in range(4)] for plane in range(16) for core in range(2)]
CORES = [(device, device ^ 1) for device in range(256)]


def other_core(value):
    return lax.ppermute(value, AXES, CORES)


def exchange(blocks, groups):
    return lax.all_to_all(blocks, AXES, 0, 0, axis_index_groups=groups, tiled=True)


def total_of(blocks):
    return jnp.sum(blocks.astype(F32), axis=0).astype(BF16)


def reduce_over_chips(rows):
    part = total_of(exchange(rows.reshape(16, 272, 128), ACROSS))
    part = total_of(exchange(jnp.broadcast_to(part, (8, 272, 128)), ALONG))
    return exchange(jnp.broadcast_to(part, (16, 272, 128)), ACROSS).reshape(4352, 128)


def neighbours(to_left, to_right):
    count = lax.axis_size("slab")
    up = [(i, i + 1) for i in range(count - 1)]
    down = [(i + 1, i) for i in range(count - 1)]
    return lax.ppermute(to_right, "slab", up), lax.ppermute(to_left, "slab", down)


def shards(cubes, weight_a, weight_b, cotangent):
    core = (lax.axis_index("rep") % 2).reshape(1)
    pair_weight = paired_weight(weight_a)
    taps_b = weight_b.reshape(9, 384, 256)
    cells = cubes.reshape(4, 512, 128)
    cot = cotangent.reshape(64, 256)
    cot_rows = [cot[:, :128], cot[:, 128:]]
    left, right = neighbours(jnp.concatenate([cells[0]] + cot_rows), jnp.concatenate([cells[3]] + cot_rows))
    window, slope_a, pooled = forward_a(left[:512], cells, right[:512], pair_weight)
    pooled_left, pooled_right = neighbours(pooled, pooled)
    cots = [jnp.concatenate([side[512:576], side[576:640]], axis=1) for side in (left, right)]
    cots = jnp.stack([cots[0], cot, cots[1]])
    cots = jnp.broadcast_to(cots[:, :, None, :], (3, 64, 2, 256)).reshape(3, 128, 256)
    features, keep_b, send_b, grad_pooled = block_b(core, pooled_left, pooled, pooled_right, taps_b, cots)
    other_b = other_core(send_b)
    grad_pre, keep_a, send_a = kernel_a(core, grad_pooled, slope_a, window)
    other_a = other_core(send_a)
    grad_left, grad_right = neighbours(grad_pre[0], grad_pre[3])
    rows = [
        (keep.astype(F32) + other.astype(F32)).astype(BF16).reshape(-1, 128)
        for keep, other in ((keep_a, other_a), (keep_b, other_b))
    ]
    mine = reduce_over_chips(jnp.concatenate(rows + [jnp.zeros((32, 128), BF16)]))
    away = other_core(mine)
    grad_cubes = back_a(grad_left, grad_pre, grad_right, pair_weight)
    sum_a, sum_b = unpack(core, mine, away)
    return (
        features.reshape(1, 1, 8, 8, 256),
        grad_cubes.reshape(1, 4, 32, 32, 64),
        sum_a.reshape(3, 3, 3, 64, 128),
        sum_b.reshape(3, 3, 3, 128, 256),
    )


def solution(mesh):
    return jax.shard_map(
        shards,
        mesh=mesh,
        in_specs=(P("rep", "slab", None, None, None), P(), P(), P("rep", "slab", None, None, None)),
        out_specs=(
            P("rep", "slab", None, None, None),
            P("rep", "slab", None, None, None),
            P(),
            P(),
        ),
        check_vma=False,
    )
```

```python
import jax
import jax.numpy as jnp
from jax import lax
from jax.experimental import pallas as pl
from jax.experimental.pallas import tpu as pltpu
from jax.sharding import PartitionSpec as P

BF16 = jnp.bfloat16
F32 = jnp.float32
ROOM = 50 * 1024 * 1024
SCALAR = pl.BlockSpec(memory_space=pltpu.SMEM)
WHOLE = pl.BlockSpec(memory_space=pltpu.VMEM)


def nt_dot(lhs, rhs):
    return lax.dot_general(lhs, rhs, (((1,), (1,)), ((), ())), preferred_element_type=F32)


def nn_dot(lhs, rhs):
    return jnp.dot(lhs, rhs, preferred_element_type=F32)


def next_rows(value, period):
    rows = value.shape[0]
    row = lax.broadcasted_iota(jnp.int32, value.shape, 0) % period
    return jnp.where(row == period - 1, 0.0, pltpu.roll(value, rows - 1, 0))


def previous_rows(value, period):
    row = lax.broadcasted_iota(jnp.int32, value.shape, 0) % period
    return jnp.where(row == 0, 0.0, pltpu.roll(value, 1, 0))


def low_lanes(shape):
    return lax.broadcasted_iota(jnp.int32, shape, 1) < 64


def forward_a_kernel(left_ref, cells_ref, right_ref, weight_ref, window_ref, slope_ref, pooled_ref):
    edge = jnp.zeros((16, 256), BF16)
    for layer in range(6):
        if layer == 0:
            pairs = left_ref[...]
        elif layer == 5:
            pairs = right_ref[...]
        else:
            pairs = cells_ref[layer - 1]
        wide = pairs.astype(F32)
        outer = jnp.where(low_lanes(wide.shape), next_rows(wide, 16), previous_rows(wide, 16))
        window_ref[layer, 0:16, :] = edge
        window_ref[layer, 528:544, :] = edge
        window_ref[layer, 16:528, 0:128] = pairs
        window_ref[layer, 16:528, 128:256] = outer.astype(BF16)
    for half in range(2):
        total = None
        for tap in range(9):
            shift_x, shift_y = tap // 3, tap % 3
            first = 2 * half + shift_x
            window = window_ref[first : first + 2, 16 * shift_y : 16 * shift_y + 512, :]
            term = nn_dot(window.reshape(1024, 256), weight_ref[tap])
            total = term if total is None else total + term
        sigma = 1.0 / (1.0 + jnp.exp(-total))
        active = total * sigma
        slope = sigma * (1.0 + total * (1.0 - sigma))
        slope_ref[2 * half : 2 * half + 2] = slope.astype(BF16).reshape(2, 512, 256)
        blocks = active.reshape(2, 16, 2, 16, 256)
        blocks = (blocks[0] + blocks[1])
        blocks = blocks[:, 0] + blocks[:, 1]
        pooled = (blocks[:, :, :128] + blocks[:, :, 128:]) * 0.125
        pooled_ref[half] = pooled.astype(BF16).reshape(256, 128)


def forward_a(left, cells, right, weight):
    return pl.pallas_call(
        forward_a_kernel,
        out_shape=(
            jax.ShapeDtypeStruct((6, 544, 256), BF16),
            jax.ShapeDtypeStruct((4, 512, 256), BF16),
            jax.ShapeDtypeStruct((2, 256, 128), BF16),
        ),
        compiler_params=pltpu.CompilerParams(vmem_limit_bytes=ROOM),
        cost_estimate=pl.CostEstimate(flops=2 * 2048 * 2304 * 256, bytes_accessed=6 * 10**6, transcendentals=10**6),
    )(left, cells, right, weight)


def block_b_kernel(core_ref, left_ref, cells_ref, right_ref, weight_ref, cot_ref, features_ref, keep_ref, send_ref, grad_ref, window, grads, column):
    edge = jnp.zeros((16, 384), BF16)
    for layer in range(6):
        if layer < 2:
            cells = left_ref[layer]
        elif layer < 4:
            cells = cells_ref[layer - 2]
        else:
            cells = right_ref[layer - 4]
        wide = cells.astype(F32)
        window[layer, 0:16, :] = edge
        window[layer, 272:288, :] = edge
        window[layer, 16:272, 0:128] = previous_rows(wide, 16).astype(BF16)
        window[layer, 16:272, 128:256] = cells
        window[layer, 16:272, 256:384] = next_rows(wide, 16).astype(BF16)
    total = None
    for tap in range(9):
        shift_x, shift_y = tap // 3, tap % 3
        view = window[shift_x : shift_x + 4, 16 * shift_y : 16 * shift_y + 256, :]
        term = nn_dot(view.reshape(1024, 384), weight_ref[tap])
        total = term if total is None else total + term
    sigma = 1.0 / (1.0 + jnp.exp(-total))
    active = (total * sigma)[256:768].reshape(2, 8, 2, 16, 256)
    active = active[0] + active[1]
    active = (active[:, 0] + active[:, 1]).reshape(128, 256)
    for part in range(2):
        lanes = slice(128 * part, 128 * part + 128)
        column[part] = active[:, lanes]
        pooled = column[part, pl.ds(0, 64, stride=2), :] + column[part, pl.ds(1, 64, stride=2), :]
        features_ref[:, lanes] = (pooled * 0.125).astype(BF16)
    slope = sigma * (1.0 + total * (1.0 - sigma))
    for layer in range(4):
        spread = cot_ref[(layer + 1) // 2].astype(F32).reshape(8, 1, 16, 256) * 0.125
        spread = jnp.broadcast_to(spread, (8, 2, 16, 256)).reshape(256, 256)
        grads[layer, 0:16, :] = edge[:, :256]
        grads[layer, 272:288, :] = edge[:, :256]
        grads[layer, 16:272, :] = (spread * slope[256 * layer : 256 * layer + 256]).astype(BF16)
    core = core_ref[0]
    own = grads[1:3, 16:272, :].reshape(512, 256)
    turned = own.T
    for tap in range(9):
        shift_x, shift_y = tap // 3, tap % 3
        view = window[1 + shift_x : 3 + shift_x, 16 * shift_y : 16 * shift_y + 256, :].reshape(512, 384)
        terms = (nn_dot(turned, view) * 0.25).T.astype(BF16)
        keep_ref[tap] = jnp.where(core == 0, terms[:, :128], terms[:, 128:])
        send_ref[tap] = jnp.where(core == 0, terms[:, 128:], terms[:, :128])
    total = None
    for tap in range(9):
        shift_x, shift_y = tap // 3, tap % 3
        view = grads[2 - shift_x : 4 - shift_x, 32 - 16 * shift_y : 288 - 16 * shift_y, :].reshape(512, 256)
        term = nt_dot(view, weight_ref[tap])
        total = term if total is None else total + term
    result = next_rows(total[:, 0:128], 16) + total[:, 128:256] + previous_rows(total[:, 256:384], 16)
    grad_ref[...] = result.astype(BF16).reshape(2, 256, 128)


def block_b(core, left, cells, right, weight, cot):
    return pl.pallas_call(
        block_b_kernel,
        in_specs=[SCALAR] + [WHOLE] * 5,
        out_shape=(
            jax.ShapeDtypeStruct((64, 256), BF16),
            jax.ShapeDtypeStruct((9, 384, 128), BF16),
            jax.ShapeDtypeStruct((9, 384, 128), BF16),
            jax.ShapeDtypeStruct((2, 256, 128), BF16),
        ),
        scratch_shapes=[
            pltpu.VMEM((6, 288, 384), BF16),
            pltpu.VMEM((4, 288, 256), BF16),
            pltpu.VMEM((2, 128, 128), F32),
        ],
        compiler_params=pltpu.CompilerParams(vmem_limit_bytes=ROOM),
        cost_estimate=pl.CostEstimate(flops=4 * 2 * 512 * 3456 * 256, bytes_accessed=5 * 10**6, transcendentals=5 * 10**5),
    )(core, left, cells, right, weight, cot)


def kernel_a_kernel(core_ref, grad_ref, slope_ref, window_ref, pre_ref, keep_ref, send_ref):
    core = core_ref[0]
    for layer in range(4):
        spread = grad_ref[layer // 2].astype(F32).reshape(16, 1, 16, 128) * 0.125
        spread = jnp.broadcast_to(spread, (16, 2, 16, 128)).reshape(512, 128)
        slope = slope_ref[layer].astype(F32)
        pre_ref[layer, :, 0:128] = (spread * slope[:, 0:128]).astype(BF16)
        pre_ref[layer, :, 128:256] = (spread * slope[:, 128:256]).astype(BF16)
    turned = pre_ref[...].reshape(2048, 256).T
    for tap in range(9):
        shift_x, shift_y = tap // 3, tap % 3
        view = window_ref[shift_x : shift_x + 4, 16 * shift_y : 16 * shift_y + 512, :].reshape(2048, 256)
        terms = nn_dot(turned, view)
        terms = (terms[:128] + pltpu.roll(terms[128:], 192, 1)) * 0.25
        terms = terms.T.astype(BF16)
        first = jnp.concatenate([terms[192:256], terms[0:32]])
        second = terms[32:128]
        keep_ref[tap] = jnp.where(core == 0, first, second)
        send_ref[tap] = jnp.where(core == 0, second, first)


def kernel_a(core, grad, slope, window):
    return pl.pallas_call(
        kernel_a_kernel,
        in_specs=[SCALAR] + [WHOLE] * 3,
        out_shape=(
            jax.ShapeDtypeStruct((4, 512, 256), BF16),
            jax.ShapeDtypeStruct((9, 96, 128), BF16),
            jax.ShapeDtypeStruct((9, 96, 128), BF16),
        ),
        compiler_params=pltpu.CompilerParams(vmem_limit_bytes=ROOM),
        cost_estimate=pl.CostEstimate(flops=2 * 2048 * 2304 * 256, bytes_accessed=6 * 10**6, transcendentals=0),
    )(core, grad, slope, window)


def back_a_kernel(left_ref, cells_ref, right_ref, weight_ref, out_ref, grads):
    edge = jnp.zeros((16, 256), BF16)
    for layer in range(6):
        grads[layer, 0:16, :] = edge
        grads[layer, 528:544, :] = edge
        if layer == 0:
            grads[layer, 16:528, :] = left_ref[...]
        elif layer == 5:
            grads[layer, 16:528, :] = right_ref[...]
        else:
            grads[layer, 16:528, :] = cells_ref[layer - 1]
    for half in range(2):
        total = None
        for tap in range(9):
            shift_x, shift_y = tap // 3, tap % 3
            first = 2 * half + 2 - shift_x
            view = grads[first : first + 2, 32 - 16 * shift_y : 544 - 16 * shift_y, :].reshape(1024, 256)
            term = nt_dot(view, weight_ref[tap])
            total = term if total is None else total + term
        outer = total[:, 128:256]
        outer = jnp.where(low_lanes(outer.shape), previous_rows(outer, 16), next_rows(outer, 16))
        out_ref[2 * half : 2 * half + 2] = (total[:, 0:128] + outer).astype(BF16).reshape(2, 512, 128)


def back_a(left, cells, right, weight):
    return pl.pallas_call(
        back_a_kernel,
        out_shape=jax.ShapeDtypeStruct((4, 512, 128), BF16),
        scratch_shapes=[pltpu.VMEM((6, 544, 256), BF16)],
        compiler_params=pltpu.CompilerParams(vmem_limit_bytes=ROOM),
        cost_estimate=pl.CostEstimate(flops=2 * 2048 * 2304 * 256, bytes_accessed=5 * 10**6, transcendentals=0),
    )(left, cells, right, weight)


def paired_weight(weight):
    taps = weight.reshape(9, 3, 64, 128)
    none = jnp.zeros((9, 64, 128), weight.dtype)
    even = jnp.concatenate([taps[:, 1], taps[:, 2], none, taps[:, 0]], axis=1)
    odd = jnp.concatenate([taps[:, 0], taps[:, 1], taps[:, 2], none], axis=1)
    return jnp.concatenate([even, odd], axis=2)


def merge_kernel(keep_a_ref, other_a_ref, keep_b_ref, other_b_ref, rows_ref):
    for tap in range(9):
        rows = keep_a_ref[tap].astype(F32) + other_a_ref[tap].astype(F32)
        rows_ref[96 * tap : 96 * tap + 96] = rows.astype(BF16)
        rows = keep_b_ref[tap].astype(F32) + other_b_ref[tap].astype(F32)
        rows_ref[864 + 384 * tap : 1248 + 384 * tap] = rows.astype(BF16)
    rows_ref[4320:4352] = jnp.zeros((32, 128), BF16)


def merge(keep_a, other_a, keep_b, other_b):
    return pl.pallas_call(
        merge_kernel,
        out_shape=jax.ShapeDtypeStruct((4352, 128), BF16),
        compiler_params=pltpu.CompilerParams(vmem_limit_bytes=ROOM),
        cost_estimate=pl.CostEstimate(flops=0, bytes_accessed=4 * 10**6, transcendentals=0),
    )(keep_a, other_a, keep_b, other_b)


def unpack_kernel(core_ref, mine_ref, away_ref, sum_a_ref, sum_b_ref):
    core = core_ref[0]
    for tap in range(9):
        rows = slice(96 * tap, 96 * tap + 96)
        mine, away = mine_ref[rows].astype(F32), away_ref[rows].astype(F32)
        sum_a_ref[tap, 0] = jnp.where(core == 0, mine, away)
        sum_a_ref[tap, 1] = jnp.where(core == 0, away, mine)
        rows = slice(864 + 384 * tap, 1248 + 384 * tap)
        mine, away = mine_ref[rows].astype(F32), away_ref[rows].astype(F32)
        sum_b_ref[tap, :, 0:128] = jnp.where(core == 0, mine, away)
        sum_b_ref[tap, :, 128:256] = jnp.where(core == 0, away, mine)


def unpack(core, mine, away):
    return pl.pallas_call(
        unpack_kernel,
        in_specs=[SCALAR] + [WHOLE] * 2,
        out_shape=(
            jax.ShapeDtypeStruct((9, 2, 96, 128), F32),
            jax.ShapeDtypeStruct((9, 384, 256), F32),
        ),
        compiler_params=pltpu.CompilerParams(vmem_limit_bytes=ROOM),
        cost_estimate=pl.CostEstimate(flops=0, bytes_accessed=7 * 10**6, transcendentals=0),
    )(core, mine, away)


AXES = ("slab", "rep")
ACROSS = [[((16 * x + 4 * y + z) * 4 + rep) for x in range(4) for y in range(4)] for z in range(4) for rep in range(4)]
LINES = [[((4 * plane + z) * 4 + rep) for z in range(4)] for plane in range(16) for rep in range(4)]
CORES = [(device, device ^ 1) for device in range(256)]
FAR = [(device, device ^ 2) for device in range(256)]


def other_core(value):
    return lax.ppermute(value, AXES, CORES)


def exchange(blocks, groups):
    return lax.all_to_all(blocks, AXES, 0, 0, axis_index_groups=groups, tiled=True)


def total_of(blocks):
    return jnp.sum(blocks.astype(F32), axis=0).astype(BF16)


def reduce_over_chips(blocks):
    part = total_of(blocks)
    part = total_of(exchange(part.reshape(4, 68, 128), LINES))
    part = (part.astype(F32) + lax.ppermute(part, AXES, FAR).astype(F32)).astype(BF16)
    part = exchange(jnp.broadcast_to(part, (4, 68, 128)), LINES).reshape(272, 128)
    return exchange(jnp.broadcast_to(part, (16, 272, 128)), ACROSS).reshape(4352, 128)


def neighbours(to_left, to_right):
    count = lax.axis_size("slab")
    up = [(i, i + 1) for i in range(count - 1)]
    down = [(i + 1, i) for i in range(count - 1)]
    return lax.ppermute(to_right, "slab", up), lax.ppermute(to_left, "slab", down)


def shards(cubes, weight_a, weight_b, cotangent):
    core = (lax.axis_index("rep") % 2).reshape(1)
    pair_weight = paired_weight(weight_a)
    taps_b = weight_b.reshape(9, 384, 256)
    cells = cubes.reshape(4, 512, 128)
    cot = cotangent.reshape(64, 256)
    cot_rows = [cot[:, :128], cot[:, 128:]]
    left, right = neighbours(jnp.concatenate([cells[0]] + cot_rows), jnp.concatenate([cells[3]] + cot_rows))
    window, slope_a, pooled = forward_a(left[:512], cells, right[:512], pair_weight)
    pooled_left, pooled_right = neighbours(pooled, pooled)
    cots = [jnp.concatenate([side[512:576], side[576:640]], axis=1) for side in (left, right)]
    cots = jnp.stack([cots[0], cot, cots[1]])
    cots = jnp.broadcast_to(cots[:, :, None, :], (3, 64, 2, 256)).reshape(3, 128, 256)
    features, keep_b, send_b, grad_pooled = block_b(core, pooled_left, pooled, pooled_right, taps_b, cots)
    other_b = other_core(send_b)
    grad_pre, keep_a, send_a = kernel_a(core, grad_pooled, slope_a, window)
    other_a = other_core(send_a)
    grad_left, grad_right = neighbours(grad_pre[0], grad_pre[3])
    rows = merge(keep_a, other_a, keep_b, other_b)
    blocks = exchange(rows.reshape(16, 272, 128), ACROSS)
    blocks, grad_left, grad_right = lax.optimization_barrier((blocks, grad_left, grad_right))
    mine = reduce_over_chips(blocks)
    away = other_core(mine)
    grad_cubes = back_a(grad_left, grad_pre, grad_right, pair_weight)
    sum_a, sum_b = unpack(core, mine, away)
    return (
        features.reshape(1, 1, 8, 8, 256),
        grad_cubes.reshape(1, 4, 32, 32, 64),
        sum_a.reshape(3, 3, 3, 64, 128),
        sum_b.reshape(3, 3, 3, 128, 256),
    )


def solution(mesh):
    return jax.shard_map(
        shards,
        mesh=mesh,
        in_specs=(P("rep", "slab", None, None, None), P(), P(), P("rep", "slab", None, None, None)),
        out_specs=(
            P("rep", "slab", None, None, None),
            P("rep", "slab", None, None, None),
            P(),
            P(),
        ),
        check_vma=False,
    )
```

```python
import jax
import jax.numpy as jnp
from jax import lax
from jax.experimental import pallas as pl
from jax.experimental.pallas import tpu as pltpu
from jax.sharding import PartitionSpec as P

BF16 = jnp.bfloat16
F32 = jnp.float32
ROOM = 50 * 1024 * 1024
SCALAR = pl.BlockSpec(memory_space=pltpu.SMEM)
WHOLE = pl.BlockSpec(memory_space=pltpu.VMEM)


def nt_dot(lhs, rhs):
    return lax.dot_general(lhs, rhs, (((1,), (1,)), ((), ())), preferred_element_type=F32)


def nn_dot(lhs, rhs):
    return jnp.dot(lhs, rhs, preferred_element_type=F32)


def tn_dot(lhs, rhs):
    return lax.dot_general(lhs, rhs, (((0,), (0,)), ((), ())), preferred_element_type=F32)


def next_rows(value, period):
    rows = value.shape[0]
    row = lax.broadcasted_iota(jnp.int32, value.shape, 0) % period
    return jnp.where(row == period - 1, 0.0, pltpu.roll(value, rows - 1, 0))


def previous_rows(value, period):
    row = lax.broadcasted_iota(jnp.int32, value.shape, 0) % period
    return jnp.where(row == 0, 0.0, pltpu.roll(value, 1, 0))


def low_lanes(shape):
    return lax.broadcasted_iota(jnp.int32, shape, 1) < 64


def forward_a_kernel(left_ref, cells_ref, right_ref, weight_ref, window_ref, slope_ref, pooled_ref):
    edge = jnp.zeros((16, 256), BF16)
    for layer in range(6):
        if layer == 0:
            pairs = left_ref[...]
        elif layer == 5:
            pairs = right_ref[...]
        else:
            pairs = cells_ref[layer - 1]
        wide = pairs.astype(F32)
        outer = jnp.where(low_lanes(wide.shape), next_rows(wide, 16), previous_rows(wide, 16))
        window_ref[layer, 0:16, :] = edge
        window_ref[layer, 528:544, :] = edge
        window_ref[layer, 16:528, 0:128] = pairs
        window_ref[layer, 16:528, 128:256] = outer.astype(BF16)
    for half in range(2):
        total = None
        for tap in range(9):
            shift_x, shift_y = tap // 3, tap % 3
            first = 2 * half + shift_x
            window = window_ref[first : first + 2, 16 * shift_y : 16 * shift_y + 512, :]
            term = nn_dot(window.reshape(1024, 256), weight_ref[tap])
            total = term if total is None else total + term
        sigma = 1.0 / (1.0 + jnp.exp(-total))
        active = total * sigma
        slope = sigma * (1.0 + total * (1.0 - sigma))
        slope_ref[2 * half : 2 * half + 2] = slope.astype(BF16).reshape(2, 512, 256)
        blocks = active.reshape(2, 16, 2, 16, 256)
        blocks = (blocks[0] + blocks[1])
        blocks = blocks[:, 0] + blocks[:, 1]
        pooled = (blocks[:, :, :128] + blocks[:, :, 128:]) * 0.125
        pooled_ref[half] = pooled.astype(BF16).reshape(256, 128)


def forward_a(left, cells, right, weight):
    return pl.pallas_call(
        forward_a_kernel,
        out_shape=(
            jax.ShapeDtypeStruct((6, 544, 256), BF16),
            jax.ShapeDtypeStruct((4, 512, 256), BF16),
            jax.ShapeDtypeStruct((2, 256, 128), BF16),
        ),
        compiler_params=pltpu.CompilerParams(vmem_limit_bytes=ROOM),
        cost_estimate=pl.CostEstimate(flops=2 * 2048 * 2304 * 256, bytes_accessed=6 * 10**6, transcendentals=10**6),
    )(left, cells, right, weight)


def block_b_kernel(core_ref, left_ref, cells_ref, right_ref, weight_ref, cot_ref, features_ref, keep_ref, send_ref, grad_ref, window, grads, column):
    edge = jnp.zeros((16, 384), BF16)
    for layer in range(6):
        if layer < 2:
            cells = left_ref[layer]
        elif layer < 4:
            cells = cells_ref[layer - 2]
        else:
            cells = right_ref[layer - 4]
        wide = cells.astype(F32)
        window[layer, 0:16, :] = edge
        window[layer, 272:288, :] = edge
        window[layer, 16:272, 0:128] = previous_rows(wide, 16).astype(BF16)
        window[layer, 16:272, 128:256] = cells
        window[layer, 16:272, 256:384] = next_rows(wide, 16).astype(BF16)
    active = None
    for layer in range(4):
        total = None
        for tap in range(9):
            shift_x, shift_y = tap // 3, tap % 3
            view = window[layer + shift_x, 16 * shift_y : 16 * shift_y + 256, :]
            term = nn_dot(view, weight_ref[tap])
            total = term if total is None else total + term
        sigma = 1.0 / (1.0 + jnp.exp(-total))
        slope = sigma * (1.0 + total * (1.0 - sigma))
        spread = cot_ref[(layer + 1) // 2].astype(F32).reshape(8, 1, 16, 256) * 0.125
        spread = jnp.broadcast_to(spread, (8, 2, 16, 256)).reshape(256, 256)
        grads[layer, 0:16, :] = edge[:, :256]
        grads[layer, 272:288, :] = edge[:, :256]
        grads[layer, 16:272, :] = (spread * slope).astype(BF16)
        if layer in (1, 2):
            blocks = (total * sigma).reshape(8, 2, 16, 256)
            blocks = blocks[:, 0] + blocks[:, 1]
            active = blocks if active is None else active + blocks
    active = active.reshape(128, 256)
    for part in range(2):
        lanes = slice(128 * part, 128 * part + 128)
        column[part] = active[:, lanes]
        pooled = column[part, pl.ds(0, 64, stride=2), :] + column[part, pl.ds(1, 64, stride=2), :]
        features_ref[:, lanes] = (pooled * 0.125).astype(BF16)
    core = core_ref[0]
    own = grads[1:3, 16:272, :].reshape(512, 256)
    for tap in range(9):
        shift_x, shift_y = tap // 3, tap % 3
        view = window[1 + shift_x : 3 + shift_x, 16 * shift_y : 16 * shift_y + 256, :].reshape(512, 384)
        terms = (tn_dot(view, own) * 0.25).astype(BF16)
        keep_ref[tap] = jnp.where(core == 0, terms[:, :128], terms[:, 128:])
        send_ref[tap] = jnp.where(core == 0, terms[:, 128:], terms[:, :128])
    for layer in range(2):
        total = None
        for tap in range(9):
            shift_x, shift_y = tap // 3, tap % 3
            view = grads[layer + 2 - shift_x, 32 - 16 * shift_y : 288 - 16 * shift_y, :]
            term = nt_dot(view, weight_ref[tap])
            total = term if total is None else total + term
        result = next_rows(total[:, 0:128], 16) + total[:, 128:256] + previous_rows(total[:, 256:384], 16)
        grad_ref[layer] = result.astype(BF16)


def block_b(core, left, cells, right, weight, cot):
    return pl.pallas_call(
        block_b_kernel,
        in_specs=[SCALAR] + [WHOLE] * 5,
        out_shape=(
            jax.ShapeDtypeStruct((64, 256), BF16),
            jax.ShapeDtypeStruct((9, 384, 128), BF16),
            jax.ShapeDtypeStruct((9, 384, 128), BF16),
            jax.ShapeDtypeStruct((2, 256, 128), BF16),
        ),
        scratch_shapes=[
            pltpu.VMEM((6, 288, 384), BF16),
            pltpu.VMEM((4, 288, 256), BF16),
            pltpu.VMEM((2, 128, 128), F32),
        ],
        compiler_params=pltpu.CompilerParams(vmem_limit_bytes=ROOM),
        cost_estimate=pl.CostEstimate(flops=4 * 2 * 512 * 3456 * 256, bytes_accessed=5 * 10**6, transcendentals=5 * 10**5),
    )(core, left, cells, right, weight, cot)


def kernel_a_kernel(core_ref, grad_ref, slope_ref, window_ref, pre_ref, keep_ref, send_ref):
    core = core_ref[0]
    edge = jnp.zeros((16, 256), BF16)
    for layer in range(4):
        spread = grad_ref[layer // 2].astype(F32).reshape(16, 1, 16, 128) * 0.125
        spread = jnp.broadcast_to(spread, (16, 2, 16, 128)).reshape(512, 128)
        slope = slope_ref[layer].astype(F32)
        pre_ref[layer, 0:16, :] = edge
        pre_ref[layer, 528:544, :] = edge
        pre_ref[layer, 16:528, 0:128] = (spread * slope[:, 0:128]).astype(BF16)
        pre_ref[layer, 16:528, 128:256] = (spread * slope[:, 128:256]).astype(BF16)
    grads = pre_ref[:, 16:528, :].reshape(2048, 256)
    for tap in range(9):
        shift_x, shift_y = tap // 3, tap % 3
        view = window_ref[shift_x : shift_x + 4, 16 * shift_y : 16 * shift_y + 512, :].reshape(2048, 256)
        terms = tn_dot(view, grads) * 0.25
        even, odd = terms[:, :128], terms[:, 128:]
        first = jnp.concatenate([even[192:256] + odd[0:64], even[0:32] + odd[64:96]]).astype(BF16)
        second = (even[32:128] + odd[96:192]).astype(BF16)
        keep_ref[tap] = jnp.where(core == 0, first, second)
        send_ref[tap] = jnp.where(core == 0, second, first)


def kernel_a(core, grad, slope, window):
    return pl.pallas_call(
        kernel_a_kernel,
        in_specs=[SCALAR] + [WHOLE] * 3,
        out_shape=(
            jax.ShapeDtypeStruct((4, 544, 256), BF16),
            jax.ShapeDtypeStruct((9, 96, 128), BF16),
            jax.ShapeDtypeStruct((9, 96, 128), BF16),
        ),
        compiler_params=pltpu.CompilerParams(vmem_limit_bytes=ROOM),
        cost_estimate=pl.CostEstimate(flops=2 * 2048 * 2304 * 256, bytes_accessed=6 * 10**6, transcendentals=0),
    )(core, grad, slope, window)


def back_a_kernel(grads_ref, weight_ref, inner_ref, to_left_ref, to_right_ref):
    for layer in range(-1, 5):
        total = None
        for tap in range(9):
            shift_x, shift_y = tap // 3, tap % 3
            source = layer + 1 - shift_x
            if 0 <= source < 4:
                view = grads_ref[source, 32 - 16 * shift_y : 544 - 16 * shift_y, :]
                term = nt_dot(view, weight_ref[tap])
                total = term if total is None else total + term
        outer = total[:, 128:256]
        outer = jnp.where(low_lanes(outer.shape), previous_rows(outer, 16), next_rows(outer, 16))
        result = (total[:, 0:128] + outer).astype(BF16)
        if layer == -1:
            to_left_ref[...] = result
        elif layer == 4:
            to_right_ref[...] = result
        else:
            inner_ref[layer] = result


def back_a(grads, weight):
    return pl.pallas_call(
        back_a_kernel,
        out_shape=(
            jax.ShapeDtypeStruct((4, 512, 128), BF16),
            jax.ShapeDtypeStruct((512, 128), BF16),
            jax.ShapeDtypeStruct((512, 128), BF16),
        ),
        compiler_params=pltpu.CompilerParams(vmem_limit_bytes=ROOM),
        cost_estimate=pl.CostEstimate(flops=2 * 2048 * 2304 * 256, bytes_accessed=4 * 10**6, transcendentals=0),
    )(grads, weight)


def paired_weight(weight):
    taps = weight.reshape(9, 3, 64, 128)
    none = jnp.zeros((9, 64, 128), weight.dtype)
    even = jnp.concatenate([taps[:, 1], taps[:, 2], none, taps[:, 0]], axis=1)
    odd = jnp.concatenate([taps[:, 0], taps[:, 1], taps[:, 2], none], axis=1)
    return jnp.concatenate([even, odd], axis=2)


def merge_kernel(keep_a_ref, other_a_ref, keep_b_ref, other_b_ref, rows_ref):
    for tap in range(9):
        rows = keep_a_ref[tap].astype(F32) + other_a_ref[tap].astype(F32)
        rows_ref[96 * tap : 96 * tap + 96] = rows.astype(BF16)
        rows = keep_b_ref[tap].astype(F32) + other_b_ref[tap].astype(F32)
        rows_ref[864 + 384 * tap : 1248 + 384 * tap] = rows.astype(BF16)
    rows_ref[4320:4352] = jnp.zeros((32, 128), BF16)


def merge(keep_a, other_a, keep_b, other_b):
    return pl.pallas_call(
        merge_kernel,
        out_shape=jax.ShapeDtypeStruct((4352, 128), BF16),
        compiler_params=pltpu.CompilerParams(vmem_limit_bytes=ROOM),
        cost_estimate=pl.CostEstimate(flops=0, bytes_accessed=4 * 10**6, transcendentals=0),
    )(keep_a, other_a, keep_b, other_b)


def unpack_kernel(core_ref, mine_ref, away_ref, sum_a_ref, sum_b_ref):
    core = core_ref[0]
    for tap in range(9):
        rows = slice(96 * tap, 96 * tap + 96)
        mine, away = mine_ref[rows].astype(F32), away_ref[rows].astype(F32)
        sum_a_ref[tap, 0] = jnp.where(core == 0, mine, away)
        sum_a_ref[tap, 1] = jnp.where(core == 0, away, mine)
        rows = slice(864 + 384 * tap, 1248 + 384 * tap)
        mine, away = mine_ref[rows].astype(F32), away_ref[rows].astype(F32)
        sum_b_ref[tap, :, 0:128] = jnp.where(core == 0, mine, away)
        sum_b_ref[tap, :, 128:256] = jnp.where(core == 0, away, mine)


def unpack(core, mine, away):
    return pl.pallas_call(
        unpack_kernel,
        in_specs=[SCALAR] + [WHOLE] * 2,
        out_shape=(
            jax.ShapeDtypeStruct((9, 2, 96, 128), F32),
            jax.ShapeDtypeStruct((9, 384, 256), F32),
        ),
        compiler_params=pltpu.CompilerParams(vmem_limit_bytes=ROOM),
        cost_estimate=pl.CostEstimate(flops=0, bytes_accessed=7 * 10**6, transcendentals=0),
    )(core, mine, away)


AXES = ("slab", "rep")
ACROSS = [[((16 * x + 4 * y + z) * 4 + rep) for x in range(4) for y in range(4)] for z in range(4) for rep in range(4)]
ALONG = [[((4 * plane + z) * 4 + 2 * far + core) for far in range(2) for z in range(4)] for plane in range(16) for core in range(2)]
CORES = [(device, device ^ 1) for device in range(256)]


def other_core(value):
    return lax.ppermute(value, AXES, CORES)


def exchange(blocks, groups):
    return lax.all_to_all(blocks, AXES, 0, 0, axis_index_groups=groups, tiled=True)


def total_of(blocks):
    return jnp.sum(blocks.astype(F32), axis=0).astype(BF16)


def reduce_over_chips(blocks):
    part = total_of(blocks)
    part = total_of(exchange(jnp.broadcast_to(part, (8, 272, 128)), ALONG))
    return exchange(jnp.broadcast_to(part, (16, 272, 128)), ACROSS).reshape(4352, 128)


def neighbours(to_left, to_right):
    count = lax.axis_size("slab")
    up = [(i, i + 1) for i in range(count - 1)]
    down = [(i + 1, i) for i in range(count - 1)]
    return lax.ppermute(to_right, "slab", up), lax.ppermute(to_left, "slab", down)


def shards(cubes, weight_a, weight_b, cotangent):
    core = (lax.axis_index("rep") % 2).reshape(1)
    pair_weight = paired_weight(weight_a)
    taps_b = weight_b.reshape(9, 384, 256)
    cells = cubes.reshape(4, 512, 128)
    cot = cotangent.reshape(64, 256)
    cot_rows = [cot[:, :128], cot[:, 128:]]
    left, right = neighbours(jnp.concatenate([cells[0]] + cot_rows), jnp.concatenate([cells[3]] + cot_rows))
    window, slope_a, pooled = forward_a(left[:512], cells, right[:512], pair_weight)
    pooled_left, pooled_right = neighbours(pooled, pooled)
    cots = [jnp.concatenate([side[512:576], side[576:640]], axis=1) for side in (left, right)]
    cots = jnp.stack([cots[0], cot, cots[1]])
    cots = jnp.broadcast_to(cots[:, :, None, :], (3, 64, 2, 256)).reshape(3, 128, 256)
    features, keep_b, send_b, grad_pooled = block_b(core, pooled_left, pooled, pooled_right, taps_b, cots)
    other_b = other_core(send_b)
    grad_pre, keep_a, send_a = kernel_a(core, grad_pooled, slope_a, window)
    other_a = other_core(send_a)
    inner, to_left, to_right = back_a(grad_pre, pair_weight)
    from_left, from_right = neighbours(to_left, to_right)
    rows = merge(keep_a, other_a, keep_b, other_b)
    blocks = exchange(rows.reshape(16, 272, 128), ACROSS)
    blocks, from_left, from_right = lax.optimization_barrier((blocks, from_left, from_right))
    mine = reduce_over_chips(blocks)
    away = other_core(mine)
    first = (inner[:1].astype(F32) + from_left.astype(F32)).astype(BF16)
    last = (inner[3:].astype(F32) + from_right.astype(F32)).astype(BF16)
    grad_cubes = jnp.concatenate([first, inner[1:3], last])
    sum_a, sum_b = unpack(core, mine, away)
    return (
        features.reshape(1, 1, 8, 8, 256),
        grad_cubes.reshape(1, 4, 32, 32, 64),
        sum_a.reshape(3, 3, 3, 64, 128),
        sum_b.reshape(3, 3, 3, 128, 256),
    )


def solution(mesh):
    return jax.shard_map(
        shards,
        mesh=mesh,
        in_specs=(P("rep", "slab", None, None, None), P(), P(), P("rep", "slab", None, None, None)),
        out_specs=(
            P("rep", "slab", None, None, None),
            P("rep", "slab", None, None, None),
            P(),
            P(),
        ),
        check_vma=False,
    )
```

```python
import jax
import jax.numpy as jnp
from jax import lax
from jax.experimental import pallas as pl
from jax.experimental.pallas import tpu as pltpu
from jax.sharding import PartitionSpec as P

BF16 = jnp.bfloat16
F32 = jnp.float32
ROOM = 16 * 1024 * 1024
SCALAR = pl.BlockSpec(memory_space=pltpu.SMEM)
WHOLE = pl.BlockSpec(memory_space=pltpu.VMEM)


def nt_dot(lhs, rhs):
    return lax.dot_general(lhs, rhs, (((1,), (1,)), ((), ())), preferred_element_type=F32)


def nn_dot(lhs, rhs):
    return jnp.dot(lhs, rhs, preferred_element_type=F32)


def tn_dot(lhs, rhs):
    return lax.dot_general(lhs, rhs, (((0,), (0,)), ((), ())), preferred_element_type=F32)


def next_rows(value, period):
    rows = value.shape[0]
    row = lax.broadcasted_iota(jnp.int32, value.shape, 0) % period
    return jnp.where(row == period - 1, 0.0, pltpu.roll(value, rows - 1, 0))


def previous_rows(value, period):
    row = lax.broadcasted_iota(jnp.int32, value.shape, 0) % period
    return jnp.where(row == 0, 0.0, pltpu.roll(value, 1, 0))


def low_lanes(shape):
    return lax.broadcasted_iota(jnp.int32, shape, 1) < 64


def forward_a_kernel(left_ref, cells_ref, right_ref, weight_ref, window_ref, slope_ref, pooled_ref):
    edge = jnp.zeros((16, 256), BF16)
    for layer in range(6):
        if layer == 0:
            pairs = left_ref[...]
        elif layer == 5:
            pairs = right_ref[...]
        else:
            pairs = cells_ref[layer - 1]
        wide = pairs.astype(F32)
        outer = jnp.where(low_lanes(wide.shape), next_rows(wide, 16), previous_rows(wide, 16))
        window_ref[layer, 0:16, :] = edge
        window_ref[layer, 528:544, :] = edge
        window_ref[layer, 16:528, 0:128] = pairs
        window_ref[layer, 16:528, 128:256] = outer.astype(BF16)
    for half in range(2):
        total = None
        for tap in range(9):
            shift_x, shift_y = tap // 3, tap % 3
            first = 2 * half + shift_x
            window = window_ref[first : first + 2, 16 * shift_y : 16 * shift_y + 512, :]
            term = nn_dot(window.reshape(1024, 256), weight_ref[tap])
            total = term if total is None else total + term
        sigma = 1.0 / (1.0 + jnp.exp(-total))
        active = total * sigma
        slope = sigma * (1.0 + total * (1.0 - sigma))
        slope_ref[2 * half : 2 * half + 2] = slope.astype(BF16).reshape(2, 512, 256)
        blocks = active.reshape(2, 16, 2, 16, 256)
        blocks = (blocks[0] + blocks[1])
        blocks = blocks[:, 0] + blocks[:, 1]
        pooled = (blocks[:, :, :128] + blocks[:, :, 128:]) * 0.125
        pooled_ref[half] = pooled.astype(BF16).reshape(256, 128)


def forward_a(left, cells, right, weight):
    return pl.pallas_call(
        forward_a_kernel,
        out_shape=(
            jax.ShapeDtypeStruct((6, 544, 256), BF16),
            jax.ShapeDtypeStruct((4, 512, 256), BF16),
            jax.ShapeDtypeStruct((2, 256, 128), BF16),
        ),
        compiler_params=pltpu.CompilerParams(vmem_limit_bytes=ROOM),
        cost_estimate=pl.CostEstimate(flops=2 * 2048 * 2304 * 256, bytes_accessed=6 * 10**6, transcendentals=10**6),
    )(left, cells, right, weight)


def block_b_kernel(core_ref, left_ref, cells_ref, right_ref, weight_ref, cot_ref, features_ref, keep_ref, send_ref, grad_ref, window, grads, column):
    edge = jnp.zeros((16, 384), BF16)
    for layer in range(6):
        if layer < 2:
            cells = left_ref[layer]
        elif layer < 4:
            cells = cells_ref[layer - 2]
        else:
            cells = right_ref[layer - 4]
        wide = cells.astype(F32)
        window[layer, 0:16, :] = edge
        window[layer, 272:288, :] = edge
        window[layer, 16:272, 0:128] = previous_rows(wide, 16).astype(BF16)
        window[layer, 16:272, 128:256] = cells
        window[layer, 16:272, 256:384] = next_rows(wide, 16).astype(BF16)
    active = None
    for layer in range(4):
        total = None
        for tap in range(9):
            shift_x, shift_y = tap // 3, tap % 3
            view = window[layer + shift_x, 16 * shift_y : 16 * shift_y + 256, :]
            term = nn_dot(view, weight_ref[tap])
            total = term if total is None else total + term
        sigma = 1.0 / (1.0 + jnp.exp(-total))
        slope = sigma * (1.0 + total * (1.0 - sigma))
        spread = cot_ref[(layer + 1) // 2].astype(F32).reshape(8, 1, 16, 256) * 0.125
        spread = jnp.broadcast_to(spread, (8, 2, 16, 256)).reshape(256, 256)
        grads[layer, 0:16, :] = edge[:, :256]
        grads[layer, 272:288, :] = edge[:, :256]
        grads[layer, 16:272, :] = (spread * slope).astype(BF16)
        if layer in (1, 2):
            blocks = (total * sigma).reshape(8, 2, 16, 256)
            blocks = blocks[:, 0] + blocks[:, 1]
            active = blocks if active is None else active + blocks
    active = active.reshape(128, 256)
    for part in range(2):
        lanes = slice(128 * part, 128 * part + 128)
        column[part] = active[:, lanes]
        pooled = column[part, pl.ds(0, 64, stride=2), :] + column[part, pl.ds(1, 64, stride=2), :]
        features_ref[:, lanes] = (pooled * 0.125).astype(BF16)
    core = core_ref[0]
    own = grads[1:3, 16:272, :].reshape(512, 256)
    for tap in range(9):
        shift_x, shift_y = tap // 3, tap % 3
        view = window[1 + shift_x : 3 + shift_x, 16 * shift_y : 16 * shift_y + 256, :].reshape(512, 384)
        terms = (tn_dot(view, own) * 0.25).astype(BF16)
        keep_ref[tap] = jnp.where(core == 0, terms[:, :128], terms[:, 128:])
        send_ref[tap] = jnp.where(core == 0, terms[:, 128:], terms[:, :128])
    for layer in range(2):
        total = None
        for tap in range(9):
            shift_x, shift_y = tap // 3, tap % 3
            view = grads[layer + 2 - shift_x, 32 - 16 * shift_y : 288 - 16 * shift_y, :]
            term = nt_dot(view, weight_ref[tap])
            total = term if total is None else total + term
        result = next_rows(total[:, 0:128], 16) + total[:, 128:256] + previous_rows(total[:, 256:384], 16)
        grad_ref[layer] = result.astype(BF16)


def block_b(core, left, cells, right, weight, cot):
    return pl.pallas_call(
        block_b_kernel,
        in_specs=[SCALAR] + [WHOLE] * 5,
        out_shape=(
            jax.ShapeDtypeStruct((64, 256), BF16),
            jax.ShapeDtypeStruct((9, 384, 128), BF16),
            jax.ShapeDtypeStruct((9, 384, 128), BF16),
            jax.ShapeDtypeStruct((2, 256, 128), BF16),
        ),
        scratch_shapes=[
            pltpu.VMEM((6, 288, 384), BF16),
            pltpu.VMEM((4, 288, 256), BF16),
            pltpu.VMEM((2, 128, 128), F32),
        ],
        compiler_params=pltpu.CompilerParams(vmem_limit_bytes=ROOM),
        cost_estimate=pl.CostEstimate(flops=4 * 2 * 512 * 3456 * 256, bytes_accessed=5 * 10**6, transcendentals=5 * 10**5),
    )(core, left, cells, right, weight, cot)


def kernel_a_kernel(core_ref, grad_ref, slope_ref, window_ref, pre_ref, keep_ref, send_ref):
    core = core_ref[0]
    edge = jnp.zeros((16, 256), BF16)
    for layer in range(4):
        spread = grad_ref[layer // 2].astype(F32).reshape(16, 1, 16, 128) * 0.125
        spread = jnp.broadcast_to(spread, (16, 2, 16, 128)).reshape(512, 128)
        slope = slope_ref[layer].astype(F32)
        pre_ref[layer, 0:16, :] = edge
        pre_ref[layer, 528:544, :] = edge
        pre_ref[layer, 16:528, 0:128] = (spread * slope[:, 0:128]).astype(BF16)
        pre_ref[layer, 16:528, 128:256] = (spread * slope[:, 128:256]).astype(BF16)
    grads = pre_ref[:, 16:528, :].reshape(2048, 256)
    for tap in range(9):
        shift_x, shift_y = tap // 3, tap % 3
        view = window_ref[shift_x : shift_x + 4, 16 * shift_y : 16 * shift_y + 512, :].reshape(2048, 256)
        terms = tn_dot(view, grads) * 0.25
        even, odd = terms[:, :128], terms[:, 128:]
        first = jnp.concatenate([even[192:256] + odd[0:64], even[0:32] + odd[64:96]]).astype(BF16)
        second = (even[32:128] + odd[96:192]).astype(BF16)
        keep_ref[tap] = jnp.where(core == 0, first, second)
        send_ref[tap] = jnp.where(core == 0, second, first)


def kernel_a(core, grad, slope, window):
    return pl.pallas_call(
        kernel_a_kernel,
        in_specs=[SCALAR] + [WHOLE] * 3,
        out_shape=(
            jax.ShapeDtypeStruct((4, 544, 256), BF16),
            jax.ShapeDtypeStruct((9, 96, 128), BF16),
            jax.ShapeDtypeStruct((9, 96, 128), BF16),
        ),
        compiler_params=pltpu.CompilerParams(vmem_limit_bytes=ROOM),
        cost_estimate=pl.CostEstimate(flops=2 * 2048 * 2304 * 256, bytes_accessed=6 * 10**6, transcendentals=0),
    )(core, grad, slope, window)


def back_a_kernel(grads_ref, weight_ref, inner_ref, to_left_ref, to_right_ref):
    for layer in range(-1, 5):
        total = None
        for tap in range(9):
            shift_x, shift_y = tap // 3, tap % 3
            source = layer + 1 - shift_x
            if 0 <= source < 4:
                view = grads_ref[source, 32 - 16 * shift_y : 544 - 16 * shift_y, :]
                term = nt_dot(view, weight_ref[tap])
                total = term if total is None else total + term
        outer = total[:, 128:256]
        outer = jnp.where(low_lanes(outer.shape), previous_rows(outer, 16), next_rows(outer, 16))
        result = (total[:, 0:128] + outer).astype(BF16)
        if layer == -1:
            to_left_ref[...] = result
        elif layer == 4:
            to_right_ref[...] = result
        else:
            inner_ref[layer] = result


def back_a(grads, weight):
    return pl.pallas_call(
        back_a_kernel,
        out_shape=(
            jax.ShapeDtypeStruct((4, 512, 128), BF16),
            jax.ShapeDtypeStruct((512, 128), BF16),
            jax.ShapeDtypeStruct((512, 128), BF16),
        ),
        compiler_params=pltpu.CompilerParams(vmem_limit_bytes=ROOM),
        cost_estimate=pl.CostEstimate(flops=2 * 2048 * 2304 * 256, bytes_accessed=4 * 10**6, transcendentals=0),
    )(grads, weight)


def paired_weight(weight):
    taps = weight.reshape(9, 3, 64, 128)
    none = jnp.zeros((9, 64, 128), weight.dtype)
    even = jnp.concatenate([taps[:, 1], taps[:, 2], none, taps[:, 0]], axis=1)
    odd = jnp.concatenate([taps[:, 0], taps[:, 1], taps[:, 2], none], axis=1)
    return jnp.concatenate([even, odd], axis=2)


def merge_kernel(keep_a_ref, other_a_ref, keep_b_ref, other_b_ref, rows_ref):
    for tap in range(9):
        rows = keep_a_ref[tap].astype(F32) + other_a_ref[tap].astype(F32)
        rows_ref[96 * tap : 96 * tap + 96] = rows.astype(BF16)
        rows = keep_b_ref[tap].astype(F32) + other_b_ref[tap].astype(F32)
        rows_ref[864 + 384 * tap : 1248 + 384 * tap] = rows.astype(BF16)
    rows_ref[4320:4352] = jnp.zeros((32, 128), BF16)


def merge(keep_a, other_a, keep_b, other_b):
    return pl.pallas_call(
        merge_kernel,
        out_shape=jax.ShapeDtypeStruct((4352, 128), BF16),
        compiler_params=pltpu.CompilerParams(vmem_limit_bytes=ROOM),
        cost_estimate=pl.CostEstimate(flops=0, bytes_accessed=4 * 10**6, transcendentals=0),
    )(keep_a, other_a, keep_b, other_b)


def unpack_kernel(core_ref, mine_ref, away_ref, sum_a_ref, sum_b_ref):
    core, tap = core_ref[0], pl.program_id(0)
    rows = pl.ds(pl.multiple_of(96 * tap, 32), 96)
    mine, away = mine_ref[rows].astype(F32), away_ref[rows].astype(F32)
    sum_a_ref[0, 0] = jnp.where(core == 0, mine, away)
    sum_a_ref[0, 1] = jnp.where(core == 0, away, mine)
    rows = pl.ds(pl.multiple_of(864 + 384 * tap, 32), 384)
    mine, away = mine_ref[rows].astype(F32), away_ref[rows].astype(F32)
    sum_b_ref[0, :, 0:128] = jnp.where(core == 0, mine, away)
    sum_b_ref[0, :, 128:256] = jnp.where(core == 0, away, mine)


def unpack(core, mine, away):
    return pl.pallas_call(
        unpack_kernel,
        grid=(9,),
        in_specs=[SCALAR, WHOLE, WHOLE],
        out_specs=(
            pl.BlockSpec((1, 2, 96, 128), lambda tap: (tap, 0, 0, 0)),
            pl.BlockSpec((1, 384, 256), lambda tap: (tap, 0, 0)),
        ),
        out_shape=(
            jax.ShapeDtypeStruct((9, 2, 96, 128), F32),
            jax.ShapeDtypeStruct((9, 384, 256), F32),
        ),
        compiler_params=pltpu.CompilerParams(vmem_limit_bytes=ROOM),
        cost_estimate=pl.CostEstimate(flops=0, bytes_accessed=7 * 10**6, transcendentals=0),
    )(core, mine, away)


AXES = ("slab", "rep")
ACROSS = [[((16 * x + 4 * y + z) * 4 + rep) for x in range(4) for y in range(4)] for z in range(4) for rep in range(4)]
ALONG = [[((4 * plane + z) * 4 + 2 * far + core) for far in range(2) for z in range(4)] for plane in range(16) for core in range(2)]
CORES = [(device, device ^ 1) for device in range(256)]


def other_core(value):
    return lax.ppermute(value, AXES, CORES)


def exchange(blocks, groups):
    return lax.all_to_all(blocks, AXES, 0, 0, axis_index_groups=groups, tiled=True)


def total_of(blocks):
    return jnp.sum(blocks.astype(F32), axis=0).astype(BF16)


def reduce_over_chips(rows, beside):
    part = total_of(exchange(rows.reshape(16, 272, 128), ACROSS))
    blocks = exchange(jnp.broadcast_to(part, (8, 272, 128)), ALONG)
    blocks, beside = lax.optimization_barrier((blocks, beside))
    part = jnp.broadcast_to(total_of(blocks), (16, 272, 128))
    return exchange(part, ACROSS).reshape(4352, 128), beside


def neighbours(to_left, to_right):
    count = lax.axis_size("slab")
    up = [(i, i + 1) for i in range(count - 1)]
    down = [(i + 1, i) for i in range(count - 1)]
    return lax.ppermute(to_right, "slab", up), lax.ppermute(to_left, "slab", down)


def shards(cubes, weight_a, weight_b, cotangent):
    core = (lax.axis_index("rep") % 2).reshape(1)
    pair_weight = paired_weight(weight_a)
    taps_b = weight_b.reshape(9, 384, 256)
    cells = cubes.reshape(4, 512, 128)
    cot = cotangent.reshape(64, 256)
    cot_rows = [cot[:, :128], cot[:, 128:]]
    left, right = neighbours(jnp.concatenate([cells[0]] + cot_rows), jnp.concatenate([cells[3]] + cot_rows))
    window, slope_a, pooled = forward_a(left[:512], cells, right[:512], pair_weight)
    pooled_left, pooled_right = neighbours(pooled, pooled)
    cots = [jnp.concatenate([side[512:576], side[576:640]], axis=1) for side in (left, right)]
    cots = jnp.stack([cots[0], cot, cots[1]])
    cots = jnp.broadcast_to(cots[:, :, None, :], (3, 64, 2, 256)).reshape(3, 128, 256)
    features, keep_b, send_b, grad_pooled = block_b(core, pooled_left, pooled, pooled_right, taps_b, cots)
    other_b = other_core(send_b)
    grad_pre, keep_a, send_a = kernel_a(core, grad_pooled, slope_a, window)
    other_a = other_core(send_a)
    inner, to_left, to_right = back_a(grad_pre, pair_weight)
    from_left, from_right = neighbours(to_left, to_right)
    rows = merge(keep_a, other_a, keep_b, other_b)
    mine, (from_left, from_right) = reduce_over_chips(rows, (from_left, from_right))
    away = other_core(mine)
    first = (inner[:1].astype(F32) + from_left.astype(F32)).astype(BF16)
    last = (inner[3:].astype(F32) + from_right.astype(F32)).astype(BF16)
    grad_cubes = jnp.concatenate([first, inner[1:3], last])
    sum_a, sum_b = unpack(core, mine, away)
    return (
        features.reshape(1, 1, 8, 8, 256),
        grad_cubes.reshape(1, 4, 32, 32, 64),
        sum_a.reshape(3, 3, 3, 64, 128),
        sum_b.reshape(3, 3, 3, 128, 256),
    )


def solution(mesh):
    return jax.shard_map(
        shards,
        mesh=mesh,
        in_specs=(P("rep", "slab", None, None, None), P(), P(), P("rep", "slab", None, None, None)),
        out_specs=(
            P("rep", "slab", None, None, None),
            P("rep", "slab", None, None, None),
            P(),
            P(),
        ),
        check_vma=False,
    )
```

```python
import jax
import jax.numpy as jnp
from jax import lax
from jax.experimental import pallas as pl
from jax.experimental.pallas import tpu as pltpu
from jax.sharding import PartitionSpec as P

BF16 = jnp.bfloat16
F32 = jnp.float32
LARGE_ROOM = 50 * 1024 * 1024
ROOM = 16 * 1024 * 1024
SCALAR = pl.BlockSpec(memory_space=pltpu.SMEM)
WHOLE = pl.BlockSpec(memory_space=pltpu.VMEM)


def nt_dot(lhs, rhs):
    return lax.dot_general(lhs, rhs, (((1,), (1,)), ((), ())), preferred_element_type=F32)


def nn_dot(lhs, rhs):
    return jnp.dot(lhs, rhs, preferred_element_type=F32)


def tn_dot(lhs, rhs):
    return lax.dot_general(lhs, rhs, (((0,), (0,)), ((), ())), preferred_element_type=F32)


def next_rows(value, period):
    rows = value.shape[0]
    row = lax.broadcasted_iota(jnp.int32, value.shape, 0) % period
    return jnp.where(row == period - 1, 0.0, pltpu.roll(value, rows - 1, 0))


def previous_rows(value, period):
    row = lax.broadcasted_iota(jnp.int32, value.shape, 0) % period
    return jnp.where(row == 0, 0.0, pltpu.roll(value, 1, 0))


def low_lanes(shape):
    return lax.broadcasted_iota(jnp.int32, shape, 1) < 64


def forward_a_kernel(left_ref, cells_ref, right_ref, weight_ref, window_ref, slope_ref, pooled_ref):
    edge = jnp.zeros((16, 256), BF16)
    for layer in range(6):
        if layer == 0:
            pairs = left_ref[...]
        elif layer == 5:
            pairs = right_ref[...]
        else:
            pairs = cells_ref[layer - 1]
        wide = pairs.astype(F32)
        outer = jnp.where(low_lanes(wide.shape), next_rows(wide, 16), previous_rows(wide, 16))
        window_ref[layer, 0:16, :] = edge
        window_ref[layer, 528:544, :] = edge
        window_ref[layer, 16:528, 0:128] = pairs
        window_ref[layer, 16:528, 128:256] = outer.astype(BF16)
    for half in range(2):
        total = None
        for tap in range(9):
            shift_x, shift_y = tap // 3, tap % 3
            first = 2 * half + shift_x
            window = window_ref[first : first + 2, 16 * shift_y : 16 * shift_y + 512, :]
            term = nn_dot(window.reshape(1024, 256), weight_ref[tap])
            total = term if total is None else total + term
        sigma = 1.0 / (1.0 + jnp.exp(-total))
        active = total * sigma
        slope = sigma * (1.0 + total * (1.0 - sigma))
        slope_ref[2 * half : 2 * half + 2] = slope.astype(BF16).reshape(2, 512, 256)
        blocks = active.reshape(2, 16, 2, 16, 256)
        blocks = (blocks[0] + blocks[1])
        blocks = blocks[:, 0] + blocks[:, 1]
        pooled = (blocks[:, :, :128] + blocks[:, :, 128:]) * 0.125
        pooled_ref[half] = pooled.astype(BF16).reshape(256, 128)


def forward_a(left, cells, right, weight):
    return pl.pallas_call(
        forward_a_kernel,
        out_shape=(
            jax.ShapeDtypeStruct((6, 544, 256), BF16),
            jax.ShapeDtypeStruct((4, 512, 256), BF16),
            jax.ShapeDtypeStruct((2, 256, 128), BF16),
        ),
        compiler_params=pltpu.CompilerParams(vmem_limit_bytes=LARGE_ROOM),
        cost_estimate=pl.CostEstimate(flops=2 * 2048 * 2304 * 256, bytes_accessed=6 * 10**6, transcendentals=10**6),
    )(left, cells, right, weight)


def block_b_kernel(core_ref, left_ref, cells_ref, right_ref, weight_ref, cot_ref, features_ref, keep_ref, send_ref, grad_ref, window, grads, column):
    edge = jnp.zeros((16, 384), BF16)
    for layer in range(6):
        if layer < 2:
            cells = left_ref[layer]
        elif layer < 4:
            cells = cells_ref[layer - 2]
        else:
            cells = right_ref[layer - 4]
        wide = cells.astype(F32)
        window[layer, 0:16, :] = edge
        window[layer, 272:288, :] = edge
        window[layer, 16:272, 0:128] = previous_rows(wide, 16).astype(BF16)
        window[layer, 16:272, 128:256] = cells
        window[layer, 16:272, 256:384] = next_rows(wide, 16).astype(BF16)
    active = None
    for layer in range(4):
        total = None
        for tap in range(9):
            shift_x, shift_y = tap // 3, tap % 3
            view = window[layer + shift_x, 16 * shift_y : 16 * shift_y + 256, :]
            term = nn_dot(view, weight_ref[tap])
            total = term if total is None else total + term
        sigma = 1.0 / (1.0 + jnp.exp(-total))
        slope = sigma * (1.0 + total * (1.0 - sigma))
        spread = cot_ref[(layer + 1) // 2].astype(F32).reshape(8, 1, 16, 256) * 0.125
        spread = jnp.broadcast_to(spread, (8, 2, 16, 256)).reshape(256, 256)
        grads[layer, 0:16, :] = edge[:, :256]
        grads[layer, 272:288, :] = edge[:, :256]
        grads[layer, 16:272, :] = (spread * slope).astype(BF16)
        if layer in (1, 2):
            blocks = (total * sigma).reshape(8, 2, 16, 256)
            blocks = blocks[:, 0] + blocks[:, 1]
            active = blocks if active is None else active + blocks
    active = active.reshape(128, 256)
    for part in range(2):
        lanes = slice(128 * part, 128 * part + 128)
        column[part] = active[:, lanes]
        pooled = column[part, pl.ds(0, 64, stride=2), :] + column[part, pl.ds(1, 64, stride=2), :]
        features_ref[:, lanes] = (pooled * 0.125).astype(BF16)
    core = core_ref[0]
    own = grads[1:3, 16:272, :].reshape(512, 256)
    for tap in range(9):
        shift_x, shift_y = tap // 3, tap % 3
        view = window[1 + shift_x : 3 + shift_x, 16 * shift_y : 16 * shift_y + 256, :].reshape(512, 384)
        terms = (tn_dot(view, own) * 0.25).astype(BF16)
        keep_ref[tap] = jnp.where(core == 0, terms[:, :128], terms[:, 128:])
        send_ref[tap] = jnp.where(core == 0, terms[:, 128:], terms[:, :128])
    for layer in range(2):
        total = None
        for tap in range(9):
            shift_x, shift_y = tap // 3, tap % 3
            view = grads[layer + 2 - shift_x, 32 - 16 * shift_y : 288 - 16 * shift_y, :]
            term = nt_dot(view, weight_ref[tap])
            total = term if total is None else total + term
        result = next_rows(total[:, 0:128], 16) + total[:, 128:256] + previous_rows(total[:, 256:384], 16)
        grad_ref[layer] = result.astype(BF16)


def block_b(core, left, cells, right, weight, cot):
    return pl.pallas_call(
        block_b_kernel,
        in_specs=[SCALAR] + [WHOLE] * 5,
        out_shape=(
            jax.ShapeDtypeStruct((64, 256), BF16),
            jax.ShapeDtypeStruct((9, 384, 128), BF16),
            jax.ShapeDtypeStruct((9, 384, 128), BF16),
            jax.ShapeDtypeStruct((2, 256, 128), BF16),
        ),
        scratch_shapes=[
            pltpu.VMEM((6, 288, 384), BF16),
            pltpu.VMEM((4, 288, 256), BF16),
            pltpu.VMEM((2, 128, 128), F32),
        ],
        compiler_params=pltpu.CompilerParams(vmem_limit_bytes=ROOM),
        cost_estimate=pl.CostEstimate(flops=4 * 2 * 512 * 3456 * 256, bytes_accessed=5 * 10**6, transcendentals=5 * 10**5),
    )(core, left, cells, right, weight, cot)


def kernel_a_kernel(core_ref, grad_ref, slope_ref, window_ref, pre_ref, keep_ref, send_ref):
    core = core_ref[0]
    edge = jnp.zeros((16, 256), BF16)
    for layer in range(4):
        spread = grad_ref[layer // 2].astype(F32).reshape(16, 1, 16, 128) * 0.125
        spread = jnp.broadcast_to(spread, (16, 2, 16, 128)).reshape(512, 128)
        slope = slope_ref[layer].astype(F32)
        pre_ref[layer, 0:16, :] = edge
        pre_ref[layer, 528:544, :] = edge
        pre_ref[layer, 16:528, 0:128] = (spread * slope[:, 0:128]).astype(BF16)
        pre_ref[layer, 16:528, 128:256] = (spread * slope[:, 128:256]).astype(BF16)
    grads = pre_ref[:, 16:528, :].reshape(2048, 256)
    for tap in range(9):
        shift_x, shift_y = tap // 3, tap % 3
        view = window_ref[shift_x : shift_x + 4, 16 * shift_y : 16 * shift_y + 512, :].reshape(2048, 256)
        terms = tn_dot(view, grads) * 0.25
        even, odd = terms[:, :128], terms[:, 128:]
        first = jnp.concatenate([even[192:256] + odd[0:64], even[0:32] + odd[64:96]]).astype(BF16)
        second = (even[32:128] + odd[96:192]).astype(BF16)
        keep_ref[tap] = jnp.where(core == 0, first, second)
        send_ref[tap] = jnp.where(core == 0, second, first)


def kernel_a(core, grad, slope, window):
    return pl.pallas_call(
        kernel_a_kernel,
        in_specs=[SCALAR] + [WHOLE] * 3,
        out_shape=(
            jax.ShapeDtypeStruct((4, 544, 256), BF16),
            jax.ShapeDtypeStruct((9, 96, 128), BF16),
            jax.ShapeDtypeStruct((9, 96, 128), BF16),
        ),
        compiler_params=pltpu.CompilerParams(vmem_limit_bytes=ROOM),
        cost_estimate=pl.CostEstimate(flops=2 * 2048 * 2304 * 256, bytes_accessed=6 * 10**6, transcendentals=0),
    )(core, grad, slope, window)


def back_a_kernel(grads_ref, weight_ref, inner_ref, to_left_ref, to_right_ref):
    for layer in range(-1, 5):
        total = None
        for tap in range(9):
            shift_x, shift_y = tap // 3, tap % 3
            source = layer + 1 - shift_x
            if 0 <= source < 4:
                view = grads_ref[source, 32 - 16 * shift_y : 544 - 16 * shift_y, :]
                term = nt_dot(view, weight_ref[tap])
                total = term if total is None else total + term
        outer = total[:, 128:256]
        outer = jnp.where(low_lanes(outer.shape), previous_rows(outer, 16), next_rows(outer, 16))
        result = (total[:, 0:128] + outer).astype(BF16)
        if layer == -1:
            to_left_ref[...] = result
        elif layer == 4:
            to_right_ref[...] = result
        else:
            inner_ref[layer] = result


def back_a(grads, weight):
    return pl.pallas_call(
        back_a_kernel,
        out_shape=(
            jax.ShapeDtypeStruct((4, 512, 128), BF16),
            jax.ShapeDtypeStruct((512, 128), BF16),
            jax.ShapeDtypeStruct((512, 128), BF16),
        ),
        compiler_params=pltpu.CompilerParams(vmem_limit_bytes=ROOM),
        cost_estimate=pl.CostEstimate(flops=2 * 2048 * 2304 * 256, bytes_accessed=4 * 10**6, transcendentals=0),
    )(grads, weight)


def paired_weight(weight):
    taps = weight.reshape(9, 3, 64, 128)
    none = jnp.zeros((9, 64, 128), weight.dtype)
    even = jnp.concatenate([taps[:, 1], taps[:, 2], none, taps[:, 0]], axis=1)
    odd = jnp.concatenate([taps[:, 0], taps[:, 1], taps[:, 2], none], axis=1)
    return jnp.concatenate([even, odd], axis=2)


def merge_kernel(keep_a_ref, other_a_ref, keep_b_ref, other_b_ref, rows_ref):
    for tap in range(9):
        rows = keep_a_ref[tap].astype(F32) + other_a_ref[tap].astype(F32)
        rows_ref[96 * tap : 96 * tap + 96] = rows.astype(BF16)
        rows = keep_b_ref[tap].astype(F32) + other_b_ref[tap].astype(F32)
        rows_ref[864 + 384 * tap : 1248 + 384 * tap] = rows.astype(BF16)
    rows_ref[4320:4352] = jnp.zeros((32, 128), BF16)


def merge(keep_a, other_a, keep_b, other_b):
    return pl.pallas_call(
        merge_kernel,
        out_shape=jax.ShapeDtypeStruct((4352, 128), BF16),
        compiler_params=pltpu.CompilerParams(vmem_limit_bytes=ROOM),
        cost_estimate=pl.CostEstimate(flops=0, bytes_accessed=4 * 10**6, transcendentals=0),
    )(keep_a, other_a, keep_b, other_b)


def unpack_kernel(core_ref, mine_ref, away_ref, sum_a_ref, sum_b_ref):
    core = core_ref[0]
    for tap in range(9):
        rows = slice(96 * tap, 96 * tap + 96)
        mine, away = mine_ref[rows].astype(F32), away_ref[rows].astype(F32)
        sum_a_ref[tap, 0] = jnp.where(core == 0, mine, away)
        sum_a_ref[tap, 1] = jnp.where(core == 0, away, mine)
        rows = slice(864 + 384 * tap, 1248 + 384 * tap)
        mine, away = mine_ref[rows].astype(F32), away_ref[rows].astype(F32)
        sum_b_ref[tap, :, 0:128] = jnp.where(core == 0, mine, away)
        sum_b_ref[tap, :, 128:256] = jnp.where(core == 0, away, mine)


def unpack(core, mine, away):
    return pl.pallas_call(
        unpack_kernel,
        in_specs=[SCALAR] + [WHOLE] * 2,
        out_shape=(
            jax.ShapeDtypeStruct((9, 2, 96, 128), F32),
            jax.ShapeDtypeStruct((9, 384, 256), F32),
        ),
        compiler_params=pltpu.CompilerParams(vmem_limit_bytes=ROOM),
        cost_estimate=pl.CostEstimate(flops=0, bytes_accessed=7 * 10**6, transcendentals=0),
    )(core, mine, away)


AXES = ("slab", "rep")
ACROSS = [[((16 * x + 4 * y + z) * 4 + rep) for x in range(4) for y in range(4)] for z in range(4) for rep in range(4)]
ALONG = [[((4 * plane + z) * 4 + 2 * far + core) for far in range(2) for z in range(4)] for plane in range(16) for core in range(2)]
CORES = [(device, device ^ 1) for device in range(256)]


def other_core(value):
    return lax.ppermute(value, AXES, CORES)


def exchange(blocks, groups):
    return lax.all_to_all(blocks, AXES, 0, 0, axis_index_groups=groups, tiled=True)


def total_of(blocks):
    return jnp.sum(blocks.astype(F32), axis=0).astype(BF16)


def reduce_over_chips(blocks):
    part = total_of(blocks)
    part = total_of(exchange(jnp.broadcast_to(part, (8, 272, 128)), ALONG))
    return exchange(jnp.broadcast_to(part, (16, 272, 128)), ACROSS).reshape(4352, 128)


def neighbours(to_left, to_right):
    count = lax.axis_size("slab")
    up = [(i, i + 1) for i in range(count - 1)]
    down = [(i + 1, i) for i in range(count - 1)]
    return lax.ppermute(to_right, "slab", up), lax.ppermute(to_left, "slab", down)


def shards(cubes, weight_a, weight_b, cotangent):
    core = (lax.axis_index("rep") % 2).reshape(1)
    pair_weight = paired_weight(weight_a)
    taps_b = weight_b.reshape(9, 384, 256)
    cells = cubes.reshape(4, 512, 128)
    cot = cotangent.reshape(64, 256)
    cot_rows = [cot[:, :128], cot[:, 128:]]
    left, right = neighbours(jnp.concatenate([cells[0]] + cot_rows), jnp.concatenate([cells[3]] + cot_rows))
    window, slope_a, pooled = forward_a(left[:512], cells, right[:512], pair_weight)
    pooled_left, pooled_right = neighbours(pooled, pooled)
    cots = [jnp.concatenate([side[512:576], side[576:640]], axis=1) for side in (left, right)]
    cots = jnp.stack([cots[0], cot, cots[1]])
    cots = jnp.broadcast_to(cots[:, :, None, :], (3, 64, 2, 256)).reshape(3, 128, 256)
    features, keep_b, send_b, grad_pooled = block_b(core, pooled_left, pooled, pooled_right, taps_b, cots)
    other_b = other_core(send_b)
    grad_pre, keep_a, send_a = kernel_a(core, grad_pooled, slope_a, window)
    other_a = other_core(send_a)
    inner, to_left, to_right = back_a(grad_pre, pair_weight)
    from_left, from_right = neighbours(to_left, to_right)
    rows = merge(keep_a, other_a, keep_b, other_b)
    blocks = exchange(rows.reshape(16, 272, 128), ACROSS)
    blocks, from_left, from_right = lax.optimization_barrier((blocks, from_left, from_right))
    mine = reduce_over_chips(blocks)
    away = other_core(mine)
    first = (inner[:1].astype(F32) + from_left.astype(F32)).astype(BF16)
    last = (inner[3:].astype(F32) + from_right.astype(F32)).astype(BF16)
    grad_cubes = jnp.concatenate([first, inner[1:3], last])
    sum_a, sum_b = unpack(core, mine, away)
    return (
        features.reshape(1, 1, 8, 8, 256),
        grad_cubes.reshape(1, 4, 32, 32, 64),
        sum_a.reshape(3, 3, 3, 64, 128),
        sum_b.reshape(3, 3, 3, 128, 256),
    )


def solution(mesh):
    return jax.shard_map(
        shards,
        mesh=mesh,
        in_specs=(P("rep", "slab", None, None, None), P(), P(), P("rep", "slab", None, None, None)),
        out_specs=(
            P("rep", "slab", None, None, None),
            P("rep", "slab", None, None, None),
            P(),
            P(),
        ),
        check_vma=False,
    )
```

```python
import jax
import jax.numpy as jnp
from jax import lax
from jax.experimental import pallas as pl
from jax.experimental.pallas import tpu as pltpu
from jax.sharding import PartitionSpec as P

BF16 = jnp.bfloat16
F32 = jnp.float32
ROOM = 50 * 1024 * 1024
SCALAR = pl.BlockSpec(memory_space=pltpu.SMEM)
WHOLE = pl.BlockSpec(memory_space=pltpu.VMEM)
APART = pl.BlockSpec(memory_space=pltpu.HBM)


def nt_dot(lhs, rhs):
    return lax.dot_general(lhs, rhs, (((1,), (1,)), ((), ())), preferred_element_type=F32)


def nn_dot(lhs, rhs):
    return jnp.dot(lhs, rhs, preferred_element_type=F32)


def tn_dot(lhs, rhs):
    return lax.dot_general(lhs, rhs, (((0,), (0,)), ((), ())), preferred_element_type=F32)


def next_rows(value, period):
    rows = value.shape[0]
    row = lax.broadcasted_iota(jnp.int32, value.shape, 0) % period
    return jnp.where(row == period - 1, 0.0, pltpu.roll(value, rows - 1, 0))


def previous_rows(value, period):
    row = lax.broadcasted_iota(jnp.int32, value.shape, 0) % period
    return jnp.where(row == 0, 0.0, pltpu.roll(value, 1, 0))


def low_lanes(shape):
    return lax.broadcasted_iota(jnp.int32, shape, 1) < 64


def pack_pairs(pairs, window_ref, layer):
    edge = jnp.zeros((16, 256), BF16)
    wide = pairs.astype(F32)
    outer = jnp.where(low_lanes(wide.shape), next_rows(wide, 16), previous_rows(wide, 16))
    window_ref[layer, 0:16, :] = edge
    window_ref[layer, 528:544, :] = edge
    window_ref[layer, 16:528, 0:128] = pairs
    window_ref[layer, 16:528, 128:256] = outer.astype(BF16)


def layer_terms(window_ref, source, weight_ref, shift_x, total):
    for shift_y in range(3):
        view = window_ref[source, 16 * shift_y : 16 * shift_y + 512, :]
        term = nn_dot(view, weight_ref[3 * shift_x + shift_y])
        total = term if total is None else total + term
    return total


def slope_and_pool(total):
    sigma = 1.0 / (1.0 + jnp.exp(-total))
    blocks = (total * sigma).reshape(16, 2, 16, 256)
    blocks = blocks[:, 0] + blocks[:, 1]
    slope = sigma * (1.0 + total * (1.0 - sigma))
    return slope.astype(BF16), (blocks[:, :, :128] + blocks[:, :, 128:]).reshape(256, 128)


def forward_inner_kernel(cells_ref, weight_ref, window_ref, partial_ref, slope_ref, pool_ref):
    for layer in range(4):
        pack_pairs(cells_ref[layer], window_ref, layer)
    for layer in range(4):
        total = None
        for shift_x in range(3):
            source = layer + shift_x - 1
            if 0 <= source < 4:
                total = layer_terms(window_ref, source, weight_ref, shift_x, total)
        if layer in (0, 3):
            partial_ref[layer // 3] = total
        else:
            slope_ref[layer - 1], pool_ref[layer - 1] = slope_and_pool(total)


def forward_inner(cells, weight):
    return pl.pallas_call(
        forward_inner_kernel,
        out_shape=(
            jax.ShapeDtypeStruct((4, 544, 256), BF16),
            jax.ShapeDtypeStruct((2, 512, 256), F32),
            jax.ShapeDtypeStruct((2, 512, 256), BF16),
            jax.ShapeDtypeStruct((2, 256, 128), F32),
        ),
        compiler_params=pltpu.CompilerParams(vmem_limit_bytes=ROOM),
        cost_estimate=pl.CostEstimate(flops=2 * 2048 * 2304 * 256, bytes_accessed=6 * 10**6, transcendentals=10**6),
    )(cells, weight)


def forward_outer_kernel(left_ref, right_ref, weight_ref, partial_ref, pool_ref, window_ref, slope_ref, pooled_ref):
    pack_pairs(left_ref[...], window_ref, 0)
    pack_pairs(right_ref[...], window_ref, 1)
    for side in range(2):
        total = layer_terms(window_ref, side, weight_ref, 2 * side, partial_ref[side])
        slope, pool = slope_and_pool(total)
        slope_ref[side] = slope
        pooled_ref[side] = ((pool + pool_ref[side]) * 0.125).astype(BF16)


def forward_outer(left, right, weight, partial, pool):
    return pl.pallas_call(
        forward_outer_kernel,
        out_shape=(
            jax.ShapeDtypeStruct((2, 544, 256), BF16),
            jax.ShapeDtypeStruct((2, 512, 256), BF16),
            jax.ShapeDtypeStruct((2, 256, 128), BF16),
        ),
        compiler_params=pltpu.CompilerParams(vmem_limit_bytes=ROOM),
        cost_estimate=pl.CostEstimate(flops=10**9, bytes_accessed=5 * 10**6, transcendentals=10**6),
    )(left, right, weight, partial, pool)


def block_b_kernel(core_ref, left_ref, cells_ref, right_ref, weight_ref, cot_ref, features_ref, keep_ref, send_ref, grad_ref, window, grads, column):
    edge = jnp.zeros((16, 384), BF16)
    for layer in range(6):
        if layer < 2:
            cells = left_ref[layer]
        elif layer < 4:
            cells = cells_ref[layer - 2]
        else:
            cells = right_ref[layer - 4]
        wide = cells.astype(F32)
        window[layer, 0:16, :] = edge
        window[layer, 272:288, :] = edge
        window[layer, 16:272, 0:128] = previous_rows(wide, 16).astype(BF16)
        window[layer, 16:272, 128:256] = cells
        window[layer, 16:272, 256:384] = next_rows(wide, 16).astype(BF16)
    active = None
    for layer in range(4):
        total = None
        for tap in range(9):
            shift_x, shift_y = tap // 3, tap % 3
            view = window[layer + shift_x, 16 * shift_y : 16 * shift_y + 256, :]
            term = nn_dot(view, weight_ref[tap])
            total = term if total is None else total + term
        sigma = 1.0 / (1.0 + jnp.exp(-total))
        slope = sigma * (1.0 + total * (1.0 - sigma))
        spread = cot_ref[(layer + 1) // 2].astype(F32).reshape(8, 1, 16, 256) * 0.125
        spread = jnp.broadcast_to(spread, (8, 2, 16, 256)).reshape(256, 256)
        grads[layer, 0:16, :] = edge[:, :256]
        grads[layer, 272:288, :] = edge[:, :256]
        grads[layer, 16:272, :] = (spread * slope).astype(BF16)
        if layer in (1, 2):
            blocks = (total * sigma).reshape(8, 2, 16, 256)
            blocks = blocks[:, 0] + blocks[:, 1]
            active = blocks if active is None else active + blocks
    active = active.reshape(128, 256)
    for part in range(2):
        lanes = slice(128 * part, 128 * part + 128)
        column[part] = active[:, lanes]
        pooled = column[part, pl.ds(0, 64, stride=2), :] + column[part, pl.ds(1, 64, stride=2), :]
        features_ref[:, lanes] = (pooled * 0.125).astype(BF16)
    core = core_ref[0]
    own = grads[1:3, 16:272, :].reshape(512, 256)
    for tap in range(9):
        shift_x, shift_y = tap // 3, tap % 3
        view = window[1 + shift_x : 3 + shift_x, 16 * shift_y : 16 * shift_y + 256, :].reshape(512, 384)
        terms = (tn_dot(view, own) * 0.25).astype(BF16)
        keep_ref[tap] = jnp.where(core == 0, terms[:, :128], terms[:, 128:])
        send_ref[tap] = jnp.where(core == 0, terms[:, 128:], terms[:, :128])
    for layer in range(2):
        total = None
        for tap in range(9):
            shift_x, shift_y = tap // 3, tap % 3
            view = grads[layer + 2 - shift_x, 32 - 16 * shift_y : 288 - 16 * shift_y, :]
            term = nt_dot(view, weight_ref[tap])
            total = term if total is None else total + term
        result = next_rows(total[:, 0:128], 16) + total[:, 128:256] + previous_rows(total[:, 256:384], 16)
        grad_ref[layer] = result.astype(BF16)


def block_b(core, left, cells, right, weight, cot):
    return pl.pallas_call(
        block_b_kernel,
        in_specs=[SCALAR] + [WHOLE] * 5,
        out_shape=(
            jax.ShapeDtypeStruct((64, 256), BF16),
            jax.ShapeDtypeStruct((9, 384, 128), BF16),
            jax.ShapeDtypeStruct((9, 384, 128), BF16),
            jax.ShapeDtypeStruct((2, 256, 128), BF16),
        ),
        scratch_shapes=[
            pltpu.VMEM((6, 288, 384), BF16),
            pltpu.VMEM((4, 288, 256), BF16),
            pltpu.VMEM((2, 128, 128), F32),
        ],
        compiler_params=pltpu.CompilerParams(vmem_limit_bytes=ROOM),
        cost_estimate=pl.CostEstimate(flops=4 * 2 * 512 * 3456 * 256, bytes_accessed=5 * 10**6, transcendentals=5 * 10**5),
    )(core, left, cells, right, weight, cot)


def kernel_a_kernel(core_ref, grad_ref, slope_ref, ends_ref, window_ref, sides_ref, pre_out, keep_ref, send_ref, pre_ref, sem):
    core = core_ref[0]
    edge = jnp.zeros((16, 256), BF16)
    for layer in range(4):
        spread = grad_ref[layer // 2].astype(F32).reshape(16, 1, 16, 128) * 0.125
        spread = jnp.broadcast_to(spread, (16, 2, 16, 128)).reshape(512, 128)
        slope = (ends_ref[layer // 3] if layer in (0, 3) else slope_ref[layer - 1]).astype(F32)
        pre_ref[layer, 0:16, :] = edge
        pre_ref[layer, 528:544, :] = edge
        pre_ref[layer, 16:528, 0:128] = (spread * slope[:, 0:128]).astype(BF16)
        pre_ref[layer, 16:528, 128:256] = (spread * slope[:, 128:256]).astype(BF16)
    store = pltpu.make_async_copy(pre_ref, pre_out, sem)
    store.start()
    grads = pre_ref[:, 16:528, :].reshape(2048, 256)
    for tap in range(9):
        shift_x, shift_y = tap // 3, tap % 3
        rows = slice(16 * shift_y, 16 * shift_y + 512)
        if shift_x == 0:
            terms = tn_dot(window_ref[0:3, rows].reshape(1536, 256), grads[512:]) + tn_dot(sides_ref[0, rows], grads[:512])
        elif shift_x == 1:
            terms = tn_dot(window_ref[:, rows].reshape(2048, 256), grads)
        else:
            terms = tn_dot(window_ref[1:4, rows].reshape(1536, 256), grads[:1536]) + tn_dot(sides_ref[1, rows], grads[1536:])
        terms = terms * 0.25
        even, odd = terms[:, :128], terms[:, 128:]
        first = jnp.concatenate([even[192:256] + odd[0:64], even[0:32] + odd[64:96]]).astype(BF16)
        second = (even[32:128] + odd[96:192]).astype(BF16)
        keep_ref[tap] = jnp.where(core == 0, first, second)
        send_ref[tap] = jnp.where(core == 0, second, first)
    store.wait()


def kernel_a(core, grad, slope, ends, window, sides):
    return pl.pallas_call(
        kernel_a_kernel,
        in_specs=[SCALAR] + [WHOLE] * 5,
        out_specs=(APART, WHOLE, WHOLE),
        scratch_shapes=[pltpu.VMEM((4, 544, 256), BF16), pltpu.SemaphoreType.DMA],
        out_shape=(
            jax.ShapeDtypeStruct((4, 544, 256), BF16),
            jax.ShapeDtypeStruct((9, 96, 128), BF16),
            jax.ShapeDtypeStruct((9, 96, 128), BF16),
        ),
        compiler_params=pltpu.CompilerParams(vmem_limit_bytes=ROOM),
        cost_estimate=pl.CostEstimate(flops=2 * 2048 * 2304 * 256, bytes_accessed=6 * 10**6, transcendentals=0),
    )(core, grad, slope, ends, window, sides)


def back_a_kernel(grads_ref, weight_ref, inner_ref, to_left_ref, to_right_ref):
    for layer in range(-1, 5):
        total = None
        for tap in range(9):
            shift_x, shift_y = tap // 3, tap % 3
            source = layer + 1 - shift_x
            if 0 <= source < 4:
                view = grads_ref[source, 32 - 16 * shift_y : 544 - 16 * shift_y, :]
                term = nt_dot(view, weight_ref[tap])
                total = term if total is None else total + term
        outer = total[:, 128:256]
        outer = jnp.where(low_lanes(outer.shape), previous_rows(outer, 16), next_rows(outer, 16))
        result = (total[:, 0:128] + outer).astype(BF16)
        if layer == -1:
            to_left_ref[...] = result
        elif layer == 4:
            to_right_ref[...] = result
        else:
            inner_ref[layer] = result


def back_a(grads, weight):
    return pl.pallas_call(
        back_a_kernel,
        out_shape=(
            jax.ShapeDtypeStruct((4, 512, 128), BF16),
            jax.ShapeDtypeStruct((512, 128), BF16),
            jax.ShapeDtypeStruct((512, 128), BF16),
        ),
        compiler_params=pltpu.CompilerParams(vmem_limit_bytes=ROOM),
        cost_estimate=pl.CostEstimate(flops=2 * 2048 * 2304 * 256, bytes_accessed=4 * 10**6, transcendentals=0),
    )(grads, weight)


def paired_weight(weight):
    taps = weight.reshape(9, 3, 64, 128)
    none = jnp.zeros((9, 64, 128), weight.dtype)
    even = jnp.concatenate([taps[:, 1], taps[:, 2], none, taps[:, 0]], axis=1)
    odd = jnp.concatenate([taps[:, 0], taps[:, 1], taps[:, 2], none], axis=1)
    return jnp.concatenate([even, odd], axis=2)


def merge_kernel(keep_a_ref, other_a_ref, keep_b_ref, other_b_ref, rows_ref):
    for tap in range(9):
        rows = keep_a_ref[tap].astype(F32) + other_a_ref[tap].astype(F32)
        rows_ref[96 * tap : 96 * tap + 96] = rows.astype(BF16)
        rows = keep_b_ref[tap].astype(F32) + other_b_ref[tap].astype(F32)
        rows_ref[864 + 384 * tap : 1248 + 384 * tap] = rows.astype(BF16)
    rows_ref[4320:4352] = jnp.zeros((32, 128), BF16)


def merge(keep_a, other_a, keep_b, other_b):
    return pl.pallas_call(
        merge_kernel,
        out_shape=jax.ShapeDtypeStruct((4352, 128), BF16),
        compiler_params=pltpu.CompilerParams(vmem_limit_bytes=ROOM),
        cost_estimate=pl.CostEstimate(flops=0, bytes_accessed=4 * 10**6, transcendentals=0),
    )(keep_a, other_a, keep_b, other_b)


def unpack_kernel(core_ref, mine_ref, away_ref, sum_a_ref, sum_b_ref):
    core = core_ref[0]
    for tap in range(9):
        rows = slice(96 * tap, 96 * tap + 96)
        mine, away = mine_ref[rows].astype(F32), away_ref[rows].astype(F32)
        sum_a_ref[tap, 0] = jnp.where(core == 0, mine, away)
        sum_a_ref[tap, 1] = jnp.where(core == 0, away, mine)
        rows = slice(864 + 384 * tap, 1248 + 384 * tap)
        mine, away = mine_ref[rows].astype(F32), away_ref[rows].astype(F32)
        sum_b_ref[tap, :, 0:128] = jnp.where(core == 0, mine, away)
        sum_b_ref[tap, :, 128:256] = jnp.where(core == 0, away, mine)


def unpack(core, mine, away):
    return pl.pallas_call(
        unpack_kernel,
        in_specs=[SCALAR] + [WHOLE] * 2,
        out_shape=(
            jax.ShapeDtypeStruct((9, 2, 96, 128), F32),
            jax.ShapeDtypeStruct((9, 384, 256), F32),
        ),
        compiler_params=pltpu.CompilerParams(vmem_limit_bytes=ROOM),
        cost_estimate=pl.CostEstimate(flops=0, bytes_accessed=7 * 10**6, transcendentals=0),
    )(core, mine, away)


AXES = ("slab", "rep")
ACROSS = [[((16 * x + 4 * y + z) * 4 + rep) for x in range(4) for y in range(4)] for z in range(4) for rep in range(4)]
ALONG = [[((4 * plane + z) * 4 + 2 * far + core) for far in range(2) for z in range(4)] for plane in range(16) for core in range(2)]
CORES = [(device, device ^ 1) for device in range(256)]


def other_core(value):
    return lax.ppermute(value, AXES, CORES)


def exchange(blocks, groups):
    return lax.all_to_all(blocks, AXES, 0, 0, axis_index_groups=groups, tiled=True)


def total_of(blocks):
    return jnp.sum(blocks.astype(F32), axis=0).astype(BF16)


def reduce_over_chips(blocks):
    part = total_of(blocks)
    part = total_of(exchange(jnp.broadcast_to(part, (8, 272, 128)), ALONG))
    return exchange(jnp.broadcast_to(part, (16, 272, 128)), ACROSS).reshape(4352, 128)


def neighbours(to_left, to_right):
    count = lax.axis_size("slab")
    up = [(i, i + 1) for i in range(count - 1)]
    down = [(i + 1, i) for i in range(count - 1)]
    return lax.ppermute(to_right, "slab", up), lax.ppermute(to_left, "slab", down)


def shards(cubes, weight_a, weight_b, cotangent):
    core = (lax.axis_index("rep") % 2).reshape(1)
    pair_weight = paired_weight(weight_a)
    taps_b = weight_b.reshape(9, 384, 256)
    cells = cubes.reshape(4, 512, 128)
    cot = cotangent.reshape(64, 256)
    cot_rows = [cot[:, :128], cot[:, 128:]]
    left, right = neighbours(jnp.concatenate([cells[0]] + cot_rows), jnp.concatenate([cells[3]] + cot_rows))
    window, partial, slope_a, pool = forward_inner(cells, pair_weight)
    sides, ends, pooled = forward_outer(left[:512], right[:512], pair_weight, partial, pool)
    pooled_left, pooled_right = neighbours(pooled, pooled)
    cots = [jnp.concatenate([side[512:576], side[576:640]], axis=1) for side in (left, right)]
    cots = jnp.stack([cots[0], cot, cots[1]])
    cots = jnp.broadcast_to(cots[:, :, None, :], (3, 64, 2, 256)).reshape(3, 128, 256)
    features, keep_b, send_b, grad_pooled = block_b(core, pooled_left, pooled, pooled_right, taps_b, cots)
    other_b = other_core(send_b)
    grad_pre, keep_a, send_a = kernel_a(core, grad_pooled, slope_a, ends, window, sides)
    other_a = other_core(send_a)
    inner, to_left, to_right = back_a(grad_pre, pair_weight)
    from_left, from_right = neighbours(to_left, to_right)
    rows = merge(keep_a, other_a, keep_b, other_b)
    blocks = exchange(rows.reshape(16, 272, 128), ACROSS)
    blocks, from_left, from_right = lax.optimization_barrier((blocks, from_left, from_right))
    mine = reduce_over_chips(blocks)
    away = other_core(mine)
    first = (inner[:1].astype(F32) + from_left.astype(F32)).astype(BF16)
    last = (inner[3:].astype(F32) + from_right.astype(F32)).astype(BF16)
    grad_cubes = jnp.concatenate([first, inner[1:3], last])
    sum_a, sum_b = unpack(core, mine, away)
    return (
        features.reshape(1, 1, 8, 8, 256),
        grad_cubes.reshape(1, 4, 32, 32, 64),
        sum_a.reshape(3, 3, 3, 64, 128),
        sum_b.reshape(3, 3, 3, 128, 256),
    )


def solution(mesh):
    return jax.shard_map(
        shards,
        mesh=mesh,
        in_specs=(P("rep", "slab", None, None, None), P(), P(), P("rep", "slab", None, None, None)),
        out_specs=(
            P("rep", "slab", None, None, None),
            P("rep", "slab", None, None, None),
            P(),
            P(),
        ),
        check_vma=False,
    )
```

```python
import jax
import jax.numpy as jnp
from jax import lax
from jax.experimental import pallas as pl
from jax.experimental.pallas import tpu as pltpu
from jax.sharding import PartitionSpec as P

BF16 = jnp.bfloat16
F32 = jnp.float32
ROOM = 50 * 1024 * 1024
SCALAR = pl.BlockSpec(memory_space=pltpu.SMEM)
WHOLE = pl.BlockSpec(memory_space=pltpu.VMEM)
APART = pl.BlockSpec(memory_space=pltpu.HBM)


def nt_dot(lhs, rhs):
    return lax.dot_general(lhs, rhs, (((1,), (1,)), ((), ())), preferred_element_type=F32)


def nn_dot(lhs, rhs):
    return jnp.dot(lhs, rhs, preferred_element_type=F32)


def tn_dot(lhs, rhs):
    return lax.dot_general(lhs, rhs, (((0,), (0,)), ((), ())), preferred_element_type=F32)


def next_rows(value, period):
    rows = value.shape[0]
    row = lax.broadcasted_iota(jnp.int32, value.shape, 0) % period
    return jnp.where(row == period - 1, 0.0, pltpu.roll(value, rows - 1, 0))


def previous_rows(value, period):
    row = lax.broadcasted_iota(jnp.int32, value.shape, 0) % period
    return jnp.where(row == 0, 0.0, pltpu.roll(value, 1, 0))


def low_lanes(shape):
    return lax.broadcasted_iota(jnp.int32, shape, 1) < 64


def pack_pairs(pairs, window_ref, layer):
    edge = jnp.zeros((16, 256), BF16)
    wide = pairs.astype(F32)
    outer = jnp.where(low_lanes(wide.shape), next_rows(wide, 16), previous_rows(wide, 16))
    window_ref[layer, 0:16, :] = edge
    window_ref[layer, 528:544, :] = edge
    window_ref[layer, 16:528, 0:128] = pairs
    window_ref[layer, 16:528, 128:256] = outer.astype(BF16)


def layer_terms(window_ref, source, weight_ref, shift_x, total):
    for shift_y in range(3):
        view = window_ref[source, 16 * shift_y : 16 * shift_y + 512, :]
        term = nn_dot(view, weight_ref[3 * shift_x + shift_y])
        total = term if total is None else total + term
    return total


def slope_and_pool(total):
    sigma = 1.0 / (1.0 + jnp.exp(-total))
    blocks = (total * sigma).reshape(16, 2, 16, 256)
    blocks = blocks[:, 0] + blocks[:, 1]
    slope = sigma * (1.0 + total * (1.0 - sigma))
    return slope.astype(BF16), (blocks[:, :, :128] + blocks[:, :, 128:]).reshape(256, 128)


def forward_inner_kernel(cells_ref, weight_ref, window_ref, partial_ref, slope_ref, pool_ref):
    for layer in range(4):
        pack_pairs(cells_ref[layer], window_ref, layer)
    for layer in range(4):
        total = None
        for shift_x in range(3):
            source = layer + shift_x - 1
            if 0 <= source < 4:
                total = layer_terms(window_ref, source, weight_ref, shift_x, total)
        if layer in (0, 3):
            partial_ref[layer // 3] = total
        else:
            slope_ref[layer - 1], pool_ref[layer - 1] = slope_and_pool(total)


def forward_inner(cells, weight):
    return pl.pallas_call(
        forward_inner_kernel,
        out_shape=(
            jax.ShapeDtypeStruct((4, 544, 256), BF16),
            jax.ShapeDtypeStruct((2, 512, 256), F32),
            jax.ShapeDtypeStruct((2, 512, 256), BF16),
            jax.ShapeDtypeStruct((2, 256, 128), F32),
        ),
        compiler_params=pltpu.CompilerParams(vmem_limit_bytes=ROOM),
        cost_estimate=pl.CostEstimate(flops=2 * 2048 * 2304 * 256, bytes_accessed=6 * 10**6, transcendentals=10**6),
    )(cells, weight)


def forward_outer_kernel(left_ref, right_ref, weight_ref, partial_ref, pool_ref, window_ref, slope_ref, pooled_ref):
    pack_pairs(left_ref[...], window_ref, 0)
    pack_pairs(right_ref[...], window_ref, 1)
    for side in range(2):
        total = layer_terms(window_ref, side, weight_ref, 2 * side, partial_ref[side])
        slope, pool = slope_and_pool(total)
        slope_ref[side] = slope
        pooled_ref[side] = ((pool + pool_ref[side]) * 0.125).astype(BF16)


def forward_outer(left, right, weight, partial, pool):
    return pl.pallas_call(
        forward_outer_kernel,
        out_shape=(
            jax.ShapeDtypeStruct((2, 544, 256), BF16),
            jax.ShapeDtypeStruct((2, 512, 256), BF16),
            jax.ShapeDtypeStruct((2, 256, 128), BF16),
        ),
        compiler_params=pltpu.CompilerParams(vmem_limit_bytes=ROOM),
        cost_estimate=pl.CostEstimate(flops=10**9, bytes_accessed=5 * 10**6, transcendentals=10**6),
    )(left, right, weight, partial, pool)


def block_b_kernel(core_ref, left_ref, cells_ref, right_ref, weight_ref, cot_ref, features_ref, keep_ref, send_ref, grad_ref, window, grads, column):
    edge = jnp.zeros((16, 384), BF16)
    for layer in range(6):
        if layer < 2:
            cells = left_ref[layer]
        elif layer < 4:
            cells = cells_ref[layer - 2]
        else:
            cells = right_ref[layer - 4]
        wide = cells.astype(F32)
        window[layer, 0:16, :] = edge
        window[layer, 272:288, :] = edge
        window[layer, 16:272, 0:128] = previous_rows(wide, 16).astype(BF16)
        window[layer, 16:272, 128:256] = cells
        window[layer, 16:272, 256:384] = next_rows(wide, 16).astype(BF16)
    active = None
    for layer in range(4):
        total = None
        for tap in range(9):
            shift_x, shift_y = tap // 3, tap % 3
            view = window[layer + shift_x, 16 * shift_y : 16 * shift_y + 256, :]
            term = nn_dot(view, weight_ref[tap])
            total = term if total is None else total + term
        sigma = 1.0 / (1.0 + jnp.exp(-total))
        slope = sigma * (1.0 + total * (1.0 - sigma))
        spread = cot_ref[(layer + 1) // 2].astype(F32).reshape(8, 1, 16, 256) * 0.125
        spread = jnp.broadcast_to(spread, (8, 2, 16, 256)).reshape(256, 256)
        grads[layer, 0:16, :] = edge[:, :256]
        grads[layer, 272:288, :] = edge[:, :256]
        grads[layer, 16:272, :] = (spread * slope).astype(BF16)
        if layer in (1, 2):
            blocks = (total * sigma).reshape(8, 2, 16, 256)
            blocks = blocks[:, 0] + blocks[:, 1]
            active = blocks if active is None else active + blocks
    active = active.reshape(128, 256)
    for part in range(2):
        lanes = slice(128 * part, 128 * part + 128)
        column[part] = active[:, lanes]
        pooled = column[part, pl.ds(0, 64, stride=2), :] + column[part, pl.ds(1, 64, stride=2), :]
        features_ref[:, lanes] = (pooled * 0.125).astype(BF16)
    core = core_ref[0]
    own = grads[1:3, 16:272, :].reshape(512, 256)
    for tap in range(9):
        shift_x, shift_y = tap // 3, tap % 3
        view = window[1 + shift_x : 3 + shift_x, 16 * shift_y : 16 * shift_y + 256, :].reshape(512, 384)
        terms = (tn_dot(view, own) * 0.25).astype(BF16)
        keep_ref[tap] = jnp.where(core == 0, terms[:, :128], terms[:, 128:])
        send_ref[tap] = jnp.where(core == 0, terms[:, 128:], terms[:, :128])
    for layer in range(2):
        total = None
        for tap in range(9):
            shift_x, shift_y = tap // 3, tap % 3
            view = grads[layer + 2 - shift_x, 32 - 16 * shift_y : 288 - 16 * shift_y, :]
            term = nt_dot(view, weight_ref[tap])
            total = term if total is None else total + term
        result = next_rows(total[:, 0:128], 16) + total[:, 128:256] + previous_rows(total[:, 256:384], 16)
        grad_ref[layer] = result.astype(BF16)


def block_b(core, left, cells, right, weight, cot):
    return pl.pallas_call(
        block_b_kernel,
        in_specs=[SCALAR] + [WHOLE] * 5,
        out_shape=(
            jax.ShapeDtypeStruct((64, 256), BF16),
            jax.ShapeDtypeStruct((9, 384, 128), BF16),
            jax.ShapeDtypeStruct((9, 384, 128), BF16),
            jax.ShapeDtypeStruct((2, 256, 128), BF16),
        ),
        scratch_shapes=[
            pltpu.VMEM((6, 288, 384), BF16),
            pltpu.VMEM((4, 288, 256), BF16),
            pltpu.VMEM((2, 128, 128), F32),
        ],
        compiler_params=pltpu.CompilerParams(vmem_limit_bytes=ROOM),
        cost_estimate=pl.CostEstimate(flops=4 * 2 * 512 * 3456 * 256, bytes_accessed=5 * 10**6, transcendentals=5 * 10**5),
    )(core, left, cells, right, weight, cot)


def kernel_a_kernel(core_ref, grad_ref, slope_ref, ends_ref, window_ref, sides_ref, pre_out, keep_ref, send_ref, pre_ref, sem):
    core = core_ref[0]
    edge = jnp.zeros((16, 256), BF16)
    for layer in range(4):
        spread = grad_ref[layer // 2].astype(F32).reshape(16, 1, 16, 128) * 0.125
        spread = jnp.broadcast_to(spread, (16, 2, 16, 128)).reshape(512, 128)
        slope = (ends_ref[layer // 3] if layer in (0, 3) else slope_ref[layer - 1]).astype(F32)
        pre_ref[layer, 0:16, :] = edge
        pre_ref[layer, 528:544, :] = edge
        pre_ref[layer, 16:528, 0:128] = (spread * slope[:, 0:128]).astype(BF16)
        pre_ref[layer, 16:528, 128:256] = (spread * slope[:, 128:256]).astype(BF16)
    store = pltpu.make_async_copy(pre_ref, pre_out, sem)
    store.start()
    grads = pre_ref[:, 16:528, :].reshape(2048, 256)
    for tap in range(9):
        shift_x, shift_y = tap // 3, tap % 3
        rows = slice(16 * shift_y, 16 * shift_y + 512)
        if shift_x == 0:
            terms = tn_dot(window_ref[0:3, rows].reshape(1536, 256), grads[512:]) + tn_dot(sides_ref[0, rows], grads[:512])
        elif shift_x == 1:
            terms = tn_dot(window_ref[:, rows].reshape(2048, 256), grads)
        else:
            terms = tn_dot(window_ref[1:4, rows].reshape(1536, 256), grads[:1536]) + tn_dot(sides_ref[1, rows], grads[1536:])
        terms = terms * 0.25
        even, odd = terms[:, :128], terms[:, 128:]
        first = jnp.concatenate([even[192:256] + odd[0:64], even[0:32] + odd[64:96]]).astype(BF16)
        second = (even[32:128] + odd[96:192]).astype(BF16)
        keep_ref[tap] = jnp.where(core == 0, first, second)
        send_ref[tap] = jnp.where(core == 0, second, first)
    store.wait()


def kernel_a(core, grad, slope, ends, window, sides):
    return pl.pallas_call(
        kernel_a_kernel,
        in_specs=[SCALAR] + [WHOLE] * 5,
        out_specs=(APART, WHOLE, WHOLE),
        scratch_shapes=[pltpu.VMEM((4, 544, 256), BF16), pltpu.SemaphoreType.DMA],
        out_shape=(
            jax.ShapeDtypeStruct((4, 544, 256), BF16),
            jax.ShapeDtypeStruct((9, 96, 128), BF16),
            jax.ShapeDtypeStruct((9, 96, 128), BF16),
        ),
        compiler_params=pltpu.CompilerParams(vmem_limit_bytes=ROOM),
        cost_estimate=pl.CostEstimate(flops=2 * 2048 * 2304 * 256, bytes_accessed=6 * 10**6, transcendentals=0),
    )(core, grad, slope, ends, window, sides)


def back_a_kernel(grads_ref, weight_ref, inner_ref, to_left_ref, to_right_ref):
    for layer in range(-1, 5):
        total = None
        for tap in range(9):
            shift_x, shift_y = tap // 3, tap % 3
            source = layer + 1 - shift_x
            if 0 <= source < 4:
                view = grads_ref[source, 32 - 16 * shift_y : 544 - 16 * shift_y, :]
                term = nt_dot(view, weight_ref[tap])
                total = term if total is None else total + term
        outer = total[:, 128:256]
        outer = jnp.where(low_lanes(outer.shape), previous_rows(outer, 16), next_rows(outer, 16))
        result = (total[:, 0:128] + outer).astype(BF16)
        if layer == -1:
            to_left_ref[...] = result
        elif layer == 4:
            to_right_ref[...] = result
        else:
            inner_ref[layer] = result


def back_a(grads, weight):
    return pl.pallas_call(
        back_a_kernel,
        out_shape=(
            jax.ShapeDtypeStruct((4, 512, 128), BF16),
            jax.ShapeDtypeStruct((512, 128), BF16),
            jax.ShapeDtypeStruct((512, 128), BF16),
        ),
        compiler_params=pltpu.CompilerParams(vmem_limit_bytes=ROOM),
        cost_estimate=pl.CostEstimate(flops=2 * 2048 * 2304 * 256, bytes_accessed=4 * 10**6, transcendentals=0),
    )(grads, weight)


def paired_weight(weight):
    taps = weight.reshape(9, 3, 64, 128)
    none = jnp.zeros((9, 64, 128), weight.dtype)
    even = jnp.concatenate([taps[:, 1], taps[:, 2], none, taps[:, 0]], axis=1)
    odd = jnp.concatenate([taps[:, 0], taps[:, 1], taps[:, 2], none], axis=1)
    return jnp.concatenate([even, odd], axis=2)


def merge_kernel(keep_a_ref, other_a_ref, keep_b_ref, other_b_ref, rows_ref):
    for tap in range(9):
        rows = keep_a_ref[tap].astype(F32) + other_a_ref[tap].astype(F32)
        rows_ref[96 * tap : 96 * tap + 96] = rows.astype(BF16)
        rows = keep_b_ref[tap].astype(F32) + other_b_ref[tap].astype(F32)
        rows_ref[864 + 384 * tap : 1248 + 384 * tap] = rows.astype(BF16)
    rows_ref[4320:4352] = jnp.zeros((32, 128), BF16)


def merge(keep_a, other_a, keep_b, other_b):
    return pl.pallas_call(
        merge_kernel,
        out_shape=jax.ShapeDtypeStruct((4352, 128), BF16),
        compiler_params=pltpu.CompilerParams(vmem_limit_bytes=ROOM),
        cost_estimate=pl.CostEstimate(flops=0, bytes_accessed=4 * 10**6, transcendentals=0),
    )(keep_a, other_a, keep_b, other_b)


def unpack_kernel(core_ref, mine_ref, away_ref, sum_a_ref, sum_b_ref):
    core = core_ref[0]
    for tap in range(9):
        rows = slice(96 * tap, 96 * tap + 96)
        mine, away = mine_ref[rows].astype(F32), away_ref[rows].astype(F32)
        sum_a_ref[tap, 0] = jnp.where(core == 0, mine, away)
        sum_a_ref[tap, 1] = jnp.where(core == 0, away, mine)
        rows = slice(864 + 384 * tap, 1248 + 384 * tap)
        mine, away = mine_ref[rows].astype(F32), away_ref[rows].astype(F32)
        sum_b_ref[tap, :, 0:128] = jnp.where(core == 0, mine, away)
        sum_b_ref[tap, :, 128:256] = jnp.where(core == 0, away, mine)


def unpack(core, mine, away):
    return pl.pallas_call(
        unpack_kernel,
        in_specs=[SCALAR] + [WHOLE] * 2,
        out_shape=(
            jax.ShapeDtypeStruct((9, 2, 96, 128), F32),
            jax.ShapeDtypeStruct((9, 384, 256), F32),
        ),
        compiler_params=pltpu.CompilerParams(vmem_limit_bytes=ROOM),
        cost_estimate=pl.CostEstimate(flops=0, bytes_accessed=7 * 10**6, transcendentals=0),
    )(core, mine, away)


AXES = ("slab", "rep")
ACROSS = [[((16 * x + 4 * y + z) * 4 + rep) for x in range(4) for y in range(4)] for z in range(4) for rep in range(4)]
ALONG = [[((4 * plane + z) * 4 + 2 * far + core) for far in range(2) for z in range(4)] for plane in range(16) for core in range(2)]
CORES = [(device, device ^ 1) for device in range(256)]


def other_core(value):
    return lax.ppermute(value, AXES, CORES)


def exchange(blocks, groups):
    return lax.all_to_all(blocks, AXES, 0, 0, axis_index_groups=groups, tiled=True)


def total_of(blocks):
    return jnp.sum(blocks.astype(F32), axis=0).astype(BF16)


def neighbours(to_left, to_right):
    count = lax.axis_size("slab")
    up = [(i, i + 1) for i in range(count - 1)]
    down = [(i + 1, i) for i in range(count - 1)]
    return lax.ppermute(to_right, "slab", up), lax.ppermute(to_left, "slab", down)


def shards(cubes, weight_a, weight_b, cotangent):
    core = (lax.axis_index("rep") % 2).reshape(1)
    pair_weight = paired_weight(weight_a)
    taps_b = weight_b.reshape(9, 384, 256)
    cells = cubes.reshape(4, 512, 128)
    cot = cotangent.reshape(64, 256)
    cot_rows = [cot[:, :128], cot[:, 128:]]
    left, right = neighbours(jnp.concatenate([cells[0]] + cot_rows), jnp.concatenate([cells[3]] + cot_rows))
    window, partial, slope_a, pool = forward_inner(cells, pair_weight)
    sides, ends, pooled = forward_outer(left[:512], right[:512], pair_weight, partial, pool)
    pooled_left, pooled_right = neighbours(pooled, pooled)
    cots = [jnp.concatenate([side[512:576], side[576:640]], axis=1) for side in (left, right)]
    cots = jnp.stack([cots[0], cot, cots[1]])
    cots = jnp.broadcast_to(cots[:, :, None, :], (3, 64, 2, 256)).reshape(3, 128, 256)
    features, keep_b, send_b, grad_pooled = block_b(core, pooled_left, pooled, pooled_right, taps_b, cots)
    other_b = other_core(send_b)
    grad_pre, keep_a, send_a = kernel_a(core, grad_pooled, slope_a, ends, window, sides)
    other_a = other_core(send_a)
    inner, to_left, to_right = back_a(grad_pre, pair_weight)
    rows = merge(keep_a, other_a, keep_b, other_b)
    blocks = exchange(rows.reshape(16, 272, 128), ACROSS)
    blocks, to_left, to_right = lax.optimization_barrier((blocks, to_left, to_right))
    blocks = exchange(jnp.broadcast_to(total_of(blocks), (8, 272, 128)), ALONG)
    blocks, to_left, to_right = lax.optimization_barrier((blocks, to_left, to_right))
    from_left, from_right = neighbours(to_left, to_right)
    blocks = exchange(jnp.broadcast_to(total_of(blocks), (16, 272, 128)), ACROSS)
    blocks, from_left, from_right = lax.optimization_barrier((blocks, from_left, from_right))
    mine = blocks.reshape(4352, 128)
    away = other_core(mine)
    first = (inner[:1].astype(F32) + from_left.astype(F32)).astype(BF16)
    last = (inner[3:].astype(F32) + from_right.astype(F32)).astype(BF16)
    grad_cubes = jnp.concatenate([first, inner[1:3], last])
    sum_a, sum_b = unpack(core, mine, away)
    return (
        features.reshape(1, 1, 8, 8, 256),
        grad_cubes.reshape(1, 4, 32, 32, 64),
        sum_a.reshape(3, 3, 3, 64, 128),
        sum_b.reshape(3, 3, 3, 128, 256),
    )


def solution(mesh):
    return jax.shard_map(
        shards,
        mesh=mesh,
        in_specs=(P("rep", "slab", None, None, None), P(), P(), P("rep", "slab", None, None, None)),
        out_specs=(
            P("rep", "slab", None, None, None),
            P("rep", "slab", None, None, None),
            P(),
            P(),
        ),
        check_vma=False,
    )
```

```python
import jax
import jax.numpy as jnp
from jax import lax
from jax.experimental import pallas as pl
from jax.experimental.pallas import tpu as pltpu
from jax.sharding import PartitionSpec as P

BF16 = jnp.bfloat16
F32 = jnp.float32
ROOM = 50 * 1024 * 1024
SCALAR = pl.BlockSpec(memory_space=pltpu.SMEM)
WHOLE = pl.BlockSpec(memory_space=pltpu.VMEM)
APART = pl.BlockSpec(memory_space=pltpu.HBM)


def nt_dot(lhs, rhs):
    return lax.dot_general(lhs, rhs, (((1,), (1,)), ((), ())), preferred_element_type=F32)


def nn_dot(lhs, rhs):
    return jnp.dot(lhs, rhs, preferred_element_type=F32)


def tn_dot(lhs, rhs):
    return lax.dot_general(lhs, rhs, (((0,), (0,)), ((), ())), preferred_element_type=F32)


def next_rows(value, period):
    rows = value.shape[0]
    row = lax.broadcasted_iota(jnp.int32, value.shape, 0) % period
    return jnp.where(row == period - 1, 0.0, pltpu.roll(value, rows - 1, 0))


def previous_rows(value, period):
    row = lax.broadcasted_iota(jnp.int32, value.shape, 0) % period
    return jnp.where(row == 0, 0.0, pltpu.roll(value, 1, 0))


def low_lanes(shape):
    return lax.broadcasted_iota(jnp.int32, shape, 1) < 64


def pack_pairs(pairs, window_ref, layer):
    edge = jnp.zeros((16, 256), BF16)
    wide = pairs.astype(F32)
    outer = jnp.where(low_lanes(wide.shape), next_rows(wide, 16), previous_rows(wide, 16))
    window_ref[layer, 0:16, :] = edge
    window_ref[layer, 528:544, :] = edge
    window_ref[layer, 16:528, 0:128] = pairs
    window_ref[layer, 16:528, 128:256] = outer.astype(BF16)


def layer_terms(window_ref, source, weight_ref, shift_x, total):
    for shift_y in range(3):
        view = window_ref[source, 16 * shift_y : 16 * shift_y + 512, :]
        term = nn_dot(view, weight_ref[3 * shift_x + shift_y])
        total = term if total is None else total + term
    return total


def slope_and_pool(total):
    sigma = 1.0 / (1.0 + jnp.exp(-total))
    blocks = (total * sigma).reshape(16, 2, 16, 256)
    blocks = blocks[:, 0] + blocks[:, 1]
    slope = sigma * (1.0 + total * (1.0 - sigma))
    return slope.astype(BF16), (blocks[:, :, :128] + blocks[:, :, 128:]).reshape(256, 128)


def forward_inner_kernel(cells_ref, weight_ref, window_ref, partial_ref, slope_ref, pool_ref):
    for layer in range(4):
        pack_pairs(cells_ref[layer], window_ref, layer)
    for layer in range(4):
        total = None
        for shift_x in range(3):
            source = layer + shift_x - 1
            if 0 <= source < 4:
                total = layer_terms(window_ref, source, weight_ref, shift_x, total)
        if layer in (0, 3):
            partial_ref[layer // 3] = total
        else:
            slope_ref[layer - 1], pool_ref[layer - 1] = slope_and_pool(total)


def forward_inner(cells, weight):
    return pl.pallas_call(
        forward_inner_kernel,
        out_shape=(
            jax.ShapeDtypeStruct((4, 544, 256), BF16),
            jax.ShapeDtypeStruct((2, 512, 256), F32),
            jax.ShapeDtypeStruct((2, 512, 256), BF16),
            jax.ShapeDtypeStruct((2, 256, 128), F32),
        ),
        compiler_params=pltpu.CompilerParams(vmem_limit_bytes=ROOM),
        cost_estimate=pl.CostEstimate(flops=2 * 2048 * 2304 * 256, bytes_accessed=6 * 10**6, transcendentals=10**6),
    )(cells, weight)


def forward_outer_kernel(left_ref, right_ref, weight_ref, partial_ref, pool_ref, window_ref, slope_ref, pooled_ref):
    pack_pairs(left_ref[...], window_ref, 0)
    pack_pairs(right_ref[...], window_ref, 1)
    for side in range(2):
        total = layer_terms(window_ref, side, weight_ref, 2 * side, partial_ref[side])
        slope, pool = slope_and_pool(total)
        slope_ref[side] = slope
        pooled_ref[side] = ((pool + pool_ref[side]) * 0.125).astype(BF16)


def forward_outer(left, right, weight, partial, pool):
    return pl.pallas_call(
        forward_outer_kernel,
        out_shape=(
            jax.ShapeDtypeStruct((2, 544, 256), BF16),
            jax.ShapeDtypeStruct((2, 512, 256), BF16),
            jax.ShapeDtypeStruct((2, 256, 128), BF16),
        ),
        compiler_params=pltpu.CompilerParams(vmem_limit_bytes=ROOM),
        cost_estimate=pl.CostEstimate(flops=10**9, bytes_accessed=5 * 10**6, transcendentals=10**6),
    )(left, right, weight, partial, pool)


def block_b_kernel(core_ref, left_ref, cells_ref, right_ref, weight_ref, cot_ref, features_ref, keep_ref, send_ref, grad_ref, window, grads, column):
    edge = jnp.zeros((16, 384), BF16)
    for layer in range(6):
        if layer < 2:
            cells = left_ref[layer]
        elif layer < 4:
            cells = cells_ref[layer - 2]
        else:
            cells = right_ref[layer - 4]
        wide = cells.astype(F32)
        window[layer, 0:16, :] = edge
        window[layer, 272:288, :] = edge
        window[layer, 16:272, 0:128] = previous_rows(wide, 16).astype(BF16)
        window[layer, 16:272, 128:256] = cells
        window[layer, 16:272, 256:384] = next_rows(wide, 16).astype(BF16)
    active = None
    for layer in range(4):
        total = None
        for tap in range(9):
            shift_x, shift_y = tap // 3, tap % 3
            view = window[layer + shift_x, 16 * shift_y : 16 * shift_y + 256, :]
            term = nn_dot(view, weight_ref[tap])
            total = term if total is None else total + term
        sigma = 1.0 / (1.0 + jnp.exp(-total))
        slope = sigma * (1.0 + total * (1.0 - sigma))
        spread = cot_ref[(layer + 1) // 2].astype(F32).reshape(8, 1, 16, 256) * 0.125
        spread = jnp.broadcast_to(spread, (8, 2, 16, 256)).reshape(256, 256)
        grads[layer, 0:16, :] = edge[:, :256]
        grads[layer, 272:288, :] = edge[:, :256]
        grads[layer, 16:272, :] = (spread * slope).astype(BF16)
        if layer in (1, 2):
            blocks = (total * sigma).reshape(8, 2, 16, 256)
            blocks = blocks[:, 0] + blocks[:, 1]
            active = blocks if active is None else active + blocks
    active = active.reshape(128, 256)
    for part in range(2):
        lanes = slice(128 * part, 128 * part + 128)
        column[part] = active[:, lanes]
        pooled = column[part, pl.ds(0, 64, stride=2), :] + column[part, pl.ds(1, 64, stride=2), :]
        features_ref[:, lanes] = (pooled * 0.125).astype(BF16)
    core = core_ref[0]
    own = grads[1:3, 16:272, :].reshape(512, 256)
    for tap in range(9):
        shift_x, shift_y = tap // 3, tap % 3
        view = window[1 + shift_x : 3 + shift_x, 16 * shift_y : 16 * shift_y + 256, :].reshape(512, 384)
        terms = (tn_dot(view, own) * 0.25).astype(BF16)
        keep_ref[tap] = jnp.where(core == 0, terms[:, :128], terms[:, 128:])
        send_ref[tap] = jnp.where(core == 0, terms[:, 128:], terms[:, :128])
    for layer in range(2):
        total = None
        for tap in range(9):
            shift_x, shift_y = tap // 3, tap % 3
            view = grads[layer + 2 - shift_x, 32 - 16 * shift_y : 288 - 16 * shift_y, :]
            term = nt_dot(view, weight_ref[tap])
            total = term if total is None else total + term
        result = next_rows(total[:, 0:128], 16) + total[:, 128:256] + previous_rows(total[:, 256:384], 16)
        grad_ref[layer] = result.astype(BF16)


def block_b(core, left, cells, right, weight, cot):
    return pl.pallas_call(
        block_b_kernel,
        in_specs=[SCALAR] + [WHOLE] * 5,
        out_shape=(
            jax.ShapeDtypeStruct((64, 256), BF16),
            jax.ShapeDtypeStruct((9, 384, 128), BF16),
            jax.ShapeDtypeStruct((9, 384, 128), BF16),
            jax.ShapeDtypeStruct((2, 256, 128), BF16),
        ),
        scratch_shapes=[
            pltpu.VMEM((6, 288, 384), BF16),
            pltpu.VMEM((4, 288, 256), BF16),
            pltpu.VMEM((2, 128, 128), F32),
        ],
        compiler_params=pltpu.CompilerParams(vmem_limit_bytes=ROOM),
        cost_estimate=pl.CostEstimate(flops=4 * 2 * 512 * 3456 * 256, bytes_accessed=5 * 10**6, transcendentals=5 * 10**5),
    )(core, left, cells, right, weight, cot)


def kernel_a_kernel(core_ref, grad_ref, slope_ref, ends_ref, window_ref, sides_ref, pre_out, keep_ref, send_ref, pre_ref, sem):
    core = core_ref[0]
    edge = jnp.zeros((16, 256), BF16)
    for layer in range(4):
        spread = grad_ref[layer // 2].astype(F32).reshape(16, 1, 16, 128) * 0.125
        spread = jnp.broadcast_to(spread, (16, 2, 16, 128)).reshape(512, 128)
        slope = (ends_ref[layer // 3] if layer in (0, 3) else slope_ref[layer - 1]).astype(F32)
        pre_ref[layer, 0:16, :] = edge
        pre_ref[layer, 528:544, :] = edge
        pre_ref[layer, 16:528, 0:128] = (spread * slope[:, 0:128]).astype(BF16)
        pre_ref[layer, 16:528, 128:256] = (spread * slope[:, 128:256]).astype(BF16)
    store = pltpu.make_async_copy(pre_ref, pre_out, sem)
    store.start()
    grads = pre_ref[:, 16:528, :].reshape(2048, 256)
    for tap in range(9):
        shift_x, shift_y = tap // 3, tap % 3
        rows = slice(16 * shift_y, 16 * shift_y + 512)
        if shift_x == 0:
            terms = tn_dot(window_ref[0:3, rows].reshape(1536, 256), grads[512:]) + tn_dot(sides_ref[0, rows], grads[:512])
        elif shift_x == 1:
            terms = tn_dot(window_ref[:, rows].reshape(2048, 256), grads)
        else:
            terms = tn_dot(window_ref[1:4, rows].reshape(1536, 256), grads[:1536]) + tn_dot(sides_ref[1, rows], grads[1536:])
        terms = terms * 0.25
        even, odd = terms[:, :128], terms[:, 128:]
        first = jnp.concatenate([even[192:256] + odd[0:64], even[0:32] + odd[64:96]]).astype(BF16)
        second = (even[32:128] + odd[96:192]).astype(BF16)
        keep_ref[tap] = jnp.where(core == 0, first, second)
        send_ref[tap] = jnp.where(core == 0, second, first)
    store.wait()


def kernel_a(core, grad, slope, ends, window, sides):
    return pl.pallas_call(
        kernel_a_kernel,
        in_specs=[SCALAR] + [WHOLE] * 5,
        out_specs=(APART, WHOLE, WHOLE),
        scratch_shapes=[pltpu.VMEM((4, 544, 256), BF16), pltpu.SemaphoreType.DMA],
        out_shape=(
            jax.ShapeDtypeStruct((4, 544, 256), BF16),
            jax.ShapeDtypeStruct((9, 96, 128), BF16),
            jax.ShapeDtypeStruct((9, 96, 128), BF16),
        ),
        compiler_params=pltpu.CompilerParams(vmem_limit_bytes=ROOM),
        cost_estimate=pl.CostEstimate(flops=2 * 2048 * 2304 * 256, bytes_accessed=6 * 10**6, transcendentals=0),
    )(core, grad, slope, ends, window, sides)


def back_a_kernel(grads_ref, weight_ref, inner_ref, to_left_ref, to_right_ref):
    for layer in range(-1, 5):
        total = None
        for tap in range(9):
            shift_x, shift_y = tap // 3, tap % 3
            source = layer + 1 - shift_x
            if 0 <= source < 4:
                view = grads_ref[source, 32 - 16 * shift_y : 544 - 16 * shift_y, :]
                term = nt_dot(view, weight_ref[tap])
                total = term if total is None else total + term
        outer = total[:, 128:256]
        outer = jnp.where(low_lanes(outer.shape), previous_rows(outer, 16), next_rows(outer, 16))
        result = (total[:, 0:128] + outer).astype(BF16)
        if layer == -1:
            to_left_ref[...] = result
        elif layer == 4:
            to_right_ref[...] = result
        else:
            inner_ref[layer] = result


def back_a(grads, weight):
    return pl.pallas_call(
        back_a_kernel,
        out_shape=(
            jax.ShapeDtypeStruct((4, 512, 128), BF16),
            jax.ShapeDtypeStruct((512, 128), BF16),
            jax.ShapeDtypeStruct((512, 128), BF16),
        ),
        compiler_params=pltpu.CompilerParams(vmem_limit_bytes=ROOM),
        cost_estimate=pl.CostEstimate(flops=2 * 2048 * 2304 * 256, bytes_accessed=4 * 10**6, transcendentals=0),
    )(grads, weight)


def paired_weight(weight):
    taps = weight.reshape(9, 3, 64, 128)
    none = jnp.zeros((9, 64, 128), weight.dtype)
    even = jnp.concatenate([taps[:, 1], taps[:, 2], none, taps[:, 0]], axis=1)
    odd = jnp.concatenate([taps[:, 0], taps[:, 1], taps[:, 2], none], axis=1)
    return jnp.concatenate([even, odd], axis=2)


def merge_kernel(keep_a_ref, other_a_ref, keep_b_ref, other_b_ref, rows_ref):
    for tap in range(9):
        rows = keep_a_ref[tap].astype(F32) + other_a_ref[tap].astype(F32)
        rows_ref[96 * tap : 96 * tap + 96] = rows.astype(BF16)
        rows = keep_b_ref[tap].astype(F32) + other_b_ref[tap].astype(F32)
        rows_ref[864 + 384 * tap : 1248 + 384 * tap] = rows.astype(BF16)
    rows_ref[4320:4352] = jnp.zeros((32, 128), BF16)


def merge(keep_a, other_a, keep_b, other_b):
    return pl.pallas_call(
        merge_kernel,
        out_shape=jax.ShapeDtypeStruct((4352, 128), BF16),
        compiler_params=pltpu.CompilerParams(vmem_limit_bytes=ROOM),
        cost_estimate=pl.CostEstimate(flops=0, bytes_accessed=4 * 10**6, transcendentals=0),
    )(keep_a, other_a, keep_b, other_b)


def unpack_kernel(core_ref, mine_ref, away_ref, sum_a_ref, sum_b_ref):
    core = core_ref[0]
    for tap in range(9):
        rows = slice(96 * tap, 96 * tap + 96)
        mine, away = mine_ref[rows].astype(F32), away_ref[rows].astype(F32)
        sum_a_ref[tap, 0] = jnp.where(core == 0, mine, away)
        sum_a_ref[tap, 1] = jnp.where(core == 0, away, mine)
        rows = slice(864 + 384 * tap, 1248 + 384 * tap)
        mine, away = mine_ref[rows].astype(F32), away_ref[rows].astype(F32)
        sum_b_ref[tap, :, 0:128] = jnp.where(core == 0, mine, away)
        sum_b_ref[tap, :, 128:256] = jnp.where(core == 0, away, mine)


def unpack(core, mine, away):
    return pl.pallas_call(
        unpack_kernel,
        in_specs=[SCALAR] + [WHOLE] * 2,
        out_shape=(
            jax.ShapeDtypeStruct((9, 2, 96, 128), F32),
            jax.ShapeDtypeStruct((9, 384, 256), F32),
        ),
        compiler_params=pltpu.CompilerParams(vmem_limit_bytes=ROOM),
        cost_estimate=pl.CostEstimate(flops=0, bytes_accessed=7 * 10**6, transcendentals=0),
    )(core, mine, away)


AXES = ("slab", "rep")
ACROSS = [[((16 * x + 4 * y + z) * 4 + rep) for x in range(4) for y in range(4)] for z in range(4) for rep in range(4)]
ALONG = [[((4 * plane + z) * 4 + 2 * far + core) for far in range(2) for z in range(4)] for plane in range(16) for core in range(2)]
CORES = [(device, device ^ 1) for device in range(256)]


def other_core(value):
    return lax.ppermute(value, AXES, CORES)


def exchange(blocks, groups):
    return lax.all_to_all(blocks, AXES, 0, 0, axis_index_groups=groups, tiled=True)


def total_of(blocks):
    return jnp.sum(blocks.astype(F32), axis=0).astype(BF16)


def neighbours(to_left, to_right):
    count = lax.axis_size("slab")
    up = [(i, i + 1) for i in range(count - 1)]
    down = [(i + 1, i) for i in range(count - 1)]
    return lax.ppermute(to_right, "slab", up), lax.ppermute(to_left, "slab", down)


def shards(cubes, weight_a, weight_b, cotangent):
    core = (lax.axis_index("rep") % 2).reshape(1)
    pair_weight = paired_weight(weight_a)
    taps_b = weight_b.reshape(9, 384, 256)
    cells = cubes.reshape(4, 512, 128)
    cot = cotangent.reshape(64, 256)
    cot_rows = [cot[:, :128], cot[:, 128:]]
    left, right = neighbours(jnp.concatenate([cells[0]] + cot_rows), jnp.concatenate([cells[3]] + cot_rows))
    window, partial, slope_a, pool = forward_inner(cells, pair_weight)
    sides, ends, pooled = forward_outer(left[:512], right[:512], pair_weight, partial, pool)
    pooled_left, pooled_right = neighbours(pooled, pooled)
    cots = [jnp.concatenate([side[512:576], side[576:640]], axis=1) for side in (left, right)]
    cots = jnp.stack([cots[0], cot, cots[1]])
    cots = jnp.broadcast_to(cots[:, :, None, :], (3, 64, 2, 256)).reshape(3, 128, 256)
    features, keep_b, send_b, grad_pooled = block_b(core, pooled_left, pooled, pooled_right, taps_b, cots)
    other_b = other_core(send_b)
    grad_pre, keep_a, send_a = kernel_a(core, grad_pooled, slope_a, ends, window, sides)
    other_a = other_core(send_a)
    inner, to_left, to_right = back_a(grad_pre, pair_weight)
    rows = merge(keep_a, other_a, keep_b, other_b)
    blocks = exchange(rows.reshape(16, 272, 128), ACROSS)
    blocks, to_left, to_right = lax.optimization_barrier((blocks, to_left, to_right))
    from_left, from_right = neighbours(to_left, to_right)
    blocks = exchange(jnp.broadcast_to(total_of(blocks), (8, 272, 128)), ALONG)
    blocks, from_left, from_right = lax.optimization_barrier((blocks, from_left, from_right))
    mine = exchange(jnp.broadcast_to(total_of(blocks), (16, 272, 128)), ACROSS).reshape(4352, 128)
    away = other_core(mine)
    first = (inner[:1].astype(F32) + from_left.astype(F32)).astype(BF16)
    last = (inner[3:].astype(F32) + from_right.astype(F32)).astype(BF16)
    grad_cubes = jnp.concatenate([first, inner[1:3], last])
    sum_a, sum_b = unpack(core, mine, away)
    return (
        features.reshape(1, 1, 8, 8, 256),
        grad_cubes.reshape(1, 4, 32, 32, 64),
        sum_a.reshape(3, 3, 3, 64, 128),
        sum_b.reshape(3, 3, 3, 128, 256),
    )


def solution(mesh):
    return jax.shard_map(
        shards,
        mesh=mesh,
        in_specs=(P("rep", "slab", None, None, None), P(), P(), P("rep", "slab", None, None, None)),
        out_specs=(
            P("rep", "slab", None, None, None),
            P("rep", "slab", None, None, None),
            P(),
            P(),
        ),
        check_vma=False,
    )
```

```python
import jax
import jax.numpy as jnp
from jax import lax
from jax.experimental import pallas as pl
from jax.experimental.pallas import tpu as pltpu
from jax.sharding import PartitionSpec as P

BF16 = jnp.bfloat16
F32 = jnp.float32
ROOM = 50 * 1024 * 1024
SCALAR = pl.BlockSpec(memory_space=pltpu.SMEM)
WHOLE = pl.BlockSpec(memory_space=pltpu.VMEM)
APART = pl.BlockSpec(memory_space=pltpu.HBM)


def nt_dot(lhs, rhs):
    return lax.dot_general(lhs, rhs, (((1,), (1,)), ((), ())), preferred_element_type=F32)


def nn_dot(lhs, rhs):
    return jnp.dot(lhs, rhs, preferred_element_type=F32)


def tn_dot(lhs, rhs):
    return lax.dot_general(lhs, rhs, (((0,), (0,)), ((), ())), preferred_element_type=F32)


def next_rows(value, period):
    rows = value.shape[0]
    row = lax.broadcasted_iota(jnp.int32, value.shape, 0) % period
    return jnp.where(row == period - 1, 0.0, pltpu.roll(value, rows - 1, 0))


def previous_rows(value, period):
    row = lax.broadcasted_iota(jnp.int32, value.shape, 0) % period
    return jnp.where(row == 0, 0.0, pltpu.roll(value, 1, 0))


def low_lanes(shape):
    return lax.broadcasted_iota(jnp.int32, shape, 1) < 64


def pack_pairs(pairs, window_ref, layer):
    edge = jnp.zeros((16, 256), BF16)
    wide = pairs.astype(F32)
    outer = jnp.where(low_lanes(wide.shape), next_rows(wide, 16), previous_rows(wide, 16))
    window_ref[layer, 0:16, :] = edge
    window_ref[layer, 528:544, :] = edge
    window_ref[layer, 16:528, 0:128] = pairs
    window_ref[layer, 16:528, 128:256] = outer.astype(BF16)


def layer_terms(window_ref, source, weight_ref, shift_x, total):
    for shift_y in range(3):
        view = window_ref[source, 16 * shift_y : 16 * shift_y + 512, :]
        term = nn_dot(view, weight_ref[3 * shift_x + shift_y])
        total = term if total is None else total + term
    return total


def slope_and_pool(total):
    sigma = 1.0 / (1.0 + jnp.exp(-total))
    blocks = (total * sigma).reshape(16, 2, 16, 256)
    blocks = blocks[:, 0] + blocks[:, 1]
    slope = sigma * (1.0 + total * (1.0 - sigma))
    return slope.astype(BF16), (blocks[:, :, :128] + blocks[:, :, 128:]).reshape(256, 128)


def forward_inner_kernel(cells_ref, weight_ref, window_ref, partial_ref, slope_ref, pool_ref):
    for layer in range(4):
        pack_pairs(cells_ref[layer], window_ref, layer)
    for layer in range(4):
        total = None
        for shift_x in range(3):
            source = layer + shift_x - 1
            if 0 <= source < 4:
                total = layer_terms(window_ref, source, weight_ref, shift_x, total)
        if layer in (0, 3):
            partial_ref[layer // 3] = total
        else:
            slope_ref[layer - 1], pool_ref[layer - 1] = slope_and_pool(total)


def forward_inner(cells, weight):
    return pl.pallas_call(
        forward_inner_kernel,
        out_shape=(
            jax.ShapeDtypeStruct((4, 544, 256), BF16),
            jax.ShapeDtypeStruct((2, 512, 256), F32),
            jax.ShapeDtypeStruct((2, 512, 256), BF16),
            jax.ShapeDtypeStruct((2, 256, 128), F32),
        ),
        compiler_params=pltpu.CompilerParams(vmem_limit_bytes=ROOM),
        cost_estimate=pl.CostEstimate(flops=2 * 2048 * 2304 * 256, bytes_accessed=6 * 10**6, transcendentals=10**6),
    )(cells, weight)


def forward_outer_kernel(left_ref, right_ref, weight_ref, partial_ref, pool_ref, window_ref, slope_ref, pooled_ref):
    pack_pairs(left_ref[...], window_ref, 0)
    pack_pairs(right_ref[...], window_ref, 1)
    for side in range(2):
        total = layer_terms(window_ref, side, weight_ref, 2 * side, partial_ref[side])
        slope, pool = slope_and_pool(total)
        slope_ref[side] = slope
        pooled_ref[side] = ((pool + pool_ref[side]) * 0.125).astype(BF16)


def forward_outer(left, right, weight, partial, pool):
    return pl.pallas_call(
        forward_outer_kernel,
        out_shape=(
            jax.ShapeDtypeStruct((2, 544, 256), BF16),
            jax.ShapeDtypeStruct((2, 512, 256), BF16),
            jax.ShapeDtypeStruct((2, 256, 128), BF16),
        ),
        compiler_params=pltpu.CompilerParams(vmem_limit_bytes=ROOM),
        cost_estimate=pl.CostEstimate(flops=10**9, bytes_accessed=5 * 10**6, transcendentals=10**6),
    )(left, right, weight, partial, pool)


def block_b_kernel(core_ref, left_ref, cells_ref, right_ref, weight_ref, cot_ref, features_ref, keep_ref, send_ref, grad_ref, window, grads, column):
    edge = jnp.zeros((16, 384), BF16)
    for layer in range(6):
        if layer < 2:
            cells = left_ref[layer]
        elif layer < 4:
            cells = cells_ref[layer - 2]
        else:
            cells = right_ref[layer - 4]
        wide = cells.astype(F32)
        window[layer, 0:16, :] = edge
        window[layer, 272:288, :] = edge
        window[layer, 16:272, 0:128] = previous_rows(wide, 16).astype(BF16)
        window[layer, 16:272, 128:256] = cells
        window[layer, 16:272, 256:384] = next_rows(wide, 16).astype(BF16)
    active = None
    for layer in range(4):
        total = None
        for tap in range(9):
            shift_x, shift_y = tap // 3, tap % 3
            view = window[layer + shift_x, 16 * shift_y : 16 * shift_y + 256, :]
            term = nn_dot(view, weight_ref[tap])
            total = term if total is None else total + term
        sigma = 1.0 / (1.0 + jnp.exp(-total))
        slope = sigma * (1.0 + total * (1.0 - sigma))
        spread = cot_ref[(layer + 1) // 2].astype(F32).reshape(8, 1, 16, 256) * 0.125
        spread = jnp.broadcast_to(spread, (8, 2, 16, 256)).reshape(256, 256)
        grads[layer, 0:16, :] = edge[:, :256]
        grads[layer, 272:288, :] = edge[:, :256]
        grads[layer, 16:272, :] = (spread * slope).astype(BF16)
        if layer in (1, 2):
            blocks = (total * sigma).reshape(8, 2, 16, 256)
            blocks = blocks[:, 0] + blocks[:, 1]
            active = blocks if active is None else active + blocks
    active = active.reshape(128, 256)
    for part in range(2):
        lanes = slice(128 * part, 128 * part + 128)
        column[part] = active[:, lanes]
        pooled = column[part, pl.ds(0, 64, stride=2), :] + column[part, pl.ds(1, 64, stride=2), :]
        features_ref[:, lanes] = (pooled * 0.125).astype(BF16)
    core = core_ref[0]
    own = grads[1:3, 16:272, :].reshape(512, 256)
    for tap in range(9):
        shift_x, shift_y = tap // 3, tap % 3
        view = window[1 + shift_x : 3 + shift_x, 16 * shift_y : 16 * shift_y + 256, :].reshape(512, 384)
        terms = (tn_dot(view, own) * 0.25).astype(BF16)
        keep_ref[tap] = jnp.where(core == 0, terms[:, :128], terms[:, 128:])
        send_ref[tap] = jnp.where(core == 0, terms[:, 128:], terms[:, :128])
    for layer in range(2):
        total = None
        for tap in range(9):
            shift_x, shift_y = tap // 3, tap % 3
            view = grads[layer + 2 - shift_x, 32 - 16 * shift_y : 288 - 16 * shift_y, :]
            term = nt_dot(view, weight_ref[tap])
            total = term if total is None else total + term
        result = next_rows(total[:, 0:128], 16) + total[:, 128:256] + previous_rows(total[:, 256:384], 16)
        grad_ref[layer] = result.astype(BF16)


def block_b(core, left, cells, right, weight, cot):
    return pl.pallas_call(
        block_b_kernel,
        in_specs=[SCALAR] + [WHOLE] * 5,
        out_shape=(
            jax.ShapeDtypeStruct((64, 256), BF16),
            jax.ShapeDtypeStruct((9, 384, 128), BF16),
            jax.ShapeDtypeStruct((9, 384, 128), BF16),
            jax.ShapeDtypeStruct((2, 256, 128), BF16),
        ),
        scratch_shapes=[
            pltpu.VMEM((6, 288, 384), BF16),
            pltpu.VMEM((4, 288, 256), BF16),
            pltpu.VMEM((2, 128, 128), F32),
        ],
        compiler_params=pltpu.CompilerParams(vmem_limit_bytes=ROOM),
        cost_estimate=pl.CostEstimate(flops=4 * 2 * 512 * 3456 * 256, bytes_accessed=5 * 10**6, transcendentals=5 * 10**5),
    )(core, left, cells, right, weight, cot)


def kernel_a_kernel(core_ref, grad_ref, slope_ref, ends_ref, window_ref, sides_ref, pre_out, keep_ref, send_ref, pre_ref, sem):
    core = core_ref[0]
    edge = jnp.zeros((16, 256), BF16)
    for layer in range(4):
        spread = grad_ref[layer // 2].astype(F32).reshape(16, 1, 16, 128) * 0.125
        spread = jnp.broadcast_to(spread, (16, 2, 16, 128)).reshape(512, 128)
        slope = (ends_ref[layer // 3] if layer in (0, 3) else slope_ref[layer - 1]).astype(F32)
        pre_ref[layer, 0:16, :] = edge
        pre_ref[layer, 528:544, :] = edge
        pre_ref[layer, 16:528, 0:128] = (spread * slope[:, 0:128]).astype(BF16)
        pre_ref[layer, 16:528, 128:256] = (spread * slope[:, 128:256]).astype(BF16)
    store = pltpu.make_async_copy(pre_ref, pre_out, sem)
    store.start()
    grads = pre_ref[:, 16:528, :].reshape(2048, 256)
    for tap in range(9):
        shift_x, shift_y = tap // 3, tap % 3
        rows = slice(16 * shift_y, 16 * shift_y + 512)
        if shift_x == 0:
            terms = tn_dot(window_ref[0:3, rows].reshape(1536, 256), grads[512:]) + tn_dot(sides_ref[0, rows], grads[:512])
        elif shift_x == 1:
            terms = tn_dot(window_ref[:, rows].reshape(2048, 256), grads)
        else:
            terms = tn_dot(window_ref[1:4, rows].reshape(1536, 256), grads[:1536]) + tn_dot(sides_ref[1, rows], grads[1536:])
        terms = terms * 0.25
        even, odd = terms[:, :128], terms[:, 128:]
        first = jnp.concatenate([even[192:256] + odd[0:64], even[0:32] + odd[64:96]]).astype(BF16)
        second = (even[32:128] + odd[96:192]).astype(BF16)
        keep_ref[tap] = jnp.where(core == 0, first, second)
        send_ref[tap] = jnp.where(core == 0, second, first)
    store.wait()


def kernel_a(core, grad, slope, ends, window, sides):
    return pl.pallas_call(
        kernel_a_kernel,
        in_specs=[SCALAR] + [WHOLE] * 5,
        out_specs=(APART, WHOLE, WHOLE),
        scratch_shapes=[pltpu.VMEM((4, 544, 256), BF16), pltpu.SemaphoreType.DMA],
        out_shape=(
            jax.ShapeDtypeStruct((4, 544, 256), BF16),
            jax.ShapeDtypeStruct((9, 96, 128), BF16),
            jax.ShapeDtypeStruct((9, 96, 128), BF16),
        ),
        compiler_params=pltpu.CompilerParams(vmem_limit_bytes=ROOM),
        cost_estimate=pl.CostEstimate(flops=2 * 2048 * 2304 * 256, bytes_accessed=6 * 10**6, transcendentals=0),
    )(core, grad, slope, ends, window, sides)


def back_a_kernel(grads_ref, weight_ref, inner_ref, to_left_ref, to_right_ref):
    for layer in range(-1, 5):
        total = None
        for tap in range(9):
            shift_x, shift_y = tap // 3, tap % 3
            source = layer + 1 - shift_x
            if 0 <= source < 4:
                view = grads_ref[source, 32 - 16 * shift_y : 544 - 16 * shift_y, :]
                term = nt_dot(view, weight_ref[tap])
                total = term if total is None else total + term
        outer = total[:, 128:256]
        outer = jnp.where(low_lanes(outer.shape), previous_rows(outer, 16), next_rows(outer, 16))
        result = (total[:, 0:128] + outer).astype(BF16)
        if layer == -1:
            to_left_ref[...] = result
        elif layer == 4:
            to_right_ref[...] = result
        else:
            inner_ref[layer] = result


def back_a(grads, weight):
    return pl.pallas_call(
        back_a_kernel,
        out_shape=(
            jax.ShapeDtypeStruct((4, 512, 128), BF16),
            jax.ShapeDtypeStruct((512, 128), BF16),
            jax.ShapeDtypeStruct((512, 128), BF16),
        ),
        compiler_params=pltpu.CompilerParams(vmem_limit_bytes=ROOM),
        cost_estimate=pl.CostEstimate(flops=2 * 2048 * 2304 * 256, bytes_accessed=4 * 10**6, transcendentals=0),
    )(grads, weight)


def paired_weight(weight):
    taps = weight.reshape(9, 3, 64, 128)
    none = jnp.zeros((9, 64, 128), weight.dtype)
    even = jnp.concatenate([taps[:, 1], taps[:, 2], none, taps[:, 0]], axis=1)
    odd = jnp.concatenate([taps[:, 0], taps[:, 1], taps[:, 2], none], axis=1)
    return jnp.concatenate([even, odd], axis=2)


def merge_kernel(keep_a_ref, other_a_ref, keep_b_ref, other_b_ref, rows_ref):
    for tap in range(9):
        rows = keep_a_ref[tap].astype(F32) + other_a_ref[tap].astype(F32)
        rows_ref[96 * tap : 96 * tap + 96] = rows.astype(BF16)
        rows = keep_b_ref[tap].astype(F32) + other_b_ref[tap].astype(F32)
        rows_ref[864 + 384 * tap : 1248 + 384 * tap] = rows.astype(BF16)
    rows_ref[4320:4352] = jnp.zeros((32, 128), BF16)


def merge(keep_a, other_a, keep_b, other_b):
    return pl.pallas_call(
        merge_kernel,
        out_shape=jax.ShapeDtypeStruct((4352, 128), BF16),
        compiler_params=pltpu.CompilerParams(vmem_limit_bytes=ROOM),
        cost_estimate=pl.CostEstimate(flops=0, bytes_accessed=4 * 10**6, transcendentals=0),
    )(keep_a, other_a, keep_b, other_b)


def unpack_kernel(core_ref, mine_ref, away_ref, sum_a_ref, sum_b_ref):
    core = core_ref[0]
    for tap in range(9):
        rows = slice(96 * tap, 96 * tap + 96)
        mine, away = mine_ref[rows].astype(F32), away_ref[rows].astype(F32)
        sum_a_ref[tap, 0] = jnp.where(core == 0, mine, away)
        sum_a_ref[tap, 1] = jnp.where(core == 0, away, mine)
        rows = slice(864 + 384 * tap, 1248 + 384 * tap)
        mine, away = mine_ref[rows].astype(F32), away_ref[rows].astype(F32)
        sum_b_ref[tap, :, 0:128] = jnp.where(core == 0, mine, away)
        sum_b_ref[tap, :, 128:256] = jnp.where(core == 0, away, mine)


def unpack(core, mine, away):
    return pl.pallas_call(
        unpack_kernel,
        in_specs=[SCALAR] + [WHOLE] * 2,
        out_shape=(
            jax.ShapeDtypeStruct((9, 2, 96, 128), F32),
            jax.ShapeDtypeStruct((9, 384, 256), F32),
        ),
        compiler_params=pltpu.CompilerParams(vmem_limit_bytes=ROOM),
        cost_estimate=pl.CostEstimate(flops=0, bytes_accessed=7 * 10**6, transcendentals=0),
    )(core, mine, away)


AXES = ("slab", "rep")
ACROSS = [[((16 * x + 4 * y + z) * 4 + rep) for x in range(4) for y in range(4)] for z in range(4) for rep in range(4)]
ALONG = [[((4 * plane + z) * 4 + 2 * far + core) for far in range(2) for z in range(4)] for plane in range(16) for core in range(2)]
CORES = [(device, device ^ 1) for device in range(256)]


def other_core(value):
    return lax.ppermute(value, AXES, CORES)


def exchange(blocks, groups):
    return lax.all_to_all(blocks, AXES, 0, 0, axis_index_groups=groups, tiled=True)


def total_of(blocks):
    return jnp.sum(blocks.astype(F32), axis=0).astype(BF16)


def move_up(value):
    return lax.ppermute(value, "slab", [(i, i + 1) for i in range(lax.axis_size("slab") - 1)])


def move_down(value):
    return lax.ppermute(value, "slab", [(i + 1, i) for i in range(lax.axis_size("slab") - 1)])


def neighbours(to_left, to_right):
    return move_up(to_right), move_down(to_left)


def shards(cubes, weight_a, weight_b, cotangent):
    core = (lax.axis_index("rep") % 2).reshape(1)
    pair_weight = paired_weight(weight_a)
    taps_b = weight_b.reshape(9, 384, 256)
    cells = cubes.reshape(4, 512, 128)
    cot = cotangent.reshape(64, 256)
    cot_rows = [cot[:, :128], cot[:, 128:]]
    left, right = neighbours(jnp.concatenate([cells[0]] + cot_rows), jnp.concatenate([cells[3]] + cot_rows))
    window, partial, slope_a, pool = forward_inner(cells, pair_weight)
    sides, ends, pooled = forward_outer(left[:512], right[:512], pair_weight, partial, pool)
    pooled_left, pooled_right = neighbours(pooled, pooled)
    cots = [jnp.concatenate([side[512:576], side[576:640]], axis=1) for side in (left, right)]
    cots = jnp.stack([cots[0], cot, cots[1]])
    cots = jnp.broadcast_to(cots[:, :, None, :], (3, 64, 2, 256)).reshape(3, 128, 256)
    features, keep_b, send_b, grad_pooled = block_b(core, pooled_left, pooled, pooled_right, taps_b, cots)
    other_b = other_core(send_b)
    grad_pre, keep_a, send_a = kernel_a(core, grad_pooled, slope_a, ends, window, sides)
    other_a = other_core(send_a)
    inner, to_left, to_right = back_a(grad_pre, pair_weight)
    rows = merge(keep_a, other_a, keep_b, other_b)
    blocks = exchange(rows.reshape(16, 272, 128), ACROSS)
    from_right = move_down(to_left)
    blocks, from_right, to_right = lax.optimization_barrier((blocks, from_right, to_right))
    blocks = exchange(jnp.broadcast_to(total_of(blocks), (8, 272, 128)), ALONG)
    blocks, to_right = lax.optimization_barrier((blocks, to_right))
    from_left = move_up(to_right)
    blocks = exchange(jnp.broadcast_to(total_of(blocks), (16, 272, 128)), ACROSS)
    blocks, from_left = lax.optimization_barrier((blocks, from_left))
    mine = blocks.reshape(4352, 128)
    away = other_core(mine)
    first = (inner[:1].astype(F32) + from_left.astype(F32)).astype(BF16)
    last = (inner[3:].astype(F32) + from_right.astype(F32)).astype(BF16)
    grad_cubes = jnp.concatenate([first, inner[1:3], last])
    sum_a, sum_b = unpack(core, mine, away)
    return (
        features.reshape(1, 1, 8, 8, 256),
        grad_cubes.reshape(1, 4, 32, 32, 64),
        sum_a.reshape(3, 3, 3, 64, 128),
        sum_b.reshape(3, 3, 3, 128, 256),
    )


def solution(mesh):
    return jax.shard_map(
        shards,
        mesh=mesh,
        in_specs=(P("rep", "slab", None, None, None), P(), P(), P("rep", "slab", None, None, None)),
        out_specs=(
            P("rep", "slab", None, None, None),
            P("rep", "slab", None, None, None),
            P(),
            P(),
        ),
        check_vma=False,
    )
```

```python
import jax
import jax.numpy as jnp
from jax import lax
from jax.experimental import pallas as pl
from jax.experimental.pallas import tpu as pltpu
from jax.sharding import PartitionSpec as P

BF16 = jnp.bfloat16
F32 = jnp.float32
ROOM = 50 * 1024 * 1024
SCALAR = pl.BlockSpec(memory_space=pltpu.SMEM)
WHOLE = pl.BlockSpec(memory_space=pltpu.VMEM)
APART = pl.BlockSpec(memory_space=pltpu.HBM)


def nt_dot(lhs, rhs):
    return lax.dot_general(lhs, rhs, (((1,), (1,)), ((), ())), preferred_element_type=F32)


def nn_dot(lhs, rhs):
    return jnp.dot(lhs, rhs, preferred_element_type=F32)


def tn_dot(lhs, rhs):
    return lax.dot_general(lhs, rhs, (((0,), (0,)), ((), ())), preferred_element_type=F32)


def next_rows(value, period):
    rows = value.shape[0]
    row = lax.broadcasted_iota(jnp.int32, value.shape, 0) % period
    return jnp.where(row == period - 1, 0.0, pltpu.roll(value, rows - 1, 0))


def previous_rows(value, period):
    row = lax.broadcasted_iota(jnp.int32, value.shape, 0) % period
    return jnp.where(row == 0, 0.0, pltpu.roll(value, 1, 0))


def low_lanes(shape):
    return lax.broadcasted_iota(jnp.int32, shape, 1) < 64


def pack_pairs(pairs, window_ref, layer):
    edge = jnp.zeros((16, 256), BF16)
    wide = pairs.astype(F32)
    outer = jnp.where(low_lanes(wide.shape), next_rows(wide, 16), previous_rows(wide, 16))
    window_ref[layer, 0:16, :] = edge
    window_ref[layer, 528:544, :] = edge
    window_ref[layer, 16:528, 0:128] = pairs
    window_ref[layer, 16:528, 128:256] = outer.astype(BF16)


def layer_terms(window_ref, source, weight_ref, shift_x, total):
    for shift_y in range(3):
        view = window_ref[source, 16 * shift_y : 16 * shift_y + 512, :]
        term = nn_dot(view, weight_ref[3 * shift_x + shift_y])
        total = term if total is None else total + term
    return total


def slope_and_pool(total):
    sigma = 1.0 / (1.0 + jnp.exp(-total))
    blocks = (total * sigma).reshape(16, 2, 16, 256)
    blocks = blocks[:, 0] + blocks[:, 1]
    slope = sigma * (1.0 + total * (1.0 - sigma))
    return slope.astype(BF16), (blocks[:, :, :128] + blocks[:, :, 128:]).reshape(256, 128)


def forward_inner_kernel(cells_ref, weight_ref, window_ref, partial_ref, slope_ref, pool_ref):
    for layer in range(4):
        pack_pairs(cells_ref[layer], window_ref, layer)
    for layer in range(4):
        total = None
        for shift_x in range(3):
            source = layer + shift_x - 1
            if 0 <= source < 4:
                total = layer_terms(window_ref, source, weight_ref, shift_x, total)
        if layer in (0, 3):
            partial_ref[layer // 3] = total
        else:
            slope_ref[layer - 1], pool_ref[layer - 1] = slope_and_pool(total)


def forward_inner(cells, weight):
    return pl.pallas_call(
        forward_inner_kernel,
        out_shape=(
            jax.ShapeDtypeStruct((4, 544, 256), BF16),
            jax.ShapeDtypeStruct((2, 512, 256), F32),
            jax.ShapeDtypeStruct((2, 512, 256), BF16),
            jax.ShapeDtypeStruct((2, 256, 128), F32),
        ),
        compiler_params=pltpu.CompilerParams(vmem_limit_bytes=ROOM),
        cost_estimate=pl.CostEstimate(flops=2 * 2048 * 2304 * 256, bytes_accessed=6 * 10**6, transcendentals=10**6),
    )(cells, weight)


def forward_outer_kernel(left_ref, right_ref, weight_ref, partial_ref, pool_ref, window_ref, slope_ref, pooled_ref):
    pack_pairs(left_ref[...], window_ref, 0)
    pack_pairs(right_ref[...], window_ref, 1)
    for side in range(2):
        total = layer_terms(window_ref, side, weight_ref, 2 * side, partial_ref[side])
        slope, pool = slope_and_pool(total)
        slope_ref[side] = slope
        pooled_ref[side] = ((pool + pool_ref[side]) * 0.125).astype(BF16)


def forward_outer(left, right, weight, partial, pool):
    return pl.pallas_call(
        forward_outer_kernel,
        out_shape=(
            jax.ShapeDtypeStruct((2, 544, 256), BF16),
            jax.ShapeDtypeStruct((2, 512, 256), BF16),
            jax.ShapeDtypeStruct((2, 256, 128), BF16),
        ),
        compiler_params=pltpu.CompilerParams(vmem_limit_bytes=ROOM),
        cost_estimate=pl.CostEstimate(flops=10**9, bytes_accessed=5 * 10**6, transcendentals=10**6),
    )(left, right, weight, partial, pool)


def block_b_kernel(core_ref, left_ref, cells_ref, right_ref, weight_ref, cot_ref, features_ref, keep_ref, send_ref, grad_ref, window, grads, column):
    edge = jnp.zeros((16, 384), BF16)
    for layer in range(6):
        if layer < 2:
            cells = left_ref[layer]
        elif layer < 4:
            cells = cells_ref[layer - 2]
        else:
            cells = right_ref[layer - 4]
        wide = cells.astype(F32)
        window[layer, 0:16, :] = edge
        window[layer, 272:288, :] = edge
        window[layer, 16:272, 0:128] = previous_rows(wide, 16).astype(BF16)
        window[layer, 16:272, 128:256] = cells
        window[layer, 16:272, 256:384] = next_rows(wide, 16).astype(BF16)
    active = None
    for layer in range(4):
        total = None
        for tap in range(9):
            shift_x, shift_y = tap // 3, tap % 3
            view = window[layer + shift_x, 16 * shift_y : 16 * shift_y + 256, :]
            term = nn_dot(view, weight_ref[tap])
            total = term if total is None else total + term
        sigma = 1.0 / (1.0 + jnp.exp(-total))
        slope = sigma * (1.0 + total * (1.0 - sigma))
        spread = cot_ref[(layer + 1) // 2].astype(F32).reshape(8, 1, 16, 256) * 0.125
        spread = jnp.broadcast_to(spread, (8, 2, 16, 256)).reshape(256, 256)
        grads[layer, 0:16, :] = edge[:, :256]
        grads[layer, 272:288, :] = edge[:, :256]
        grads[layer, 16:272, :] = (spread * slope).astype(BF16)
        if layer in (1, 2):
            blocks = (total * sigma).reshape(8, 2, 16, 256)
            blocks = blocks[:, 0] + blocks[:, 1]
            active = blocks if active is None else active + blocks
    active = active.reshape(128, 256)
    for part in range(2):
        lanes = slice(128 * part, 128 * part + 128)
        column[part] = active[:, lanes]
        pooled = column[part, pl.ds(0, 64, stride=2), :] + column[part, pl.ds(1, 64, stride=2), :]
        features_ref[:, lanes] = (pooled * 0.125).astype(BF16)
    core = core_ref[0]
    own = grads[1:3, 16:272, :].reshape(512, 256)
    for tap in range(9):
        shift_x, shift_y = tap // 3, tap % 3
        view = window[1 + shift_x : 3 + shift_x, 16 * shift_y : 16 * shift_y + 256, :].reshape(512, 384)
        terms = (tn_dot(view, own) * 0.25).astype(BF16)
        keep_ref[tap] = jnp.where(core == 0, terms[:, :128], terms[:, 128:])
        send_ref[tap] = jnp.where(core == 0, terms[:, 128:], terms[:, :128])
    for layer in range(2):
        total = None
        for tap in range(9):
            shift_x, shift_y = tap // 3, tap % 3
            view = grads[layer + 2 - shift_x, 32 - 16 * shift_y : 288 - 16 * shift_y, :]
            term = nt_dot(view, weight_ref[tap])
            total = term if total is None else total + term
        result = next_rows(total[:, 0:128], 16) + total[:, 128:256] + previous_rows(total[:, 256:384], 16)
        grad_ref[layer] = result.astype(BF16)


def block_b(core, left, cells, right, weight, cot):
    return pl.pallas_call(
        block_b_kernel,
        in_specs=[SCALAR] + [WHOLE] * 5,
        out_shape=(
            jax.ShapeDtypeStruct((64, 256), BF16),
            jax.ShapeDtypeStruct((9, 384, 128), BF16),
            jax.ShapeDtypeStruct((9, 384, 128), BF16),
            jax.ShapeDtypeStruct((2, 256, 128), BF16),
        ),
        scratch_shapes=[
            pltpu.VMEM((6, 288, 384), BF16),
            pltpu.VMEM((4, 288, 256), BF16),
            pltpu.VMEM((2, 128, 128), F32),
        ],
        compiler_params=pltpu.CompilerParams(vmem_limit_bytes=ROOM),
        cost_estimate=pl.CostEstimate(flops=4 * 2 * 512 * 3456 * 256, bytes_accessed=5 * 10**6, transcendentals=5 * 10**5),
    )(core, left, cells, right, weight, cot)


def kernel_a_kernel(core_ref, grad_ref, slope_ref, ends_ref, window_ref, sides_ref, pre_out, keep_ref, send_ref, pre_ref, sem):
    core = core_ref[0]
    edge = jnp.zeros((16, 256), BF16)
    for layer in range(4):
        spread = grad_ref[layer // 2].astype(F32).reshape(16, 1, 16, 128) * 0.125
        spread = jnp.broadcast_to(spread, (16, 2, 16, 128)).reshape(512, 128)
        slope = (ends_ref[layer // 3] if layer in (0, 3) else slope_ref[layer - 1]).astype(F32)
        pre_ref[layer, 0:16, :] = edge
        pre_ref[layer, 528:544, :] = edge
        pre_ref[layer, 16:528, 0:128] = (spread * slope[:, 0:128]).astype(BF16)
        pre_ref[layer, 16:528, 128:256] = (spread * slope[:, 128:256]).astype(BF16)
    store = pltpu.make_async_copy(pre_ref, pre_out, sem)
    store.start()
    grads = pre_ref[:, 16:528, :].reshape(2048, 256)
    for tap in range(9):
        shift_x, shift_y = tap // 3, tap % 3
        rows = slice(16 * shift_y, 16 * shift_y + 512)
        if shift_x == 0:
            terms = tn_dot(window_ref[0:3, rows].reshape(1536, 256), grads[512:]) + tn_dot(sides_ref[0, rows], grads[:512])
        elif shift_x == 1:
            terms = tn_dot(window_ref[:, rows].reshape(2048, 256), grads)
        else:
            terms = tn_dot(window_ref[1:4, rows].reshape(1536, 256), grads[:1536]) + tn_dot(sides_ref[1, rows], grads[1536:])
        terms = terms * 0.25
        even, odd = terms[:, :128], terms[:, 128:]
        first = jnp.concatenate([even[192:256] + odd[0:64], even[0:32] + odd[64:96]]).astype(BF16)
        second = (even[32:128] + odd[96:192]).astype(BF16)
        keep_ref[tap] = jnp.where(core == 0, first, second)
        send_ref[tap] = jnp.where(core == 0, second, first)
    store.wait()


def kernel_a(core, grad, slope, ends, window, sides):
    return pl.pallas_call(
        kernel_a_kernel,
        in_specs=[SCALAR] + [WHOLE] * 5,
        out_specs=(APART, WHOLE, WHOLE),
        scratch_shapes=[pltpu.VMEM((4, 544, 256), BF16), pltpu.SemaphoreType.DMA],
        out_shape=(
            jax.ShapeDtypeStruct((4, 544, 256), BF16),
            jax.ShapeDtypeStruct((9, 96, 128), BF16),
            jax.ShapeDtypeStruct((9, 96, 128), BF16),
        ),
        compiler_params=pltpu.CompilerParams(vmem_limit_bytes=ROOM),
        cost_estimate=pl.CostEstimate(flops=2 * 2048 * 2304 * 256, bytes_accessed=6 * 10**6, transcendentals=0),
    )(core, grad, slope, ends, window, sides)


def back_a_kernel(grads_ref, weight_ref, inner_ref, to_left_ref, to_right_ref):
    for layer in range(-1, 5):
        total = None
        for tap in range(9):
            shift_x, shift_y = tap // 3, tap % 3
            source = layer + 1 - shift_x
            if 0 <= source < 4:
                view = grads_ref[source, 32 - 16 * shift_y : 544 - 16 * shift_y, :]
                term = nt_dot(view, weight_ref[tap])
                total = term if total is None else total + term
        outer = total[:, 128:256]
        outer = jnp.where(low_lanes(outer.shape), previous_rows(outer, 16), next_rows(outer, 16))
        result = (total[:, 0:128] + outer).astype(BF16)
        if layer == -1:
            to_left_ref[...] = result
        elif layer == 4:
            to_right_ref[...] = result
        else:
            inner_ref[layer] = result


def back_a(grads, weight):
    return pl.pallas_call(
        back_a_kernel,
        out_shape=(
            jax.ShapeDtypeStruct((4, 512, 128), BF16),
            jax.ShapeDtypeStruct((512, 128), BF16),
            jax.ShapeDtypeStruct((512, 128), BF16),
        ),
        compiler_params=pltpu.CompilerParams(vmem_limit_bytes=ROOM),
        cost_estimate=pl.CostEstimate(flops=2 * 2048 * 2304 * 256, bytes_accessed=4 * 10**6, transcendentals=0),
    )(grads, weight)


def paired_weight(weight):
    taps = weight.reshape(9, 3, 64, 128)
    none = jnp.zeros((9, 64, 128), weight.dtype)
    even = jnp.concatenate([taps[:, 1], taps[:, 2], none, taps[:, 0]], axis=1)
    odd = jnp.concatenate([taps[:, 0], taps[:, 1], taps[:, 2], none], axis=1)
    return jnp.concatenate([even, odd], axis=2)


def merge_kernel(keep_a_ref, other_a_ref, keep_b_ref, other_b_ref, rows_ref):
    for tap in range(9):
        rows = keep_a_ref[tap].astype(F32) + other_a_ref[tap].astype(F32)
        rows_ref[96 * tap : 96 * tap + 96] = rows.astype(BF16)
        rows = keep_b_ref[tap].astype(F32) + other_b_ref[tap].astype(F32)
        rows_ref[864 + 384 * tap : 1248 + 384 * tap] = rows.astype(BF16)
    rows_ref[4320:4352] = jnp.zeros((32, 128), BF16)


def merge(keep_a, other_a, keep_b, other_b):
    return pl.pallas_call(
        merge_kernel,
        out_shape=jax.ShapeDtypeStruct((4352, 128), BF16),
        compiler_params=pltpu.CompilerParams(vmem_limit_bytes=ROOM),
        cost_estimate=pl.CostEstimate(flops=0, bytes_accessed=4 * 10**6, transcendentals=0),
    )(keep_a, other_a, keep_b, other_b)


def total_kernel(blocks_ref, copies_ref):
    total = blocks_ref[0].astype(F32)
    for block in range(1, blocks_ref.shape[0]):
        total = total + blocks_ref[block].astype(F32)
    total = total.astype(BF16)
    for copy in range(copies_ref.shape[0]):
        copies_ref[copy] = total


def total_copies(blocks, count):
    return pl.pallas_call(
        total_kernel,
        out_shape=jax.ShapeDtypeStruct((count, 272, 128), BF16),
        compiler_params=pltpu.CompilerParams(vmem_limit_bytes=ROOM),
        cost_estimate=pl.CostEstimate(flops=10**6, bytes_accessed=2 * 10**6, transcendentals=0),
    )(blocks)


def unpack_kernel(core_ref, mine_ref, away_ref, sum_a_out, sum_b_out, sum_a_ref, sum_b_ref, sems):
    core = core_ref[0]
    copies = []
    for tap in range(9):
        rows = slice(864 + 384 * tap, 1248 + 384 * tap)
        mine, away = mine_ref[rows].astype(F32), away_ref[rows].astype(F32)
        sum_b_ref[tap, :, 0:128] = jnp.where(core == 0, mine, away)
        sum_b_ref[tap, :, 128:256] = jnp.where(core == 0, away, mine)
        copies.append(pltpu.make_async_copy(sum_b_ref.at[tap], sum_b_out.at[tap], sems.at[tap]))
        copies[-1].start()
    for tap in range(9):
        rows = slice(96 * tap, 96 * tap + 96)
        mine, away = mine_ref[rows].astype(F32), away_ref[rows].astype(F32)
        sum_a_ref[tap, 0] = jnp.where(core == 0, mine, away)
        sum_a_ref[tap, 1] = jnp.where(core == 0, away, mine)
    copies.append(pltpu.make_async_copy(sum_a_ref, sum_a_out, sems.at[9]))
    copies[-1].start()
    for copy in copies:
        copy.wait()


def unpack(core, mine, away):
    return pl.pallas_call(
        unpack_kernel,
        in_specs=[SCALAR] + [WHOLE] * 2,
        out_specs=(APART, APART),
        out_shape=(
            jax.ShapeDtypeStruct((9, 2, 96, 128), F32),
            jax.ShapeDtypeStruct((9, 384, 256), F32),
        ),
        scratch_shapes=[
            pltpu.VMEM((9, 2, 96, 128), F32),
            pltpu.VMEM((9, 384, 256), F32),
            pltpu.SemaphoreType.DMA((10,)),
        ],
        compiler_params=pltpu.CompilerParams(vmem_limit_bytes=ROOM),
        cost_estimate=pl.CostEstimate(flops=0, bytes_accessed=7 * 10**6, transcendentals=0),
    )(core, mine, away)


AXES = ("slab", "rep")
ACROSS = [[((16 * x + 4 * y + z) * 4 + rep) for x in range(4) for y in range(4)] for z in range(4) for rep in range(4)]
ALONG = [[((4 * plane + z) * 4 + 2 * far + core) for far in range(2) for z in range(4)] for plane in range(16) for core in range(2)]
CORES = [(device, device ^ 1) for device in range(256)]


def other_core(value):
    return lax.ppermute(value, AXES, CORES)


def exchange(blocks, groups):
    return lax.all_to_all(blocks, AXES, 0, 0, axis_index_groups=groups, tiled=True)


def neighbours(to_left, to_right):
    count = lax.axis_size("slab")
    up = [(i, i + 1) for i in range(count - 1)]
    down = [(i + 1, i) for i in range(count - 1)]
    return lax.ppermute(to_right, "slab", up), lax.ppermute(to_left, "slab", down)


def shards(cubes, weight_a, weight_b, cotangent):
    core = (lax.axis_index("rep") % 2).reshape(1)
    pair_weight = paired_weight(weight_a)
    taps_b = weight_b.reshape(9, 384, 256)
    cells = cubes.reshape(4, 512, 128)
    cot = cotangent.reshape(64, 256)
    cot_rows = [cot[:, :128], cot[:, 128:]]
    left, right = neighbours(jnp.concatenate([cells[0]] + cot_rows), jnp.concatenate([cells[3]] + cot_rows))
    window, partial, slope_a, pool = forward_inner(cells, pair_weight)
    sides, ends, pooled = forward_outer(left[:512], right[:512], pair_weight, partial, pool)
    pooled_left, pooled_right = neighbours(pooled, pooled)
    cots = [jnp.concatenate([side[512:576], side[576:640]], axis=1) for side in (left, right)]
    cots = jnp.stack([cots[0], cot, cots[1]])
    cots = jnp.broadcast_to(cots[:, :, None, :], (3, 64, 2, 256)).reshape(3, 128, 256)
    features, keep_b, send_b, grad_pooled = block_b(core, pooled_left, pooled, pooled_right, taps_b, cots)
    other_b = other_core(send_b)
    grad_pre, keep_a, send_a = kernel_a(core, grad_pooled, slope_a, ends, window, sides)
    other_a = other_core(send_a)
    inner, to_left, to_right = back_a(grad_pre, pair_weight)
    rows = merge(keep_a, other_a, keep_b, other_b)
    blocks = exchange(rows.reshape(16, 272, 128), ACROSS)
    blocks, to_left, to_right = lax.optimization_barrier((blocks, to_left, to_right))
    blocks = exchange(total_copies(blocks, 8), ALONG)
    blocks, to_left, to_right = lax.optimization_barrier((blocks, to_left, to_right))
    from_left, from_right = neighbours(to_left, to_right)
    blocks = exchange(total_copies(blocks, 16), ACROSS)
    blocks, from_left, from_right = lax.optimization_barrier((blocks, from_left, from_right))
    mine = blocks.reshape(4352, 128)
    away = other_core(mine)
    first = (inner[:1].astype(F32) + from_left.astype(F32)).astype(BF16)
    last = (inner[3:].astype(F32) + from_right.astype(F32)).astype(BF16)
    grad_cubes = jnp.concatenate([first, inner[1:3], last])
    sum_a, sum_b = unpack(core, mine, away)
    return (
        features.reshape(1, 1, 8, 8, 256),
        grad_cubes.reshape(1, 4, 32, 32, 64),
        sum_a.reshape(3, 3, 3, 64, 128),
        sum_b.reshape(3, 3, 3, 128, 256),
    )


def solution(mesh):
    return jax.shard_map(
        shards,
        mesh=mesh,
        in_specs=(P("rep", "slab", None, None, None), P(), P(), P("rep", "slab", None, None, None)),
        out_specs=(
            P("rep", "slab", None, None, None),
            P("rep", "slab", None, None, None),
            P(),
            P(),
        ),
        check_vma=False,
    )
```
